256 devices in a mesh: pen: 32 (over z, y), slab: 8 (over x, core).
Axes of the slice: x: 4, y: 4, z: 8, core: 2. Of those that a mesh axis runs over, the one named last changes fastest.
Arguments:
- features: bfloat16 [524288, 128], P(('pen', 'slab')), may hold values from -6 to 6
- fractions: float32 [3, 524288], P(None, ('pen', 'slab')), may hold values from 0 to 1
- row_ids: int32 [256, 512], P(('pen', 'slab')), may hold values from -1 to 65535, as said below
- stencil_slots: int32 [16, 524288], P(None, ('pen', 'slab')), may hold values from 0 to 511, as said below
- stencil_z: int32 [524288], P(('pen', 'slab')), may hold values from 0 to 255
- atom_count: int32 [256], P(('pen', 'slab')), may hold values from 1 to 2048
- w_in: bfloat16 [128, 128], replicated, may hold values from -0.5 to 0.5
- w_out: float32 [128], replicated, may hold values from -0.5 to 0.5
Outputs:
- forces: float32 [3, 524288], P(None, ('pen', 'slab'))
- feature_grad: bfloat16 [524288, 128], P(('pen', 'slab'))
The draws below stay inside these ranges and needn't reach their ends.
Inputs may be any that keep to these rules, and one draw needn't show every extreme that they name: `row_ids`: entries of a block's list are -1 or a row id x * 256 + y; the ids come first and are distinct within the block; at most 2 of one block's ids share both x mod 32 and y mod 8, and some block reaches that for every such pair. `stencil_slots`: entry 4 i + j of atom a names an id entry of the list of a's block, whose row is (x + i, y + j) modulo 256 for the atom's stencil corner (x, y).
All inputs are finite; a program needn't handle non-finite values.
Results may differ from the reference program's by a relative error of at most 0.0049.
Values sent between devices are 32-bit elements; how exact they have to be, the bound alone decides.
A program may use at most 64 MiB of HBM per device.

```python
import math
import jax
import jax.numpy as jnp
from jax import lax

GRID = 256
FEAT = 128
HIDDEN_SIZE = 128
ATOM_DEV = 2048
FOOT_X = 32
FOOT_Y = 16
ROWS_DEV = 512
ATOMS = 524288
DEVICES = 256


def block_layout(key):
    keys = jax.random.split(key, 10)
    block_index = jnp.arange(DEVICES, dtype=jnp.int32)
    extent_x = jax.random.randint(keys[0], (DEVICES,), 4, FOOT_X + 1)
    extent_y = jax.random.randint(keys[1], (DEVICES,), 4, FOOT_Y + 1)
    widest = jax.random.randint(keys[2], (), 0, DEVICES)
    extent_x = jnp.where(block_index == widest, FOOT_X, extent_x)
    extent_y = jnp.where(block_index == widest, FOOT_Y, extent_y)
    anchor_x = jax.random.randint(keys[3], (DEVICES,), 0, GRID)
    anchor_y = jax.random.randint(keys[4], (DEVICES,), 0, GRID)
    positions = jnp.arange(ROWS_DEV, dtype=jnp.int32)
    live_rows = positions[None, :] < (extent_x * extent_y)[:, None]
    row_x = (anchor_x[:, None] + positions[None, :] // extent_y[:, None]) % GRID
    row_y = (anchor_y[:, None] + positions[None, :] % extent_y[:, None]) % GRID
    row_list = jnp.where(live_rows, row_x * GRID + row_y, -1).astype(jnp.int32)
    divisor = jax.random.randint(keys[5], (DEVICES,), 1, 7)
    counts = ATOM_DEV // divisor
    busiest = jax.random.randint(keys[6], (), 0, DEVICES)
    counts = jnp.where(block_index == busiest, ATOM_DEV, counts).astype(jnp.int32)
    atom_index = jnp.arange(ATOMS, dtype=jnp.int32)
    owner_block = atom_index // ATOM_DEV
    start_x = jax.random.randint(keys[7], (ATOMS,), 0, 1 << 20) % (extent_x[owner_block] - 3)
    start_y = jax.random.randint(keys[8], (ATOMS,), 0, 1 << 20) % (extent_y[owner_block] - 3)
    far_atom = atom_index == widest * ATOM_DEV
    near_atom = atom_index == widest * ATOM_DEV + 1
    start_x = jnp.where(far_atom, FOOT_X - 4, jnp.where(near_atom, 0, start_x))
    start_y = jnp.where(far_atom, FOOT_Y - 4, jnp.where(near_atom, 0, start_y))
    offsets = jnp.arange(4, dtype=jnp.int32)
    slot_table = (start_x[None, None, :] + offsets[:, None, None]) * extent_y[owner_block][None, None, :]
    slot_table = slot_table + start_y[None, None, :] + offsets[None, :, None]
    base_z = jax.random.randint(keys[9], (ATOMS,), 0, GRID)
    return (row_list, slot_table.reshape(16, ATOMS).astype(jnp.int32), base_z.astype(jnp.int32), counts)


def draw_row_ids(key, part):
    shared = block_layout(key)
    return shared[0]


def draw_stencil_slots(key, part):
    shared = block_layout(key)
    return shared[1]


def draw_stencil_z(key, part):
    shared = block_layout(key)
    return shared[2]


def draw_atom_count(key, part):
    shared = block_layout(key)
    return shared[3]


def level_of(stream_key, shape, cuts, low, top_value):
    level, own = 1.0, jax.random.fold_in(stream_key, 6)
    for position, shards_of in cuts:
        steps = jnp.exp(jax.random.uniform(jax.random.fold_in(own, position), (shards_of,), jnp.float32, low / len(cuts), top_value / len(cuts)))
        level = level * jnp.repeat(steps, shape[position] // shards_of).reshape([-1 if axis == position else 1 for axis in range(len(shape))])
    return level


def bell_draw(rng, extent, deviation, bound, pieces=(), kind=jnp.bfloat16):
    factor_of = level_of(rng, extent, pieces, -0.22, 0.18) if pieces else 1.0
    result = jax.random.normal(rng, extent, jnp.float32) * deviation * factor_of
    return jnp.minimum(jnp.maximum(result, -bound), bound).astype(kind)


def setup_inputs(seed: int = 0) -> dict:
    key_list = jax.random.split(jax.random.key(seed), 9)
    features = bell_draw(key_list[0], (ATOMS, FEAT), 1.0, 6.0, ((0, 256),))
    fractions = jnp.clip(1.0 * jax.random.uniform(key_list[1], (3, ATOMS), jnp.float32) ** level_of(key_list[1], (3, ATOMS), ((1, 256),), -0.2, 0.2), 0.0, 1.0)
    row_ids = draw_row_ids(jax.random.fold_in(key_list[8], 71), 0)
    stencil_slots = draw_stencil_slots(jax.random.fold_in(key_list[8], 71), 0)
    stencil_z = draw_stencil_z(jax.random.fold_in(key_list[8], 71), 0)
    atom_count = draw_atom_count(jax.random.fold_in(key_list[8], 71), 0)
    w_in = bell_draw(key_list[6], (FEAT, HIDDEN_SIZE), FEAT ** -0.5, 0.5)
    w_out = bell_draw(key_list[7], (HIDDEN_SIZE,), HIDDEN_SIZE ** -0.5, 0.5, (), jnp.float32)
    return dict(features=features, fractions=fractions, row_ids=row_ids, stencil_slots=stencil_slots, stencil_z=stencil_z, atom_count=atom_count, w_in=w_in, w_out=w_out)


COUPLE = 8.0
SMOOTH = 1.0


def spline_weights(fraction):
    rest = 1.0 - fraction
    square = fraction * fraction
    cube = square * fraction
    values = jnp.stack([rest * rest * rest / 6.0, (3.0 * cube - 6.0 * square + 4.0) / 6.0,
                        (-3.0 * cube + 3.0 * square + 3.0 * fraction + 1.0) / 6.0, cube / 6.0])
    slopes = jnp.stack([-rest * rest / 2.0, (3.0 * square - 4.0 * fraction) / 2.0,
                        (-3.0 * square + 2.0 * fraction + 1.0) / 2.0, square / 2.0])
    return values, slopes


def kernel_values(wave_a, wave_b, wave_c, grid_size):
    squared = (wave_a * wave_a + wave_b * wave_b + wave_c * wave_c).astype(jnp.float32)
    midpoint = grid_size // 2
    nyquist = (jnp.abs(wave_a) == midpoint) | (jnp.abs(wave_b) == midpoint) | (jnp.abs(wave_c) == midpoint)
    safe = jnp.maximum(squared, 1.0)
    damped = jnp.exp(-((SMOOTH * math.pi / grid_size) ** 2) * squared)
    values = COUPLE * damped * (grid_size * grid_size) / (4.0 * math.pi * math.pi * safe)
    return jnp.where((squared > 0) & jnp.logical_not(nyquist), values, 0.0)


def signed_index(index, grid_size):
    return jnp.where(index < grid_size // 2, index, index - grid_size)


def charge_head(features, w_in, w_out):
    hidden_pre = jnp.dot(features, w_in, preferred_element_type=jnp.float32)
    sigma = jax.nn.sigmoid(hidden_pre)
    charges = jnp.dot(hidden_pre * sigma, w_out, precision=lax.Precision.HIGHEST)
    lifted = (sigma * (1.0 + hidden_pre * (1.0 - sigma)) * w_out).astype(jnp.bfloat16)
    direction = lax.dot_general(lifted, w_in, (((1,), (1,)), ((), ())), preferred_element_type=jnp.float32)
    return charges, direction


def reference(features, fractions, row_ids, stencil_slots, stencil_z, atom_count, w_in, w_out):
    atom_total = features.shape[0]
    atom_index = jnp.arange(atom_total, dtype=jnp.int32)
    block_of = atom_index // ATOM_DEV
    live = (atom_index % ATOM_DEV) < atom_count[block_of]
    charges, direction = charge_head(features, w_in, w_out)
    charges = jnp.where(live, charges, 0.0)
    weight_x, slope_x = spline_weights(fractions[0])
    weight_y, slope_y = spline_weights(fractions[1])
    weight_z, slope_z = spline_weights(fractions[2])
    flat_ids = row_ids.reshape(-1)
    global_rows = flat_ids[(block_of[None, :] * ROWS_DEV + stencil_slots).astype(jnp.int32)]
    x_cells = (global_rows // GRID).reshape(4, 4, atom_total)
    y_cells = (global_rows % GRID).reshape(4, 4, atom_total)
    z_cells = (stencil_z[None, :] + jnp.arange(4, dtype=jnp.int32)[:, None]) % GRID
    density = jnp.zeros((GRID, GRID, GRID), jnp.float32)
    for offset_x in range(4):
        for offset_y in range(4):
            amount = charges[None, :] * weight_x[offset_x][None, :] * weight_y[offset_y][None, :] * weight_z
            density = density.at[x_cells[offset_x, offset_y][None, :], y_cells[offset_x, offset_y][None, :], z_cells].add(amount)
    spectrum = jnp.fft.rfftn(density)
    axis_full = signed_index(jnp.arange(GRID, dtype=jnp.int32), GRID)
    axis_half = jnp.arange(GRID // 2 + 1, dtype=jnp.int32)
    kernel = kernel_values(axis_full[:, None, None], axis_full[None, :, None], axis_half[None, None, :], GRID)
    field = jnp.fft.irfftn(spectrum * kernel, s=(GRID, GRID, GRID)).astype(jnp.float32)
    samples = field[x_cells[:, :, None, :], y_cells[:, :, None, :], z_cells[None, None, :, :]]
    potential = jnp.sum(weight_x[:, None, None, :] * weight_y[None, :, None, :] * weight_z[None, None, :, :] * samples, axis=(0, 1, 2))
    grad_x = jnp.sum(slope_x[:, None, None, :] * weight_y[None, :, None, :] * weight_z[None, None, :, :] * samples, axis=(0, 1, 2))
    grad_y = jnp.sum(weight_x[:, None, None, :] * slope_y[None, :, None, :] * weight_z[None, None, :, :] * samples, axis=(0, 1, 2))
    grad_z = jnp.sum(weight_x[:, None, None, :] * weight_y[None, :, None, :] * slope_z[None, None, :, :] * samples, axis=(0, 1, 2))
    forces = -charges[None, :] * jnp.stack([grad_x, grad_y, grad_z])
    feature_grad = jnp.where(live[:, None], potential[:, None] * direction, 0.0).astype(jnp.bfloat16)
    return forces, feature_grad
```

```python
import functools
import math

import jax
import jax.numpy as jnp
import ml_dtypes
import numpy as np
from jax import lax
from jax.experimental import pallas as pl
from jax.experimental.pallas import tpu as pltpu
from jax.sharding import PartitionSpec as P

GRID = 256
COUPLE = 8.0
SMOOTH = 1.0
ROWS = 512
ATOMS = 2048
DEVICES = 256
CHUNK = 512
VMEM_LIMIT = 56 * 1024 * 1024
F32 = jnp.float32
BF16 = jnp.bfloat16

NN = (((1,), (0,)), ((), ()))
NT = (((1,), (1,)), ((), ()))


def dot(left, right, dims=NN):
    return lax.dot_general(left, right, dims, preferred_element_type=F32)


def split(value):
    high = value.astype(BF16)
    low = (value - high.astype(F32)).astype(BF16)
    return (high, low)


def dot3(left, right, dims=NN):
    return (
        dot(left[0], right[0], dims)
        + dot(left[0], right[1], dims)
        + dot(left[1], right[0], dims)
    )


def fourier_basis():
    cell = np.arange(GRID)
    wave = np.arange(GRID)
    wave = np.where(wave <= GRID // 2, wave, wave - GRID // 2)
    angle = 2.0 * np.pi * ((wave[:, None] * cell[None, :]) % GRID) / GRID
    basis = np.where(np.arange(GRID)[:, None] <= GRID // 2, np.cos(angle), np.sin(angle))
    scale = np.where((np.arange(GRID) == 0) | (np.arange(GRID) == GRID // 2), 1.0, 2.0)
    return basis * np.sqrt(scale / GRID)[:, None]


def split_table(table):
    table = table.astype(np.float32)
    high = table.astype(ml_dtypes.bfloat16)
    low = (table - high.astype(np.float32)).astype(ml_dtypes.bfloat16)
    return [high, low]


def tables():
    basis = fourier_basis()
    place = np.arange(GRID)
    along_x = basis[:, (place % 8) * 32 + place // 8]
    along_y = basis[:, (place % 32) * 8 + place // 32]
    plane = np.stack(split_table(along_x) + split_table(along_x.T) + split_table(along_y))
    return (np.stack(split_table(basis)), np.stack(split_table(basis.T)), plane)


def spline_values(u):
    rest = 1.0 - u
    square = u * u
    cube = square * u
    return (
        rest * rest * rest / 6.0,
        (3.0 * cube - 6.0 * square + 4.0) / 6.0,
        (-3.0 * cube + 3.0 * square + 3.0 * u + 1.0) / 6.0,
        cube / 6.0,
    )


def spline_slopes(u):
    rest = 1.0 - u
    square = u * u
    return (
        -rest * rest / 2.0,
        (3.0 * square - 4.0 * u) / 2.0,
        (-3.0 * square + 2.0 * u + 1.0) / 2.0,
        square / 2.0,
    )


def pick(step, values):
    out = jnp.where(step == 3, values[3], 0.0)
    for k in (2, 1, 0):
        out = jnp.where(step == k, values[k], out)
    return out


def row_to_columns(row):
    return jnp.transpose(jnp.broadcast_to(row, (128, 128)))


def bin_labels(row_ids, ids_cols, bins_cols):
    ids = row_ids[...]
    used = ids >= 0
    x = ids >> 8
    y = ids & 255
    group = jnp.where(used, (x & 31) * 8 + (y & 7), -1)
    label = ((x >> 5) * 32 + (y >> 3)).astype(F32)
    group_f = group.astype(F32)
    place = lax.broadcasted_iota(jnp.int32, (128, ROWS), 1)
    row = lax.broadcasted_iota(jnp.int32, (128, ROWS), 0)
    rank = jnp.zeros((1, ROWS), F32)
    for c in range(ROWS // 128):
        lanes = slice(c * 128, (c + 1) * 128)
        ids_cols[lanes, :] = row_to_columns(ids[:, lanes].astype(F32))
        column = row_to_columns(group_f[:, lanes])
        column = jnp.concatenate([column] * (ROWS // 128), axis=1)
        same = (column == group_f) & (row + c * 128 < place)
        rank += jnp.sum(jnp.where(same, 1.0, 0.0), axis=0, keepdims=True)
    target = jnp.where(used, rank.astype(jnp.int32) * 256 + group, -1)
    for c in range(ROWS // 128):
        hit = target == row + c * 128
        value = jnp.sum(jnp.where(hit, label + 1.0, 0.0), axis=1, keepdims=True) - 1.0
        bins_cols[c * 128 : (c + 1) * 128, :] = jnp.broadcast_to(value, (128, 128))


def corners(slots, ids_cols, corner):
    row = lax.broadcasted_iota(jnp.int32, (ROWS, 128), 0)
    for c in range(ATOMS // 128):
        lanes = slice(c * 128, (c + 1) * 128)
        hit = slots[0:1, lanes] == row
        value = jnp.sum(jnp.where(hit, ids_cols[...], 0.0), axis=0, keepdims=True)
        corner[0:1, lanes] = value.astype(jnp.int32)


def class_weights(corner, fractions, tab_x, tab_y, slopes):
    x0 = corner[0:1, :] >> 8
    y0 = corner[0:1, :] & 255
    value_x = spline_values(fractions[0:1, :])
    value_y = spline_values(fractions[1:2, :])
    step_y = (lax.broadcasted_iota(jnp.int32, (8, ATOMS), 0) - y0) & 7
    tab_y[0:8, :] = pick(step_y, value_y)
    tab_y[8:16, :] = ((((y0 + step_y) >> 3) & 31)).astype(F32)
    if slopes:
        slope_x = spline_slopes(fractions[0:1, :])
        slope_y = spline_slopes(fractions[1:2, :])
        tab_y[16:24, :] = pick(step_y, slope_y)
    for b in range(4):
        rows = slice(b * 8, (b + 1) * 8)
        step_x = (lax.broadcasted_iota(jnp.int32, (8, ATOMS), 0) + b * 8 - x0) & 31
        tab_x[0, rows, :] = pick(step_x, value_x)
        tab_x[1, rows, :] = ((((x0 + step_x) >> 5) & 7) * 32).astype(F32)
        if slopes:
            tab_x[2, rows, :] = pick(step_x, slope_x)


def class_weights_z(stencil_z, fractions, tab_z, slopes):
    z0 = stencil_z[0:1, :]
    step_z = (lax.broadcasted_iota(jnp.int32, (8, ATOMS), 0) - z0) & 7
    tab_z[0:8, :] = pick(step_z, spline_values(fractions[2:3, :]))
    tab_z[8:16, :] = ((((z0 + step_z) >> 3) & 31)).astype(F32)
    if slopes:
        tab_z[16:24, :] = pick(step_z, spline_slopes(fractions[2:3, :]))


def row_weights(tab_x, tab_y, bins_cols, lanes, outs, kinds):
    def twice(part):
        return jnp.concatenate([part, part], axis=0)

    wy = twice(tab_y[0:8, lanes])
    ky = twice(tab_y[8:16, lanes])
    sy = twice(tab_y[16:24, lanes]) if kinds > 1 else None
    width = wy.shape[1]

    def pair(index, i):
        rows = [tab_x[index, pl.ds(2 * i + k, 1), lanes] for k in range(2)]
        return jnp.concatenate([jnp.broadcast_to(row, (8, width)) for row in rows], axis=0)

    @pl.loop(0, 16)
    def _(i):
        wx = pair(0, i)
        key = pair(1, i) + ky
        values = [wx * wy]
        if kinds > 1:
            values += [pair(2, i) * wy, wx * sy]
        for rank in range(2):
            rows = pl.ds(pl.multiple_of(rank * 256 + i * 16, 16), 16)
            label = bins_cols[rows, :]
            label = jnp.concatenate([label] * (width // 128), axis=1)
            hit = key == label
            for k, value in enumerate(values):
                high, low = split(jnp.where(hit, value, 0.0))
                outs[2 * k][rows, :] = high
                outs[2 * k + 1][rows, :] = low


def hidden(features, w_in, w_out, lanes):
    w_in_t = jnp.transpose(w_in[...].astype(F32)).astype(BF16)
    pre = dot(w_in_t, features[lanes, :], NT)
    sigma = jax.nn.sigmoid(pre)
    out_w = row_to_columns(w_out[...])
    out_w = jnp.concatenate([out_w] * (pre.shape[1] // 128), axis=1)
    return (pre, sigma, out_w)


def spread_kernel(
    row_ids,
    slots,
    stencil_z,
    fractions,
    atom_count,
    features,
    w_in,
    w_out,
    basis,
    sent,
    labels,
    bins_cols,
    charges,
    corner,
    ids_cols,
    tab_x,
    tab_y,
    tab_z,
    high,
    low,
    z_high,
    z_low,
    mesh_rows,
):
    bin_labels(row_ids, ids_cols, bins_cols)
    for c in range(ROWS // 128):
        part = jnp.transpose(bins_cols[c * 128 : (c + 1) * 128, :])
        labels[0:1, c * 128 : (c + 1) * 128] = part[0:1, :]
    corners(slots, ids_cols, corner)
    for c in range(ATOMS // CHUNK):
        lanes = slice(c * CHUNK, (c + 1) * CHUNK)
        pre, sigma, out_w = hidden(features, w_in, w_out, lanes)
        charge = jnp.sum(pre * sigma * out_w, axis=0, keepdims=True)
        atom = lax.broadcasted_iota(jnp.int32, (1, CHUNK), 1) + c * CHUNK
        charges[0:1, lanes] = jnp.where(atom < atom_count[0], charge, 0.0)
    class_weights(corner, fractions, tab_x, tab_y, False)
    class_weights_z(stencil_z, fractions, tab_z, False)
    for c in range(ATOMS // CHUNK):
        lanes = slice(c * CHUNK, (c + 1) * CHUNK)
        row_weights(tab_x, tab_y, bins_cols, lanes, [high, low], 1)
        key = tab_z[8:16, lanes]
        amount = tab_z[0:8, lanes] * charges[0:1, lanes]
        amount_high = amount.astype(BF16).astype(F32)
        amount_low = amount - amount_high
        for h in range(0, 32, 2):
            rows = slice(h * 8, h * 8 + 16)
            hits = (key == float(h), key == float(h + 1))
            z_high[rows, :] = jnp.concatenate(
                [jnp.where(hit, amount_high, 0.0) for hit in hits], axis=0
            ).astype(BF16)
            z_low[rows, :] = jnp.concatenate(
                [jnp.where(hit, amount_low, 0.0) for hit in hits], axis=0
            ).astype(BF16)
        total = dot3((z_high[...], z_low[...]), (high[...], low[...]), NT)
        if c == 0:
            mesh_rows[...] = total
        else:
            mesh_rows[...] += total
    sent[...] = dot3((basis[0], basis[1]), split(mesh_rows[...]))


def solve_kernel(rows, labels, tabs, out, rows_t, labels_t, plane, replies):
    for b in range(2):
        for c in range(ROWS // 128):
            src = (slice(b * 128, (b + 1) * 128), slice(c * 128, (c + 1) * 128))
            dst = (slice(c * 128, (c + 1) * 128), slice(b * 128, (b + 1) * 128))
            rows_t[dst] = jnp.transpose(rows[src])
            labels_t[dst] = jnp.transpose(labels[src])
    lane_class = lax.broadcasted_iota(jnp.int32, (8, GRID), 0).astype(F32)
    cell_y = lax.broadcasted_iota(jnp.int32, (32, GRID), 0).astype(F32)

    @pl.loop(0, 32)
    def _(xb):
        groups = []
        for rank in range(2):
            at = pl.ds(pl.multiple_of(rank * 256 + xb * 8, 8), 8)
            value = rows_t[at, :]
            value_high = value.astype(BF16).astype(F32)
            label = labels_t[at, :]
            label_x = jnp.floor(label * (1.0 / 32.0))
            groups.append((value_high, value - value_high, label_x, label - 32.0 * label_x))
        pieces = []
        for yb in range(8):
            left, right = [], []
            for value_high, value_low, label_x, label_y in groups:
                hit = jnp.broadcast_to(label_x[yb : yb + 1], (8, GRID)) == lane_class
                both = [
                    jnp.where(hit, jnp.broadcast_to(part[yb : yb + 1], (8, GRID)), 0.0)
                    for part in (value_high, value_low)
                ]
                left.append(jnp.concatenate(both, axis=0).astype(BF16))
                hit = jnp.broadcast_to(label_y[yb : yb + 1], (32, GRID)) == cell_y
                right.append(jnp.where(hit, 1.0, 0.0).astype(BF16))
            piece = dot(jnp.concatenate(left, axis=1), jnp.concatenate(right, axis=1), NT)
            pieces.append(piece[0:8] + piece[8:16])
        plane[pl.ds(pl.multiple_of(xb * 8, 8), 8), :] = jnp.concatenate(pieces, axis=1)

    along_x, back_x, along_y = [(tabs[2 * k], tabs[2 * k + 1]) for k in range(3)]
    spectrum = dot3(along_x, split(plane[...]))
    spectrum = dot3(split(spectrum), along_y, NT)
    half = GRID // 2
    device = lax.axis_index("pen") * lax.axis_size("slab") + lax.axis_index("slab")

    def wave(index):
        return jnp.where(index <= half, index, index - half)

    wave_x = wave(lax.broadcasted_iota(jnp.int32, (GRID, GRID), 0))
    wave_y = wave(lax.broadcasted_iota(jnp.int32, (GRID, GRID), 1))
    wave_z = wave(device)
    squared = (wave_x * wave_x + wave_y * wave_y + wave_z * wave_z).astype(F32)
    damped = jnp.exp(-((SMOOTH * math.pi / GRID) ** 2) * squared)
    values = COUPLE * damped * (GRID * GRID) / (4.0 * math.pi * math.pi * jnp.maximum(squared, 1.0))
    keep = (squared > 0) & (wave_x != half) & (wave_y != half) & (wave_z != half)
    spectrum = spectrum * jnp.where(keep, values, 0.0)
    field = dot3(back_x, split(spectrum))
    plane[...] = dot3(split(field), along_y)

    upper = lax.broadcasted_iota(jnp.int32, (8, 128), 0) >= 4
    offset = (lax.broadcasted_iota(jnp.int32, (8, 128), 0) & 3) * 32

    @pl.loop(0, 32)
    def _(xb):
        sources = []
        field_rows = plane[pl.ds(pl.multiple_of(xb * 8, 8), 8), :]
        for h in range(8):
            row = jnp.broadcast_to(field_rows[h : h + 1], (8, GRID))
            sources.append(jnp.where(upper, row[:, 128:], row[:, :128]))
        for rank in range(2):
            at = pl.ds(pl.multiple_of(rank * 256 + xb * 8, 8), 8)
            for b in range(2):
                label = labels_t[at, b * 128 : (b + 1) * 128].astype(jnp.int32)
                label_x = label >> 5
                index = (label & 31) + offset
                value = jnp.zeros((8, 128), F32)
                for h in range(8):
                    taken = jnp.take_along_axis(
                        sources[h], index, axis=1, mode="promise_in_bounds"
                    )
                    value = jnp.where(label_x == h, taken, value)
                replies[at, b * 128 : (b + 1) * 128] = value

    for b in range(2):
        for c in range(ROWS // 128):
            src = (slice(c * 128, (c + 1) * 128), slice(b * 128, (b + 1) * 128))
            dst = (slice(b * 128, (b + 1) * 128), slice(c * 128, (c + 1) * 128))
            out[dst] = jnp.transpose(replies[src])


def sample_kernel(
    returned,
    corner,
    charges,
    bins_cols,
    stencil_z,
    fractions,
    atom_count,
    features,
    w_in,
    w_out,
    basis_t,
    forces,
    grads,
    tab_x,
    tab_y,
    tab_z,
    field_high,
    field_low,
    *weights,
):
    class_weights(corner, fractions, tab_x, tab_y, True)
    class_weights_z(stencil_z, fractions, tab_z, True)
    field_high[...], field_low[...] = split(
        dot3((basis_t[0], basis_t[1]), split(returned[...]))
    )
    for c in range(ATOMS // CHUNK):
        lanes = slice(c * CHUNK, (c + 1) * CHUNK)
        row_weights(tab_x, tab_y, bins_cols, lanes, weights, 3)
        key = tab_z[8:16, lanes]
        sums = []
        for k in range(3):
            total = dot3(
                (field_high[...], field_low[...]), (weights[2 * k][...], weights[2 * k + 1][...])
            )
            chosen = jnp.zeros((8, CHUNK), F32)
            for h in range(32):
                chosen = jnp.where(key == float(h), total[h * 8 : (h + 1) * 8], chosen)
            sums.append(chosen)
        wz = tab_z[0:8, lanes]
        potential = jnp.sum(wz * sums[0], axis=0, keepdims=True)
        charge = -charges[0:1, lanes]
        forces[0:1, lanes] = charge * jnp.sum(wz * sums[1], axis=0, keepdims=True)
        forces[1:2, lanes] = charge * jnp.sum(wz * sums[2], axis=0, keepdims=True)
        forces[2:3, lanes] = charge * jnp.sum(tab_z[16:24, lanes] * sums[0], axis=0, keepdims=True)
        atom = lax.broadcasted_iota(jnp.int32, (1, CHUNK), 1) + c * CHUNK
        potential = jnp.where(atom < atom_count[0], potential, 0.0)
        pre, sigma, out_w = hidden(features, w_in, w_out, lanes)
        lift = (sigma * (1.0 + pre * (1.0 - sigma)) * out_w).astype(BF16)
        grad = potential * dot(w_in[...], lift)
        for b in range(CHUNK // 128):
            rows = slice(c * CHUNK + b * 128, c * CHUNK + (b + 1) * 128)
            grads[rows, :] = jnp.transpose(grad[:, b * 128 : (b + 1) * 128]).astype(BF16)


VM = pl.BlockSpec(memory_space=pltpu.VMEM)
SM = pl.BlockSpec(memory_space=pltpu.SMEM)
PARAMS = pltpu.CompilerParams(vmem_limit_bytes=VMEM_LIMIT)


def spread(row_ids, slots, stencil_z, fractions, atom_count, features, w_in, w_out, basis):
    shape = jax.ShapeDtypeStruct
    return pl.pallas_call(
        spread_kernel,
        out_shape=(
            shape((DEVICES, ROWS), F32),
            shape((1, ROWS), F32),
            shape((ROWS, 128), F32),
            shape((1, ATOMS), F32),
            shape((1, ATOMS), jnp.int32),
        ),
        in_specs=[VM] * 4 + [SM] + [VM] * 4,
        out_specs=(VM,) * 5,
        scratch_shapes=[
            pltpu.VMEM((ROWS, 128), F32),
            pltpu.VMEM((2, 32, ATOMS), F32),
            pltpu.VMEM((16, ATOMS), F32),
            pltpu.VMEM((16, ATOMS), F32),
            pltpu.VMEM((ROWS, CHUNK), BF16),
            pltpu.VMEM((ROWS, CHUNK), BF16),
            pltpu.VMEM((GRID, CHUNK), BF16),
            pltpu.VMEM((GRID, CHUNK), BF16),
            pltpu.VMEM((GRID, ROWS), F32),
        ],
        compiler_params=PARAMS,
        name="spread",
    )(row_ids, slots, stencil_z, fractions, atom_count, features, w_in, w_out, basis)


def solve(rows, labels, tabs):
    return pl.pallas_call(
        solve_kernel,
        out_shape=jax.ShapeDtypeStruct((DEVICES, ROWS), F32),
        in_specs=[VM] * 3,
        out_specs=VM,
        scratch_shapes=[
            pltpu.VMEM((ROWS, GRID), F32),
            pltpu.VMEM((ROWS, GRID), F32),
            pltpu.VMEM((GRID, GRID), F32),
            pltpu.VMEM((ROWS, GRID), F32),
        ],
        compiler_params=PARAMS,
        name="solve",
    )(rows, labels, tabs)


def sample(
    returned, corner, charges, bins, stencil_z, fractions, atom_count, features, w_in, w_out, basis_t
):
    return pl.pallas_call(
        sample_kernel,
        out_shape=(
            jax.ShapeDtypeStruct((3, ATOMS), F32),
            jax.ShapeDtypeStruct((ATOMS, 128), BF16),
        ),
        in_specs=[VM] * 6 + [SM] + [VM] * 4,
        out_specs=(VM, VM),
        scratch_shapes=[
            pltpu.VMEM((3, 32, ATOMS), F32),
            pltpu.VMEM((24, ATOMS), F32),
            pltpu.VMEM((24, ATOMS), F32),
            pltpu.VMEM((GRID, ROWS), BF16),
            pltpu.VMEM((GRID, ROWS), BF16),
        ]
        + [pltpu.VMEM((ROWS, CHUNK), BF16)] * 6,
        compiler_params=PARAMS,
        name="sample",
    )(returned, corner, charges, bins, stencil_z, fractions, atom_count, features, w_in, w_out, basis_t)


def exchange(rows):
    return lax.all_to_all(rows, ("pen", "slab"), split_axis=0, concat_axis=0, tiled=True)


def local(features, fractions, row_ids, stencil_slots, stencil_z, atom_count, w_in, w_out):
    basis, basis_t, plane = tables()
    z_row = stencil_z.reshape(1, ATOMS)
    w_row = w_out.reshape(1, 128)
    sent, labels, bins, charges, corner = spread(
        row_ids, stencil_slots, z_row, fractions, atom_count, features, w_in, w_row, jnp.asarray(basis)
    )
    all_labels = lax.all_gather(labels, ("pen", "slab"), axis=0, tiled=True)
    replies = solve(exchange(sent), all_labels, jnp.asarray(plane))
    return sample(
        exchange(replies),
        corner,
        charges,
        bins,
        z_row,
        fractions,
        atom_count,
        features,
        w_in,
        w_row,
        jnp.asarray(basis_t),
    )


def solution(mesh):
    placed = (
        P(("pen", "slab"), None),
        P(None, ("pen", "slab")),
        P(("pen", "slab"), None),
        P(None, ("pen", "slab")),
        P(("pen", "slab")),
        P(("pen", "slab")),
        P(),
        P(),
    )
    return jax.shard_map(
        local,
        mesh=mesh,
        in_specs=placed,
        out_specs=(P(None, ("pen", "slab")), P(("pen", "slab"), None)),
        check_vma=False,
    )
```

```python
import functools
import math

import jax
import jax.numpy as jnp
import ml_dtypes
import numpy as np
from jax import lax
from jax.experimental import pallas as pl
from jax.experimental.pallas import tpu as pltpu
from jax.sharding import PartitionSpec as P

GRID = 256
COUPLE = 8.0
SMOOTH = 1.0
ROWS = 512
ATOMS = 2048
DEVICES = 256
CHUNK = 512
VMEM_LIMIT = 56 * 1024 * 1024
F32 = jnp.float32
BF16 = jnp.bfloat16

NN = (((1,), (0,)), ((), ()))
NT = (((1,), (1,)), ((), ()))


def dot(left, right, dims=NN):
    return lax.dot_general(left, right, dims, preferred_element_type=F32)


def split(value):
    high = value.astype(BF16)
    low = (value - high.astype(F32)).astype(BF16)
    return (high, low)


def dot3(left, right, dims=NN):
    return (
        dot(left[0], right[0], dims)
        + dot(left[0], right[1], dims)
        + dot(left[1], right[0], dims)
    )


def fourier_basis():
    cell = np.arange(GRID)
    wave = np.arange(GRID)
    wave = np.where(wave <= GRID // 2, wave, wave - GRID // 2)
    angle = 2.0 * np.pi * ((wave[:, None] * cell[None, :]) % GRID) / GRID
    basis = np.where(np.arange(GRID)[:, None] <= GRID // 2, np.cos(angle), np.sin(angle))
    scale = np.where((np.arange(GRID) == 0) | (np.arange(GRID) == GRID // 2), 1.0, 2.0)
    return basis * np.sqrt(scale / GRID)[:, None]


def split_table(table):
    table = table.astype(np.float32)
    high = table.astype(ml_dtypes.bfloat16)
    low = (table - high.astype(np.float32)).astype(ml_dtypes.bfloat16)
    return [high, low]


def tables():
    basis = fourier_basis()
    place = np.arange(GRID)
    along_x = basis[:, (place % 8) * 32 + place // 8]
    along_y = basis[:, (place % 32) * 8 + place // 32]
    plane = np.stack(split_table(along_x) + split_table(along_x.T) + split_table(along_y))
    return (np.stack(split_table(basis)), np.stack(split_table(basis.T)), plane)


def spline_values(u):
    rest = 1.0 - u
    square = u * u
    cube = square * u
    return (
        rest * rest * rest / 6.0,
        (3.0 * cube - 6.0 * square + 4.0) / 6.0,
        (-3.0 * cube + 3.0 * square + 3.0 * u + 1.0) / 6.0,
        cube / 6.0,
    )


def spline_slopes(u):
    rest = 1.0 - u
    square = u * u
    return (
        -rest * rest / 2.0,
        (3.0 * square - 4.0 * u) / 2.0,
        (-3.0 * square + 2.0 * u + 1.0) / 2.0,
        square / 2.0,
    )


def pick(step, values):
    out = jnp.where(step == 3, values[3], 0.0)
    for k in (2, 1, 0):
        out = jnp.where(step == k, values[k], out)
    return out


def row_to_columns(row):
    return jnp.transpose(jnp.broadcast_to(row, (128, 128)))


def bin_labels(row_ids, ids_cols, bins_cols):
    ids = row_ids[...]
    used = ids >= 0
    x = ids >> 8
    y = ids & 255
    group = jnp.where(used, (x & 31) * 8 + (y & 7), -1)
    label = ((x >> 5) * 32 + (y >> 3)).astype(F32)
    group_f = group.astype(F32)
    place = lax.broadcasted_iota(jnp.int32, (128, ROWS), 1)
    row = lax.broadcasted_iota(jnp.int32, (128, ROWS), 0)
    rank = jnp.zeros((1, ROWS), F32)
    for c in range(ROWS // 128):
        lanes = slice(c * 128, (c + 1) * 128)
        ids_cols[lanes, :] = row_to_columns(ids[:, lanes].astype(F32))
        column = row_to_columns(group_f[:, lanes])
        column = jnp.concatenate([column] * (ROWS // 128), axis=1)
        same = (column == group_f) & (row + c * 128 < place)
        rank += jnp.sum(jnp.where(same, 1.0, 0.0), axis=0, keepdims=True)
    target = jnp.where(used, rank.astype(jnp.int32) * 256 + group, -1)
    for c in range(ROWS // 128):
        hit = target == row + c * 128
        value = jnp.sum(jnp.where(hit, label + 1.0, 0.0), axis=1, keepdims=True) - 1.0
        bins_cols[c * 128 : (c + 1) * 128, :] = jnp.broadcast_to(value, (128, 128))


def corners(slots, ids_cols, corner):
    row = lax.broadcasted_iota(jnp.int32, (ROWS, 128), 0)
    for c in range(ATOMS // 128):
        lanes = slice(c * 128, (c + 1) * 128)
        hit = slots[0:1, lanes] == row
        value = jnp.sum(jnp.where(hit, ids_cols[...], 0.0), axis=0, keepdims=True)
        corner[0:1, lanes] = value.astype(jnp.int32)


def class_weights(corner, fractions, tab_x, tab_y, slopes):
    x0 = corner[0:1, :] >> 8
    y0 = corner[0:1, :] & 255
    value_x = spline_values(fractions[0:1, :])
    value_y = spline_values(fractions[1:2, :])
    step_y = (lax.broadcasted_iota(jnp.int32, (8, ATOMS), 0) - y0) & 7
    tab_y[0:8, :] = pick(step_y, value_y)
    tab_y[8:16, :] = ((((y0 + step_y) >> 3) & 31)).astype(F32)
    if slopes:
        slope_x = spline_slopes(fractions[0:1, :])
        slope_y = spline_slopes(fractions[1:2, :])
        tab_y[16:24, :] = pick(step_y, slope_y)
    for b in range(4):
        rows = slice(b * 8, (b + 1) * 8)
        step_x = (lax.broadcasted_iota(jnp.int32, (8, ATOMS), 0) + b * 8 - x0) & 31
        tab_x[0, rows, :] = pick(step_x, value_x)
        tab_x[1, rows, :] = ((((x0 + step_x) >> 5) & 7) * 32).astype(F32)
        if slopes:
            tab_x[2, rows, :] = pick(step_x, slope_x)


def class_weights_z(stencil_z, fractions, tab_z, slopes):
    z0 = stencil_z[0:1, :]
    step_z = (lax.broadcasted_iota(jnp.int32, (8, ATOMS), 0) - z0) & 7
    tab_z[0:8, :] = pick(step_z, spline_values(fractions[2:3, :]))
    tab_z[8:16, :] = ((((z0 + step_z) >> 3) & 31)).astype(F32)
    if slopes:
        tab_z[16:24, :] = pick(step_z, spline_slopes(fractions[2:3, :]))


def row_weights(tab_x, tab_y, bins_cols, lanes, outs, first, last):
    def twice(part):
        return jnp.concatenate([part, part], axis=0)

    wy = twice(tab_y[0:8, lanes])
    ky = twice(tab_y[8:16, lanes])
    sy = twice(tab_y[16:24, lanes])
    width = wy.shape[1]

    def pair(index, i):
        rows = [tab_x[index, pl.ds(2 * i + k, 1), lanes] for k in range(2)]
        return jnp.concatenate([jnp.broadcast_to(row, (8, width)) for row in rows], axis=0)

    @pl.loop(0, 16)
    def _(i):
        wx = pair(0, i)
        key = pair(1, i) + ky
        values = [wx * wy, pair(2, i) * wy, wx * sy][first:last]
        for rank in range(2):
            rows = pl.ds(pl.multiple_of(rank * 256 + i * 16, 16), 16)
            label = bins_cols[rows, :]
            label = jnp.concatenate([label] * (width // 128), axis=1)
            hit = key == label
            for k, value in enumerate(values):
                high, low = split(jnp.where(hit, value, 0.0))
                outs[2 * k][rows, :] = high
                outs[2 * k + 1][rows, :] = low


def hidden(features, w_in, w_out, lanes):
    w_in_t = jnp.transpose(w_in[...].astype(F32)).astype(BF16)
    pre = dot(w_in_t, features[lanes, :], NT)
    sigma = jax.nn.sigmoid(pre)
    out_w = row_to_columns(w_out[...])
    out_w = jnp.concatenate([out_w] * (pre.shape[1] // 128), axis=1)
    return (pre, sigma, out_w)


MESH = pl.DeviceIdType.MESH
DZ = (4, 1, 7, 2, 6, 3, 5, 0)


def here():
    pen = lax.axis_index("pen")
    slab = lax.axis_index("slab")
    return (pen // 4, lax.rem(pen, 4), slab // 2, lax.rem(slab, 2))


def place_of(z, y, x, core):
    return ((core * 4 + x) * 4 + y) * 8 + z


def target_of(z, y, x, core):
    return (z * 4 + y, x * 2 + core)


def for_all_others(visit):
    z, y, x, core = here()

    @pl.loop(0, 32)
    def _(k):
        other_y = lax.rem(y + lax.rem(k, 4), 4)
        other_x = lax.rem(x + lax.rem(k // 4, 4), 4)
        other_core = lax.rem(core + k // 16, 2)
        for dz in DZ:
            there = (lax.rem(z + dz, 8), other_y, other_x, other_core)
            if dz == 0:
                pl.when(k > 0)(functools.partial(visit, there))
            else:
                visit(there)


def enter():
    barrier = pltpu.get_barrier_semaphore()

    def greet(there):
        pl.semaphore_signal(barrier, inc=1, device_id=target_of(*there), device_id_type=MESH)

    for_all_others(greet)
    return barrier


def send_rows(rows, landed, spare, send_sem, recv_sem):
    me = place_of(*here())
    pltpu.make_async_copy(rows.at[me], landed.at[me], recv_sem).start()
    pltpu.make_async_copy(rows.at[me], spare, send_sem).start()

    def send(there):
        pltpu.make_async_remote_copy(
            src_ref=rows.at[place_of(*there)],
            dst_ref=landed.at[me],
            send_sem=send_sem,
            recv_sem=recv_sem,
            device_id=target_of(*there),
            device_id_type=MESH,
        ).start()

    for_all_others(send)


def await_rows(rows, landed, sem):
    pltpu.make_async_copy(rows, landed, sem).wait()


def label_copies(stage, all_labels, send_sems, recv_sems):
    z, y, x, core = here()
    if stage == 0:
        part = all_labels.at[core, x, y, z]
        peers = [(lax.rem(z + k, 8), y, x, core) for k in range(1, 8)]
        first = 0
    elif stage == 1:
        part = all_labels.at[core, x, y]
        peers = [(z, lax.rem(y + k, 4), x, core) for k in range(1, 4)]
        first = 7
    elif stage == 2:
        part = all_labels.at[core, x]
        peers = [(z, y, lax.rem(x + k, 4), core) for k in range(1, 4)]
        first = 10
    else:
        part = all_labels.at[core]
        peers = [(z, y, x, 1 - core)]
        first = 13
    return [
        pltpu.make_async_remote_copy(
            src_ref=part,
            dst_ref=part,
            send_sem=send_sems.at[first + k],
            recv_sem=recv_sems.at[first + k],
            device_id=target_of(*peer),
            device_id_type=MESH,
        )
        for k, peer in enumerate(peers)
    ]


def step_kernel(
    row_ids,
    slots,
    stencil_z,
    fractions,
    atom_count,
    features,
    w_in,
    w_out,
    basis,
    basis_t,
    tabs,
    forces,
    grads,
    ids_cols,
    bins_cols,
    own_labels,
    all_labels,
    charges,
    corner,
    tab_x,
    tab_y,
    tab_z,
    z_high,
    z_low,
    mesh_rows,
    sent,
    arrived,
    rows_t,
    labels_t,
    onehot_y,
    plane,
    replies_t,
    replies,
    returned,
    spare,
    lifts,
    kernel,
    field_high,
    field_low,
    weights,
    label_send,
    label_recv,
    sem_own,
    send_one,
    recv_one,
    send_two,
    recv_two,
):
    barrier = enter()
    z, y, x, core = here()
    bin_labels(row_ids, ids_cols, bins_cols)
    for c in range(ROWS // 128):
        part = jnp.transpose(bins_cols[c * 128 : (c + 1) * 128, :])
        own_labels[0:1, c * 128 : (c + 1) * 128] = part[0:1, :]
    pl.semaphore_wait(barrier, DEVICES - 1)
    mine = pltpu.make_async_copy(own_labels.at[0], all_labels.at[core, x, y, z], sem_own)
    mine.start()
    mine.wait()

    def labels_on(stage):
        if stage > 0:
            for copy in label_copies(stage - 1, all_labels, label_send, label_recv):
                copy.wait()
        if stage < 4:
            for copy in label_copies(stage, all_labels, label_send, label_recv):
                copy.start()

    labels_on(0)
    corners(slots, ids_cols, corner)
    class_weights(corner, fractions, tab_x, tab_y, True)
    class_weights_z(stencil_z, fractions, tab_z, True)
    labels_on(1)
    for c in range(ATOMS // CHUNK):
        lanes = slice(c * CHUNK, (c + 1) * CHUNK)
        pre, sigma, out_w = hidden(features, w_in, w_out, lanes)
        charge = jnp.sum(pre * sigma * out_w, axis=0, keepdims=True)
        atom = lax.broadcasted_iota(jnp.int32, (1, CHUNK), 1) + c * CHUNK
        charges[0:1, lanes] = jnp.where(atom < atom_count[0], charge, 0.0)
        lifts[:, lanes] = (sigma * (1.0 + pre * (1.0 - sigma)) * out_w).astype(BF16)
    labels_on(2)
    for c in range(ATOMS // CHUNK):
        lanes = slice(c * CHUNK, (c + 1) * CHUNK)
        row_weights(tab_x, tab_y, bins_cols, lanes, [weights.at[k, c] for k in range(2)], 0, 1)
        key = tab_z[8:16, lanes]
        amount = tab_z[0:8, lanes] * charges[0:1, lanes]
        amount_high = amount.astype(BF16).astype(F32)
        amount_low = amount - amount_high
        for h in range(0, 32, 2):
            rows = slice(h * 8, h * 8 + 16)
            hits = (key == float(h), key == float(h + 1))
            z_high[rows, :] = jnp.concatenate(
                [jnp.where(hit, amount_high, 0.0) for hit in hits], axis=0
            ).astype(BF16)
            z_low[rows, :] = jnp.concatenate(
                [jnp.where(hit, amount_low, 0.0) for hit in hits], axis=0
            ).astype(BF16)
        total = dot3((z_high[...], z_low[...]), (weights[0, c], weights[1, c]), NT)
        if c == 0:
            mesh_rows[...] = total
        else:
            mesh_rows[...] += total
        if c == 1:
            labels_on(3)
    sent[...] = dot3((basis[0], basis[1]), split(mesh_rows[...]))
    send_rows(sent, arrived, spare, send_one, recv_one)
    labels_on(4)

    blocks = DEVICES // 2
    for b in range(2):
        for c in range(ROWS // 128):
            part = all_labels[b, :, :, :, c * 128 : (c + 1) * 128].reshape(128, 128)
            dst = (slice(c * 128, (c + 1) * 128), slice(b * 128, (b + 1) * 128))
            labels_t[dst] = jnp.transpose(part)
    cell_y = lax.broadcasted_iota(jnp.int32, (32, GRID), 0).astype(F32)

    @pl.loop(0, 32)
    def _(xb):
        for rank in range(2):
            label = labels_t[pl.ds(pl.multiple_of(rank * 256 + xb * 8, 8), 8), :]
            label_y = label - 32.0 * jnp.floor(label * (1.0 / 32.0))
            for yb in range(8):
                hit = jnp.broadcast_to(label_y[yb : yb + 1], (32, GRID)) == cell_y
                onehot_y[xb * 8 + yb, :, rank * GRID : (rank + 1) * GRID] = jnp.where(
                    hit, 1.0, 0.0
                ).astype(BF16)

    for c in range(ATOMS // CHUNK):
        lanes = slice(c * CHUNK, (c + 1) * CHUNK)
        row_weights(tab_x, tab_y, bins_cols, lanes, [weights.at[k, c] for k in range(2, 6)], 1, 3)
    coulomb(kernel, place_of(z, y, x, core))
    await_rows(sent, arrived, recv_one)

    for b in range(2):
        for c in range(ROWS // 128):
            src = (slice(b * 128, (b + 1) * 128), slice(c * 128, (c + 1) * 128))
            dst = (slice(c * 128, (c + 1) * 128), slice(b * 128, (b + 1) * 128))
            rows_t[dst] = jnp.transpose(arrived[src])
    solve_plane(rows_t, labels_t, onehot_y, tabs, kernel, plane, replies_t)
    for b in range(2):
        for c in range(ROWS // 128):
            src = (slice(c * 128, (c + 1) * 128), slice(b * 128, (b + 1) * 128))
            dst = (slice(b * 128, (b + 1) * 128), slice(c * 128, (c + 1) * 128))
            replies[dst] = jnp.transpose(replies_t[src])
    await_rows(sent, arrived, send_one)
    send_rows(replies, returned, spare, send_two, recv_two)
    await_rows(replies, returned, recv_two)

    field_high[...], field_low[...] = split(
        dot3((basis_t[0], basis_t[1]), split(returned[...]))
    )
    for c in range(ATOMS // CHUNK):
        lanes = slice(c * CHUNK, (c + 1) * CHUNK)
        key = tab_z[8:16, lanes]
        sums = []
        for k in range(3):
            total = dot3(
                (field_high[...], field_low[...]), (weights[2 * k, c], weights[2 * k + 1, c])
            )
            chosen = jnp.zeros((8, CHUNK), F32)
            for h in range(32):
                chosen = jnp.where(key == float(h), total[h * 8 : (h + 1) * 8], chosen)
            sums.append(chosen)
        wz = tab_z[0:8, lanes]
        potential = jnp.sum(wz * sums[0], axis=0, keepdims=True)
        charge = -charges[0:1, lanes]
        forces[0:1, lanes] = charge * jnp.sum(wz * sums[1], axis=0, keepdims=True)
        forces[1:2, lanes] = charge * jnp.sum(wz * sums[2], axis=0, keepdims=True)
        forces[2:3, lanes] = charge * jnp.sum(tab_z[16:24, lanes] * sums[0], axis=0, keepdims=True)
        atom = lax.broadcasted_iota(jnp.int32, (1, CHUNK), 1) + c * CHUNK
        potential = jnp.where(atom < atom_count[0], potential, 0.0)
        grad = potential * dot(w_in[...], lifts[:, lanes])
        for b in range(CHUNK // 128):
            rows = slice(c * CHUNK + b * 128, c * CHUNK + (b + 1) * 128)
            grads[rows, :] = jnp.transpose(grad[:, b * 128 : (b + 1) * 128]).astype(BF16)
    await_rows(replies, returned, send_two)


def coulomb(kernel, wave_index):
    half = GRID // 2

    def wave(index):
        return jnp.where(index <= half, index, index - half)

    wave_x = wave(lax.broadcasted_iota(jnp.int32, (GRID, GRID), 0))
    wave_y = wave(lax.broadcasted_iota(jnp.int32, (GRID, GRID), 1))
    wave_z = wave(wave_index)
    squared = (wave_x * wave_x + wave_y * wave_y + wave_z * wave_z).astype(F32)
    damped = jnp.exp(-((SMOOTH * math.pi / GRID) ** 2) * squared)
    values = COUPLE * damped * (GRID * GRID) / (4.0 * math.pi * math.pi * jnp.maximum(squared, 1.0))
    keep = (squared > 0) & (wave_x != half) & (wave_y != half) & (wave_z != half)
    kernel[...] = jnp.where(keep, values, 0.0)


def solve_plane(rows_t, labels_t, onehot_y, tabs, kernel, plane, replies_t):
    lane_class = lax.broadcasted_iota(jnp.int32, (8, GRID), 0).astype(F32)

    @pl.loop(0, 32)
    def _(xb):
        groups = []
        for rank in range(2):
            at = pl.ds(pl.multiple_of(rank * 256 + xb * 8, 8), 8)
            value = rows_t[at, :]
            value_high = value.astype(BF16).astype(F32)
            label_x = jnp.floor(labels_t[at, :] * (1.0 / 32.0))
            groups.append((value_high, value - value_high, label_x))
        pieces = []
        for yb in range(8):
            left = []
            for value_high, value_low, label_x in groups:
                hit = jnp.broadcast_to(label_x[yb : yb + 1], (8, GRID)) == lane_class
                both = [
                    jnp.where(hit, jnp.broadcast_to(part[yb : yb + 1], (8, GRID)), 0.0)
                    for part in (value_high, value_low)
                ]
                left.append(jnp.concatenate(both, axis=0).astype(BF16))
            piece = dot(jnp.concatenate(left, axis=1), onehot_y[xb * 8 + yb], NT)
            pieces.append(piece[0:8] + piece[8:16])
        plane[pl.ds(pl.multiple_of(xb * 8, 8), 8), :] = jnp.concatenate(pieces, axis=1)

    along_x, back_x, along_y = [(tabs[2 * k], tabs[2 * k + 1]) for k in range(3)]
    spectrum = dot3(along_x, split(plane[...]))
    spectrum = dot3(split(spectrum), along_y, NT) * kernel[...]
    field = dot3(back_x, split(spectrum))
    plane[...] = dot3(split(field), along_y)

    upper = lax.broadcasted_iota(jnp.int32, (8, 128), 0) >= 4
    offset = (lax.broadcasted_iota(jnp.int32, (8, 128), 0) & 3) * 32

    @pl.loop(0, 32)
    def _(xb):
        sources = []
        field_rows = plane[pl.ds(pl.multiple_of(xb * 8, 8), 8), :]
        for h in range(8):
            row = jnp.broadcast_to(field_rows[h : h + 1], (8, GRID))
            sources.append(jnp.where(upper, row[:, 128:], row[:, :128]))
        for rank in range(2):
            at = pl.ds(pl.multiple_of(rank * 256 + xb * 8, 8), 8)
            for b in range(2):
                label = labels_t[at, b * 128 : (b + 1) * 128].astype(jnp.int32)
                label_x = label >> 5
                index = (label & 31) + offset
                value = jnp.zeros((8, 128), F32)
                for h in range(8):
                    taken = jnp.take_along_axis(
                        sources[h], index, axis=1, mode="promise_in_bounds"
                    )
                    value = jnp.where(label_x == h, taken, value)
                replies_t[at, b * 128 : (b + 1) * 128] = value


VM = pl.BlockSpec(memory_space=pltpu.VMEM)
SM = pl.BlockSpec(memory_space=pltpu.SMEM)


def local(features, fractions, row_ids, stencil_slots, stencil_z, atom_count, w_in, w_out):
    basis, basis_t, plane = [jnp.asarray(table) for table in tables()]
    vmem = pltpu.VMEM
    chunks = ATOMS // CHUNK
    return pl.pallas_call(
        step_kernel,
        out_shape=(
            jax.ShapeDtypeStruct((3, ATOMS), F32),
            jax.ShapeDtypeStruct((ATOMS, 128), BF16),
        ),
        in_specs=[VM] * 4 + [SM] + [VM] * 6,
        out_specs=(VM, VM),
        scratch_shapes=[
            vmem((ROWS, 128), F32),
            vmem((ROWS, 128), F32),
            vmem((8, ROWS), F32),
            vmem((2, 4, 4, 8, ROWS), F32),
            vmem((1, ATOMS), F32),
            vmem((1, ATOMS), jnp.int32),
            vmem((3, 32, ATOMS), F32),
            vmem((24, ATOMS), F32),
            vmem((24, ATOMS), F32),
            vmem((GRID, CHUNK), BF16),
            vmem((GRID, CHUNK), BF16),
            vmem((GRID, ROWS), F32),
            vmem((DEVICES, ROWS), F32),
            vmem((DEVICES, ROWS), F32),
            vmem((ROWS, GRID), F32),
            vmem((ROWS, GRID), F32),
            vmem((GRID, 32, 2 * GRID), BF16),
            vmem((GRID, GRID), F32),
            vmem((ROWS, GRID), F32),
            vmem((DEVICES, ROWS), F32),
            vmem((DEVICES, ROWS), F32),
            vmem((ROWS,), F32),
            vmem((128, ATOMS), BF16),
            vmem((GRID, GRID), F32),
            vmem((GRID, ROWS), BF16),
            vmem((GRID, ROWS), BF16),
            vmem((6, chunks, ROWS, CHUNK), BF16),
            pltpu.SemaphoreType.DMA((14,)),
            pltpu.SemaphoreType.DMA((14,)),
        ]
        + [pltpu.SemaphoreType.DMA] * 5,
        compiler_params=pltpu.CompilerParams(
            vmem_limit_bytes=VMEM_LIMIT, collective_id=0, has_side_effects=True
        ),
        name="step",
    )(
        row_ids,
        stencil_slots,
        stencil_z.reshape(1, ATOMS),
        fractions,
        atom_count,
        features,
        w_in,
        w_out.reshape(1, 128),
        basis,
        basis_t,
        plane,
    )


def solution(mesh):
    placed = (
        P(("pen", "slab"), None),
        P(None, ("pen", "slab")),
        P(("pen", "slab"), None),
        P(None, ("pen", "slab")),
        P(("pen", "slab")),
        P(("pen", "slab")),
        P(),
        P(),
    )
    return jax.shard_map(
        local,
        mesh=mesh,
        in_specs=placed,
        out_specs=(P(None, ("pen", "slab")), P(("pen", "slab"), None)),
        check_vma=False,
    )
```

```python
import functools
import math

import jax
import jax.numpy as jnp
import ml_dtypes
import numpy as np
from jax import lax
from jax.experimental import pallas as pl
from jax.experimental.pallas import tpu as pltpu
from jax.sharding import PartitionSpec as P

GRID = 256
COUPLE = 8.0
SMOOTH = 1.0
ROWS = 512
ATOMS = 2048
DEVICES = 256
CHUNK = 512
VMEM_LIMIT = 56 * 1024 * 1024
F32 = jnp.float32
BF16 = jnp.bfloat16

NN = (((1,), (0,)), ((), ()))
NT = (((1,), (1,)), ((), ()))


def dot(left, right, dims=NN):
    return lax.dot_general(left, right, dims, preferred_element_type=F32)


def split(value):
    high = value.astype(BF16)
    low = (value - high.astype(F32)).astype(BF16)
    return (high, low)


def dot3(left, right, dims=NN):
    return (
        dot(left[0], right[0], dims)
        + dot(left[0], right[1], dims)
        + dot(left[1], right[0], dims)
    )


def fourier_basis():
    cell = np.arange(GRID)
    wave = np.arange(GRID)
    wave = np.where(wave <= GRID // 2, wave, wave - GRID // 2)
    angle = 2.0 * np.pi * ((wave[:, None] * cell[None, :]) % GRID) / GRID
    basis = np.where(np.arange(GRID)[:, None] <= GRID // 2, np.cos(angle), np.sin(angle))
    scale = np.where((np.arange(GRID) == 0) | (np.arange(GRID) == GRID // 2), 1.0, 2.0)
    return basis * np.sqrt(scale / GRID)[:, None]


def split_table(table):
    table = table.astype(np.float32)
    high = table.astype(ml_dtypes.bfloat16)
    low = (table - high.astype(np.float32)).astype(ml_dtypes.bfloat16)
    return [high, low]


def tables():
    basis = fourier_basis()
    place = np.arange(GRID)
    along_x = basis[:, (place % 8) * 32 + place // 8]
    along_y = basis[:, (place % 32) * 8 + place // 32]
    plane = np.stack(split_table(along_x) + split_table(along_x.T) + split_table(along_y))
    return (np.stack(split_table(basis)), np.stack(split_table(basis.T)), plane)


def spline_values(u):
    rest = 1.0 - u
    square = u * u
    cube = square * u
    return (
        rest * rest * rest / 6.0,
        (3.0 * cube - 6.0 * square + 4.0) / 6.0,
        (-3.0 * cube + 3.0 * square + 3.0 * u + 1.0) / 6.0,
        cube / 6.0,
    )


def spline_slopes(u):
    rest = 1.0 - u
    square = u * u
    return (
        -rest * rest / 2.0,
        (3.0 * square - 4.0 * u) / 2.0,
        (-3.0 * square + 2.0 * u + 1.0) / 2.0,
        square / 2.0,
    )


def pick(step, values):
    out = jnp.where(step == 3, values[3], 0.0)
    for k in (2, 1, 0):
        out = jnp.where(step == k, values[k], out)
    return out


def row_to_columns(row):
    return jnp.transpose(jnp.broadcast_to(row, (128, 128)))


def bin_labels(row_ids, ids_cols, bins_cols):
    ids = row_ids[...]
    used = ids >= 0
    x = ids >> 8
    y = ids & 255
    group = jnp.where(used, (x & 31) * 8 + (y & 7), -1)
    label = ((x >> 5) * 32 + (y >> 3)).astype(F32)
    place = lax.broadcasted_iota(jnp.int32, (128, ROWS), 1)
    row = lax.broadcasted_iota(jnp.int32, (128, ROWS), 0)
    rank = jnp.zeros((1, ROWS), F32)
    for c in range(ROWS // 128):
        lanes = slice(c * 128, (c + 1) * 128)
        column = row_to_columns(ids[:, lanes])
        ids_cols[lanes, :] = column.astype(F32)
        column = (column >> 8 & 31) * 8 + (column & 7)
        column = jnp.concatenate([column] * (ROWS // 128), axis=1)
        same = (column == group) & (row + c * 128 < place)
        rank += jnp.sum(jnp.where(same, 1.0, 0.0), axis=0, keepdims=True)
    target = jnp.where(used, rank.astype(jnp.int32) * 256 + group, -1)
    for c in range(ROWS // 128):
        hit = target == row + c * 128
        value = jnp.sum(jnp.where(hit, label + 1.0, 0.0), axis=1, keepdims=True) - 1.0
        bins_cols[c * 128 : (c + 1) * 128, :] = jnp.broadcast_to(value, (128, 128))


def corners(slots, ids_cols, corner):
    row = lax.broadcasted_iota(jnp.int32, (ROWS, 128), 0)
    for c in range(ATOMS // 128):
        lanes = slice(c * 128, (c + 1) * 128)
        hit = slots[0:1, lanes] == row
        value = jnp.sum(jnp.where(hit, ids_cols[...], 0.0), axis=0, keepdims=True)
        corner[0:1, lanes] = value.astype(jnp.int32)


def class_weights(corner, fractions, tab_x, tab_y, slopes):
    x0 = corner[0:1, :] >> 8
    y0 = corner[0:1, :] & 255
    value_x = spline_values(fractions[0:1, :])
    value_y = spline_values(fractions[1:2, :])
    step_y = (lax.broadcasted_iota(jnp.int32, (8, ATOMS), 0) - y0) & 7
    tab_y[0:8, :] = pick(step_y, value_y)
    tab_y[8:16, :] = ((((y0 + step_y) >> 3) & 31)).astype(F32)
    if slopes:
        slope_x = spline_slopes(fractions[0:1, :])
        slope_y = spline_slopes(fractions[1:2, :])
        tab_y[16:24, :] = pick(step_y, slope_y)
    for b in range(4):
        rows = slice(b * 8, (b + 1) * 8)
        step_x = (lax.broadcasted_iota(jnp.int32, (8, ATOMS), 0) + b * 8 - x0) & 31
        tab_x[0, rows, :] = pick(step_x, value_x)
        tab_x[1, rows, :] = ((((x0 + step_x) >> 5) & 7) * 32).astype(F32)
        if slopes:
            tab_x[2, rows, :] = pick(step_x, slope_x)


def class_weights_z(stencil_z, fractions, tab_z, slopes):
    z0 = stencil_z[0:1, :]
    step_z = (lax.broadcasted_iota(jnp.int32, (8, ATOMS), 0) - z0) & 7
    tab_z[0:8, :] = pick(step_z, spline_values(fractions[2:3, :]))
    tab_z[8:16, :] = ((((z0 + step_z) >> 3) & 31)).astype(F32)
    if slopes:
        tab_z[16:24, :] = pick(step_z, spline_slopes(fractions[2:3, :]))


def row_weights(tab_x, tab_y, bins_cols, lanes, outs, first, last):
    def twice(part):
        return jnp.concatenate([part, part], axis=0)

    wy = twice(tab_y[0:8, lanes])
    ky = twice(tab_y[8:16, lanes])
    sy = twice(tab_y[16:24, lanes])
    width = wy.shape[1]

    def pair(index, i):
        rows = [tab_x[index, pl.ds(2 * i + k, 1), lanes] for k in range(2)]
        return jnp.concatenate([jnp.broadcast_to(row, (8, width)) for row in rows], axis=0)

    @pl.loop(0, 16)
    def _(i):
        wx = pair(0, i)
        key = pair(1, i) + ky
        values = [wx * wy, pair(2, i) * wy, wx * sy][first:last]
        for rank in range(2):
            rows = pl.ds(pl.multiple_of(rank * 256 + i * 16, 16), 16)
            label = bins_cols[rows, :]
            label = jnp.concatenate([label] * (width // 128), axis=1)
            hit = key == label
            for k, value in enumerate(values):
                high, low = split(jnp.where(hit, value, 0.0))
                outs[2 * k][rows, :] = high
                outs[2 * k + 1][rows, :] = low


def hidden(features, w_in, w_out, lanes):
    w_in_t = jnp.transpose(w_in[...].astype(F32)).astype(BF16)
    pre = dot(w_in_t, features[lanes, :], NT)
    sigma = jax.nn.sigmoid(pre)
    out_w = row_to_columns(w_out[...])
    out_w = jnp.concatenate([out_w] * (pre.shape[1] // 128), axis=1)
    return (pre, sigma, out_w)


MESH = pl.DeviceIdType.MESH
DZ = (4, 1, 7, 2, 6, 3, 5, 0)


def here():
    pen = lax.axis_index("pen")
    slab = lax.axis_index("slab")
    return (pen // 4, lax.rem(pen, 4), slab // 2, lax.rem(slab, 2))


def place_of(z, y, x, core):
    return ((core * 4 + x) * 4 + y) * 8 + z


def target_of(z, y, x, core):
    return (z * 4 + y, x * 2 + core)


def for_others(half, visit):
    z, y, x, core = here()
    other_core = lax.rem(core + half, 2)

    @pl.loop(0, 16)
    def _(k):
        other_y = lax.rem(y + lax.rem(k, 4), 4)
        other_x = lax.rem(x + k // 4, 4)
        for dz in DZ:
            there = (lax.rem(z + dz, 8), other_y, other_x, other_core)
            if dz == 0 and half == 0:
                pl.when(k > 0)(functools.partial(visit, there))
            else:
                visit(there)


def lines():
    z, y, x, core = here()
    return (
        [(lax.rem(z + k, 8), y, x, core) for k in range(1, 8)],
        [(z, lax.rem(y + k, 4), x, core) for k in range(1, 4)],
        [(z, y, lax.rem(x + k, 4), core) for k in range(1, 4)],
        [(z, y, x, 1 - core)],
    )


def send_half(half, row_of, landed, send_sem, recv_sem):
    def send(there):
        pltpu.make_async_remote_copy(
            src_ref=row_of(there),
            dst_ref=landed,
            send_sem=send_sem,
            recv_sem=recv_sem,
            device_id=target_of(*there),
            device_id_type=MESH,
        ).start()

    for_others(half, send)


def await_bytes(like, sem):
    pltpu.make_async_copy(like, like, sem).wait()


def label_copies(stage, all_labels, send_sems, recv_sems):
    z, y, x, core = here()
    part = (
        all_labels.at[core, x, y, z],
        all_labels.at[core, x, y],
        all_labels.at[core, x],
        all_labels.at[core],
    )[stage]
    first = (0, 7, 10, 13)[stage]
    peers = lines()[stage]
    return [
        pltpu.make_async_remote_copy(
            src_ref=part,
            dst_ref=part,
            send_sem=send_sems.at[first + k],
            recv_sem=recv_sems.at[first + k],
            device_id=target_of(*peer),
            device_id_type=MESH,
        )
        for k, peer in enumerate(peers)
    ]


def step_kernel(
    row_ids,
    slots,
    stencil_z,
    fractions,
    atom_count,
    features,
    w_in,
    w_out,
    basis,
    basis_t,
    tabs,
    forces,
    grads,
    ids_cols,
    bins_cols,
    own_labels,
    all_labels,
    charges,
    corner,
    tab_x,
    tab_y,
    tab_z,
    z_high,
    z_low,
    mesh_rows,
    sent,
    arrived,
    rows_high,
    rows_low,
    labels_t,
    labels_x,
    onehot_y,
    plane,
    fields,
    cells,
    replies_t,
    replies,
    returned,
    spare,
    spare_two,
    lifts,
    kernel,
    field_high,
    field_low,
    weights,
    label_send,
    label_recv,
    sem_own,
    send_one,
    recv_one,
    send_two,
    recv_two,
):
    barrier = pltpu.get_barrier_semaphore()
    for peers in lines():
        for peer in peers:
            pl.semaphore_signal(barrier, inc=1, device_id=target_of(*peer), device_id_type=MESH)
    z, y, x, core = here()
    low = place_of(z, y, x, 0)
    bin_labels(row_ids, ids_cols, bins_cols)
    for c in range(ROWS // 128):
        part = jnp.transpose(bins_cols[c * 128 : (c + 1) * 128, :])
        own_labels[0:1, c * 128 : (c + 1) * 128] = part[0:1, :]
    pl.semaphore_wait(barrier, 14)
    mine = pltpu.make_async_copy(own_labels.at[0], all_labels.at[core, x, y, z], sem_own)
    mine.start()
    mine.wait()

    def labels_on(stage):
        if stage > 0:
            for copy in label_copies(stage - 1, all_labels, label_send, label_recv):
                copy.wait()
        if stage < 4:
            for copy in label_copies(stage, all_labels, label_send, label_recv):
                copy.start()

    labels_on(0)
    corners(slots, ids_cols, corner)
    class_weights(corner, fractions, tab_x, tab_y, True)
    class_weights_z(stencil_z, fractions, tab_z, True)
    for c in range(ATOMS // CHUNK):
        lanes = slice(c * CHUNK, (c + 1) * CHUNK)
        pre, sigma, out_w = hidden(features, w_in, w_out, lanes)
        charge = jnp.sum(pre * sigma * out_w, axis=0, keepdims=True)
        atom = lax.broadcasted_iota(jnp.int32, (1, CHUNK), 1) + c * CHUNK
        charges[0:1, lanes] = jnp.where(atom < atom_count[0], charge, 0.0)
        lifts[:, lanes] = (sigma * (1.0 + pre * (1.0 - sigma)) * out_w).astype(BF16)
    labels_on(1)
    for c in range(ATOMS // CHUNK):
        lanes = slice(c * CHUNK, (c + 1) * CHUNK)
        row_weights(tab_x, tab_y, bins_cols, lanes, [weights.at[k, c] for k in range(2)], 0, 1)
        key = tab_z[8:16, lanes]
        amount = tab_z[0:8, lanes] * charges[0:1, lanes]
        amount_high = amount.astype(BF16).astype(F32)
        amount_low = amount - amount_high
        for h in range(0, 32, 2):
            rows = slice(h * 8, h * 8 + 16)
            hits = (key == float(h), key == float(h + 1))
            z_high[rows, :] = jnp.concatenate(
                [jnp.where(hit, amount_high, 0.0) for hit in hits], axis=0
            ).astype(BF16)
            z_low[rows, :] = jnp.concatenate(
                [jnp.where(hit, amount_low, 0.0) for hit in hits], axis=0
            ).astype(BF16)
        total = dot3((z_high[...], z_low[...]), (weights[0, c], weights[1, c]), NT)
        if c == 0:
            mesh_rows[...] = total
        else:
            mesh_rows[...] += total
        if c in (0, 2):
            labels_on(2 + c // 2)
    sent[...] = dot3((basis[0], basis[1]), split(mesh_rows[...]))
    labels_on(4)
    own = sent.at[core * 128 + low]
    pltpu.make_async_copy(own, arrived.at[0, low], recv_one.at[0]).start()
    pltpu.make_async_copy(own, spare, send_one).start()
    for half in range(2):
        send_half(
            half,
            lambda there: sent.at[place_of(*there)],
            arrived.at[half, low],
            send_one,
            recv_one.at[half],
        )

    cell_y = lax.broadcasted_iota(jnp.int32, (32, 128), 0).astype(F32)
    for half in range(2):
        for c in range(ROWS // 128):
            bins = slice(c * 128, (c + 1) * 128)
            part = all_labels[lax.rem(core + half, 2), :, :, :, bins].reshape(128, 128)
            part = jnp.transpose(part)
            labels_t[half, bins, :] = part.astype(jnp.int32)
            labels_x[half, bins, :] = jnp.floor(part * (1.0 / 32.0))

        @pl.loop(0, 32)
        def _(xb):
            for rank in range(2):
                at = pl.ds(pl.multiple_of(rank * 256 + xb * 8, 8), 8)
                label_y = (labels_t[half, at, :] & 31).astype(F32)
                for yb in range(8):
                    hit = jnp.broadcast_to(label_y[yb : yb + 1], (32, 128)) == cell_y
                    onehot_y[half, xb * 8 + yb, :, rank * 128 : (rank + 1) * 128] = jnp.where(
                        hit, 1.0, 0.0
                    ).astype(BF16)

    for c in range(ATOMS // CHUNK):
        lanes = slice(c * CHUNK, (c + 1) * CHUNK)
        row_weights(tab_x, tab_y, bins_cols, lanes, [weights.at[k, c] for k in range(2, 6)], 1, 3)
    coulomb(kernel, core * 128 + low)
    for half in range(2):
        await_bytes(arrived.at[half], recv_one.at[half])
        for c in range(ROWS // 128):
            bins = slice(c * 128, (c + 1) * 128)
            part = jnp.transpose(arrived[half, :, bins])
            part_high = part.astype(BF16).astype(F32)
            rows_high[half, bins, :] = part_high
            rows_low[half, bins, :] = part - part_high
        gather_plane(half, rows_high, rows_low, labels_x, onehot_y, plane)
    solve_plane(tabs, kernel, plane, fields)
    spread_cells(fields, cells)
    own = replies.at[0, low]
    for half in range(2):
        answer(half, cells, labels_t, replies_t)
        for c in range(ROWS // 128):
            bins = slice(c * 128, (c + 1) * 128)
            replies[half, :, bins] = jnp.transpose(replies_t[half, bins, :])
        if half == 0:
            pltpu.make_async_copy(own, returned.at[core * 128 + low], recv_two).start()
            pltpu.make_async_copy(own, spare_two, send_two).start()
        send_half(
            half,
            lambda there: replies.at[half, place_of(there[0], there[1], there[2], 0)],
            returned.at[core * 128 + low],
            send_two,
            recv_two,
        )
    await_bytes(sent, send_one)
    await_bytes(returned, recv_two)

    field_high[...], field_low[...] = split(
        dot3((basis_t[0], basis_t[1]), split(returned[...]))
    )
    for c in range(ATOMS // CHUNK):
        lanes = slice(c * CHUNK, (c + 1) * CHUNK)
        key = tab_z[8:16, lanes]
        sums = []
        for k in range(3):
            total = dot3(
                (field_high[...], field_low[...]), (weights[2 * k, c], weights[2 * k + 1, c])
            )
            chosen = jnp.zeros((8, CHUNK), F32)
            for h in range(32):
                chosen = jnp.where(key == float(h), total[h * 8 : (h + 1) * 8], chosen)
            sums.append(chosen)
        wz = tab_z[0:8, lanes]
        potential = jnp.sum(wz * sums[0], axis=0, keepdims=True)
        charge = -charges[0:1, lanes]
        forces[0:1, lanes] = charge * jnp.sum(wz * sums[1], axis=0, keepdims=True)
        forces[1:2, lanes] = charge * jnp.sum(wz * sums[2], axis=0, keepdims=True)
        forces[2:3, lanes] = charge * jnp.sum(tab_z[16:24, lanes] * sums[0], axis=0, keepdims=True)
        atom = lax.broadcasted_iota(jnp.int32, (1, CHUNK), 1) + c * CHUNK
        potential = jnp.where(atom < atom_count[0], potential, 0.0)
        grad = potential * dot(w_in[...], lifts[:, lanes])
        for b in range(CHUNK // 128):
            rows = slice(c * CHUNK + b * 128, c * CHUNK + (b + 1) * 128)
            grads[rows, :] = jnp.transpose(grad[:, b * 128 : (b + 1) * 128]).astype(BF16)
    await_bytes(returned, send_two)


def coulomb(kernel, wave_index):
    half = GRID // 2

    def wave(index):
        return jnp.where(index <= half, index, index - half)

    wave_x = wave(lax.broadcasted_iota(jnp.int32, (GRID, GRID), 0))
    wave_y = wave(lax.broadcasted_iota(jnp.int32, (GRID, GRID), 1))
    wave_z = wave(wave_index)
    squared = (wave_x * wave_x + wave_y * wave_y + wave_z * wave_z).astype(F32)
    damped = jnp.exp(-((SMOOTH * math.pi / GRID) ** 2) * squared)
    values = COUPLE * damped * (GRID * GRID) / (4.0 * math.pi * math.pi * jnp.maximum(squared, 1.0))
    keep = (squared > 0) & (wave_x != half) & (wave_y != half) & (wave_z != half)
    kernel[...] = jnp.where(keep, values, 0.0)


def gather_plane(half, rows_high, rows_low, labels_x, onehot_y, plane):
    lane_class = lax.broadcasted_iota(jnp.int32, (8, 128), 0).astype(F32)

    @pl.loop(0, 32)
    def _(xb):
        pieces = []
        for yb in range(8):
            high, low = [], []
            for rank in range(2):
                at = pl.ds(rank * 256 + xb * 8 + yb, 1)
                hit = jnp.broadcast_to(labels_x[half, at, :], (8, 128)) == lane_class
                high.append(jnp.where(hit, jnp.broadcast_to(rows_high[half, at, :], (8, 128)), 0.0))
                low.append(jnp.where(hit, jnp.broadcast_to(rows_low[half, at, :], (8, 128)), 0.0))
            left = [jnp.concatenate([high[r], low[r]], axis=0).astype(BF16) for r in range(2)]
            piece = dot(jnp.concatenate(left, axis=1), onehot_y[half, xb * 8 + yb], NT)
            pieces.append(piece[0:8] + piece[8:16])
        at = pl.ds(pl.multiple_of(xb * 8, 8), 8)
        total = jnp.concatenate(pieces, axis=1)
        if half == 0:
            plane[at, :] = total
        else:
            plane[at, :] += total


def solve_plane(tabs, kernel, plane, fields):
    along_x, back_x, along_y = [(tabs[2 * k], tabs[2 * k + 1]) for k in range(3)]
    spectrum = dot3(along_x, split(plane[...]))
    spectrum = dot3(split(spectrum), along_y, NT) * kernel[...]
    field = dot3(back_x, split(spectrum))
    field = dot3(split(field), along_y)
    fields[0] = field[:, :128]
    fields[1] = field[:, 128:]


def spread_cells(fields, cells):
    block = lax.broadcasted_iota(jnp.int32, (32, 128), 1) // 32
    for yb in range(8):
        for h in range(2):
            chosen = None
            for q in range(4):
                part = fields[yb // 4, pl.ds(4 * h + q, 32, stride=8), :]
                shift = (q - yb % 4) % 4 * 32
                part = pltpu.roll(part, shift, 1) if shift else part
                chosen = part if q == 0 else jnp.where(block == q, part, chosen)
            cells[yb, h] = chosen


def answer(half, cells, labels_t, replies_t):
    for yb in range(8):
        for rank in range(2):
            at = pl.ds(rank * 256 + yb, 32, stride=8)
            label = labels_t[half, at, :]
            index = label & 127
            upper = label >> 7
            value = jnp.zeros((32, 128), F32)
            for h in range(2):
                taken = jnp.take_along_axis(cells[yb, h], index, axis=1, mode="promise_in_bounds")
                value = jnp.where(upper == h, taken, value)
            replies_t[half, at, :] = value


VM = pl.BlockSpec(memory_space=pltpu.VMEM)
SM = pl.BlockSpec(memory_space=pltpu.SMEM)


def local(features, fractions, row_ids, stencil_slots, stencil_z, atom_count, w_in, w_out):
    basis, basis_t, plane = [jnp.asarray(table) for table in tables()]
    vmem = pltpu.VMEM
    chunks = ATOMS // CHUNK
    return pl.pallas_call(
        step_kernel,
        out_shape=(
            jax.ShapeDtypeStruct((3, ATOMS), F32),
            jax.ShapeDtypeStruct((ATOMS, 128), BF16),
        ),
        in_specs=[VM] * 4 + [SM] + [VM] * 6,
        out_specs=(VM, VM),
        scratch_shapes=[
            vmem((ROWS, 128), F32),
            vmem((ROWS, 128), F32),
            vmem((8, ROWS), F32),
            vmem((2, 4, 4, 8, ROWS), F32),
            vmem((1, ATOMS), F32),
            vmem((1, ATOMS), jnp.int32),
            vmem((3, 32, ATOMS), F32),
            vmem((24, ATOMS), F32),
            vmem((24, ATOMS), F32),
            vmem((GRID, CHUNK), BF16),
            vmem((GRID, CHUNK), BF16),
            vmem((GRID, ROWS), F32),
            vmem((DEVICES, ROWS), F32),
            vmem((2, 128, ROWS), F32),
            vmem((2, ROWS, 128), F32),
            vmem((2, ROWS, 128), F32),
            vmem((2, ROWS, 128), jnp.int32),
            vmem((2, ROWS, 128), F32),
            vmem((2, GRID, 32, 256), BF16),
            vmem((GRID, GRID), F32),
            vmem((2, GRID, 128), F32),
            vmem((8, 2, 32, 128), F32),
            vmem((2, ROWS, 128), F32),
            vmem((2, 128, ROWS), F32),
            vmem((DEVICES, ROWS), F32),
            vmem((ROWS,), F32),
            vmem((ROWS,), F32),
            vmem((128, ATOMS), BF16),
            vmem((GRID, GRID), F32),
            vmem((GRID, ROWS), BF16),
            vmem((GRID, ROWS), BF16),
            vmem((6, chunks, ROWS, CHUNK), BF16),
            pltpu.SemaphoreType.DMA((14,)),
            pltpu.SemaphoreType.DMA((14,)),
        ]
        + [
            pltpu.SemaphoreType.DMA,
            pltpu.SemaphoreType.DMA,
            pltpu.SemaphoreType.DMA((2,)),
            pltpu.SemaphoreType.DMA,
            pltpu.SemaphoreType.DMA,
        ],
        compiler_params=pltpu.CompilerParams(
            vmem_limit_bytes=VMEM_LIMIT, collective_id=0, has_side_effects=True
        ),
        name="step",
    )(
        row_ids,
        stencil_slots,
        stencil_z.reshape(1, ATOMS),
        fractions,
        atom_count,
        features,
        w_in,
        w_out.reshape(1, 128),
        basis,
        basis_t,
        plane,
    )


def solution(mesh):
    placed = (
        P(("pen", "slab"), None),
        P(None, ("pen", "slab")),
        P(("pen", "slab"), None),
        P(None, ("pen", "slab")),
        P(("pen", "slab")),
        P(("pen", "slab")),
        P(),
        P(),
    )
    return jax.shard_map(
        local,
        mesh=mesh,
        in_specs=placed,
        out_specs=(P(None, ("pen", "slab")), P(("pen", "slab"), None)),
        check_vma=False,
    )
```

```python
import functools
import math

import jax
import jax.numpy as jnp
import ml_dtypes
import numpy as np
from jax import lax
from jax.experimental import pallas as pl
from jax.experimental.pallas import tpu as pltpu
from jax.sharding import PartitionSpec as P

GRID = 256
COUPLE = 8.0
SMOOTH = 1.0
ROWS = 512
ATOMS = 2048
DEVICES = 256
CHUNK = 512
VMEM_LIMIT = 56 * 1024 * 1024
F32 = jnp.float32
BF16 = jnp.bfloat16

NN = (((1,), (0,)), ((), ()))
NT = (((1,), (1,)), ((), ()))


def dot(left, right, dims=NN):
    return lax.dot_general(left, right, dims, preferred_element_type=F32)


def split(value):
    high = value.astype(BF16)
    low = (value - high.astype(F32)).astype(BF16)
    return (high, low)


def dot3(left, right, dims=NN):
    return (
        dot(left[0], right[0], dims)
        + dot(left[0], right[1], dims)
        + dot(left[1], right[0], dims)
    )


def fourier_basis():
    cell = np.arange(GRID)
    wave = np.arange(GRID)
    wave = np.where(wave <= GRID // 2, wave, wave - GRID // 2)
    angle = 2.0 * np.pi * ((wave[:, None] * cell[None, :]) % GRID) / GRID
    basis = np.where(np.arange(GRID)[:, None] <= GRID // 2, np.cos(angle), np.sin(angle))
    scale = np.where((np.arange(GRID) == 0) | (np.arange(GRID) == GRID // 2), 1.0, 2.0)
    return basis * np.sqrt(scale / GRID)[:, None]


def split_table(table):
    table = table.astype(np.float32)
    high = table.astype(ml_dtypes.bfloat16)
    low = (table - high.astype(np.float32)).astype(ml_dtypes.bfloat16)
    return [high, low]


def tables():
    basis = fourier_basis()
    place = np.arange(GRID)
    along_x = basis[:, (place % 8) * 32 + place // 8]
    along_y = basis[:, (place % 32) * 8 + place // 32]
    plane = np.stack(split_table(along_x) + split_table(along_x.T) + split_table(along_y))
    return (np.stack(split_table(basis)), np.stack(split_table(basis.T)), plane)


def spline_values(u):
    rest = 1.0 - u
    square = u * u
    cube = square * u
    return (
        rest * rest * rest / 6.0,
        (3.0 * cube - 6.0 * square + 4.0) / 6.0,
        (-3.0 * cube + 3.0 * square + 3.0 * u + 1.0) / 6.0,
        cube / 6.0,
    )


def spline_slopes(u):
    rest = 1.0 - u
    square = u * u
    return (
        -rest * rest / 2.0,
        (3.0 * square - 4.0 * u) / 2.0,
        (-3.0 * square + 2.0 * u + 1.0) / 2.0,
        square / 2.0,
    )


def pick(step, values):
    out = jnp.where(step == 3, values[3], 0.0)
    for k in (2, 1, 0):
        out = jnp.where(step == k, values[k], out)
    return out


def row_to_columns(row):
    return jnp.transpose(jnp.broadcast_to(row, (128, 128)))


def bin_labels(row_ids, ids_cols, bins_cols):
    ids = row_ids[...]
    used = ids >= 0
    x = ids >> 8
    y = ids & 255
    group = jnp.where(used, (x & 31) * 8 + (y & 7), -1)
    label = ((x >> 5) * 32 + (y >> 3)).astype(F32)
    place = lax.broadcasted_iota(jnp.int32, (128, ROWS), 1)
    row = lax.broadcasted_iota(jnp.int32, (128, ROWS), 0)
    rank = jnp.zeros((1, ROWS), F32)
    for c in range(ROWS // 128):
        lanes = slice(c * 128, (c + 1) * 128)
        column = row_to_columns(ids[:, lanes])
        ids_cols[lanes, :] = column.astype(F32)
        column = (column >> 8 & 31) * 8 + (column & 7)
        column = jnp.concatenate([column] * (ROWS // 128), axis=1)
        same = (column == group) & (row + c * 128 < place)
        rank += jnp.sum(jnp.where(same, 1.0, 0.0), axis=0, keepdims=True)
    target = jnp.where(used, rank.astype(jnp.int32) * 256 + group, -1)
    for c in range(ROWS // 128):
        hit = target == row + c * 128
        value = jnp.sum(jnp.where(hit, label + 1.0, 0.0), axis=1, keepdims=True) - 1.0
        bins_cols[c * 128 : (c + 1) * 128, :] = jnp.broadcast_to(value, (128, 128))


def corners(slots, ids_cols, corner):
    row = lax.broadcasted_iota(jnp.int32, (ROWS, 128), 0)
    for c in range(ATOMS // 128):
        lanes = slice(c * 128, (c + 1) * 128)
        hit = slots[0:1, lanes] == row
        value = jnp.sum(jnp.where(hit, ids_cols[...], 0.0), axis=0, keepdims=True)
        corner[0:1, lanes] = value.astype(jnp.int32)


def class_weights(corner, fractions, tab_x, tab_y, slopes):
    x0 = corner[0:1, :] >> 8
    y0 = corner[0:1, :] & 255
    value_x = spline_values(fractions[0:1, :])
    value_y = spline_values(fractions[1:2, :])
    step_y = (lax.broadcasted_iota(jnp.int32, (8, ATOMS), 0) - y0) & 7
    tab_y[0:8, :] = pick(step_y, value_y)
    tab_y[8:16, :] = ((((y0 + step_y) >> 3) & 31)).astype(F32)
    if slopes:
        slope_x = spline_slopes(fractions[0:1, :])
        slope_y = spline_slopes(fractions[1:2, :])
        tab_y[16:24, :] = pick(step_y, slope_y)
    for b in range(4):
        rows = slice(b * 8, (b + 1) * 8)
        step_x = (lax.broadcasted_iota(jnp.int32, (8, ATOMS), 0) + b * 8 - x0) & 31
        tab_x[0, rows, :] = pick(step_x, value_x)
        tab_x[1, rows, :] = ((((x0 + step_x) >> 5) & 7) * 32).astype(F32)
        if slopes:
            tab_x[2, rows, :] = pick(step_x, slope_x)


def class_weights_z(stencil_z, fractions, tab_z, slopes):
    z0 = stencil_z[0:1, :]
    step_z = (lax.broadcasted_iota(jnp.int32, (8, ATOMS), 0) - z0) & 7
    tab_z[0:8, :] = pick(step_z, spline_values(fractions[2:3, :]))
    tab_z[8:16, :] = ((((z0 + step_z) >> 3) & 31)).astype(F32)
    if slopes:
        tab_z[16:24, :] = pick(step_z, spline_slopes(fractions[2:3, :]))


def row_weights(tab_x, tab_y, bins_cols, lanes, outs, first, last):
    def twice(part):
        return jnp.concatenate([part, part], axis=0)

    wy = twice(tab_y[0:8, lanes])
    ky = twice(tab_y[8:16, lanes])
    sy = twice(tab_y[16:24, lanes])
    width = wy.shape[1]

    def pair(index, i):
        rows = [tab_x[index, pl.ds(2 * i + k, 1), lanes] for k in range(2)]
        return jnp.concatenate([jnp.broadcast_to(row, (8, width)) for row in rows], axis=0)

    @pl.loop(0, 16)
    def _(i):
        wx = pair(0, i)
        key = pair(1, i) + ky
        values = [wx * wy, pair(2, i) * wy, wx * sy][first:last]
        for rank in range(2):
            rows = pl.ds(pl.multiple_of(rank * 256 + i * 16, 16), 16)
            label = bins_cols[rows, :]
            label = jnp.concatenate([label] * (width // 128), axis=1)
            hit = key == label
            for k, value in enumerate(values):
                high, low = split(jnp.where(hit, value, 0.0))
                outs[2 * k][rows, :] = high
                outs[2 * k + 1][rows, :] = low


def hidden(features, w_in, w_out, lanes):
    w_in_t = jnp.transpose(w_in[...].astype(F32)).astype(BF16)
    pre = dot(w_in_t, features[lanes, :], NT)
    sigma = jax.nn.sigmoid(pre)
    out_w = row_to_columns(w_out[...])
    out_w = jnp.concatenate([out_w] * (pre.shape[1] // 128), axis=1)
    return (pre, sigma, out_w)


MESH = pl.DeviceIdType.MESH
DZ = (4, 1, 7, 2, 6, 3, 5, 0)


def here():
    pen = lax.axis_index("pen")
    slab = lax.axis_index("slab")
    return (pen // 4, lax.rem(pen, 4), slab // 2, lax.rem(slab, 2))


def place_of(z, y, x, core):
    return ((core * 4 + x) * 4 + y) * 8 + z


def target_of(z, y, x, core):
    return (z * 4 + y, x * 2 + core)


def for_others(half, visit):
    z, y, x, core = here()
    other_core = lax.rem(core + half, 2)

    @pl.loop(0, 16)
    def _(k):
        other_y = lax.rem(y + lax.rem(k, 4), 4)
        other_x = lax.rem(x + k // 4, 4)
        for dz in DZ:
            there = (lax.rem(z + dz, 8), other_y, other_x, other_core)
            if dz == 0 and half == 0:
                pl.when(k > 0)(functools.partial(visit, there))
            else:
                visit(there)


def lines():
    z, y, x, core = here()
    return (
        [(lax.rem(z + k, 8), y, x, core) for k in range(1, 8)],
        [(z, lax.rem(y + k, 4), x, core) for k in range(1, 4)],
        [(z, y, lax.rem(x + k, 4), core) for k in range(1, 4)],
        [(z, y, x, 1 - core)],
    )


def send_half(half, row_of, landed, send_sem, recv_sem):
    def send(there):
        pltpu.make_async_remote_copy(
            src_ref=row_of(there),
            dst_ref=landed,
            send_sem=send_sem,
            recv_sem=recv_sem,
            device_id=target_of(*there),
            device_id_type=MESH,
        ).start()

    for_others(half, send)


def await_bytes(like, sem):
    pltpu.make_async_copy(like, like, sem).wait()


def label_copies(stage, all_labels, send_sems, recv_sems):
    z, y, x, core = here()
    part = (
        all_labels.at[core, x, y, z],
        all_labels.at[core, x, y],
        all_labels.at[core, x],
        all_labels.at[core],
    )[stage]
    first = (0, 7, 10, 13)[stage]
    peers = lines()[stage]
    return [
        pltpu.make_async_remote_copy(
            src_ref=part,
            dst_ref=part,
            send_sem=send_sems.at[first + k],
            recv_sem=recv_sems.at[first + k],
            device_id=target_of(*peer),
            device_id_type=MESH,
        )
        for k, peer in enumerate(peers)
    ]


def step_kernel(
    row_ids,
    slots,
    stencil_z,
    fractions,
    atom_count,
    features,
    w_in,
    w_out,
    basis,
    basis_t,
    tabs,
    forces,
    grads,
    ids_cols,
    bins_cols,
    own_labels,
    all_labels,
    charges,
    corner,
    tab_x,
    tab_y,
    tab_z,
    z_high,
    z_low,
    mesh_rows,
    sent,
    arrived,
    rows_high,
    rows_low,
    labels_t,
    labels_x,
    onehot_y,
    crossed,
    plane,
    fields,
    cells,
    replies_t,
    replies,
    returned,
    spare,
    spare_two,
    lifts,
    kernel,
    field_high,
    field_low,
    weights,
    label_send,
    label_recv,
    line_sems,
    sem_own,
    send_one,
    recv_one,
    send_two,
    recv_two,
):
    barrier = pltpu.get_barrier_semaphore()
    for peers in lines():
        for peer in peers:
            pl.semaphore_signal(barrier, inc=1, device_id=target_of(*peer), device_id_type=MESH)
    z, y, x, core = here()
    low = place_of(z, y, x, 0)
    bin_labels(row_ids, ids_cols, bins_cols)
    for c in range(ROWS // 128):
        part = jnp.transpose(bins_cols[c * 128 : (c + 1) * 128, :])
        own_labels[0:1, c * 128 : (c + 1) * 128] = part[0:1, :]
    pl.semaphore_wait(barrier, 14)
    mine = pltpu.make_async_copy(own_labels.at[0], all_labels.at[core, x, y, z], sem_own)
    mine.start()
    mine.wait()

    def labels_on(stage):
        if stage > 0:
            for copy in label_copies(stage - 1, all_labels, label_send, label_recv):
                copy.wait()
        if stage < 4:
            for copy in label_copies(stage, all_labels, label_send, label_recv):
                copy.start()

    def heard_from(stage):
        if stage > 0:
            pl.semaphore_wait(line_sems.at[stage - 1], (3, 3, 1)[stage - 1])
        if stage < 3:
            for peer in lines()[stage + 1]:
                pl.semaphore_signal(
                    line_sems.at[stage], inc=1, device_id=target_of(*peer), device_id_type=MESH
                )

    heard_from(0)
    labels_on(0)
    corners(slots, ids_cols, corner)
    class_weights(corner, fractions, tab_x, tab_y, True)
    class_weights_z(stencil_z, fractions, tab_z, True)
    for c in range(ATOMS // CHUNK):
        lanes = slice(c * CHUNK, (c + 1) * CHUNK)
        pre, sigma, out_w = hidden(features, w_in, w_out, lanes)
        charge = jnp.sum(pre * sigma * out_w, axis=0, keepdims=True)
        atom = lax.broadcasted_iota(jnp.int32, (1, CHUNK), 1) + c * CHUNK
        charges[0:1, lanes] = jnp.where(atom < atom_count[0], charge, 0.0)
        lifts[:, lanes] = (sigma * (1.0 + pre * (1.0 - sigma)) * out_w).astype(BF16)
    heard_from(1)
    labels_on(1)
    for c in range(ATOMS // CHUNK):
        lanes = slice(c * CHUNK, (c + 1) * CHUNK)
        row_weights(tab_x, tab_y, bins_cols, lanes, [weights.at[k, c] for k in range(2)], 0, 1)
        key = tab_z[8:16, lanes]
        amount = tab_z[0:8, lanes] * charges[0:1, lanes]
        amount_high = amount.astype(BF16).astype(F32)
        amount_low = amount - amount_high
        for h in range(0, 32, 2):
            rows = slice(h * 8, h * 8 + 16)
            hits = (key == float(h), key == float(h + 1))
            z_high[rows, :] = jnp.concatenate(
                [jnp.where(hit, amount_high, 0.0) for hit in hits], axis=0
            ).astype(BF16)
            z_low[rows, :] = jnp.concatenate(
                [jnp.where(hit, amount_low, 0.0) for hit in hits], axis=0
            ).astype(BF16)
        total = dot3((z_high[...], z_low[...]), (weights[0, c], weights[1, c]), NT)
        if c == 0:
            mesh_rows[...] = total
        else:
            mesh_rows[...] += total
        if c == 1:
            heard_from(2)
            labels_on(2)
    sent[...] = dot3((basis[0], basis[1]), split(mesh_rows[...]))
    heard_from(3)
    own = sent.at[core * 128 + low]
    pltpu.make_async_copy(own, arrived.at[0, low], recv_one.at[0]).start()
    pltpu.make_async_copy(own, spare, send_one).start()
    for half in range(2):
        send_half(
            half,
            lambda there: sent.at[place_of(*there)],
            arrived.at[half, low],
            send_one,
            recv_one.at[half],
        )
        if half == 0:
            labels_on(3)
    for c in range(ATOMS // CHUNK):
        lanes = slice(c * CHUNK, (c + 1) * CHUNK)
        row_weights(tab_x, tab_y, bins_cols, lanes, [weights.at[k, c] for k in range(2, 6)], 1, 3)
    coulomb(kernel, core * 128 + low)
    labels_on(4)
    cell_y = lax.broadcasted_iota(jnp.int32, (32, 128), 0).astype(F32)
    for half in range(2):
        for c in range(ROWS // 128):
            bins = slice(c * 128, (c + 1) * 128)
            part = all_labels[lax.rem(core + half, 2), :, :, :, bins].reshape(128, 128)
            part = jnp.transpose(part)
            labels_t[half, bins, :] = part.astype(jnp.int32)
            labels_x[half, bins, :] = jnp.floor(part * (1.0 / 32.0))

        @pl.loop(0, 32)
        def _(xb):
            for rank in range(2):
                at = pl.ds(pl.multiple_of(rank * 256 + xb * 8, 8), 8)
                label_y = (labels_t[half, at, :] & 31).astype(F32)
                for yb in range(8):
                    hit = jnp.broadcast_to(label_y[yb : yb + 1], (32, 128)) == cell_y
                    onehot_y[half, xb, yb * 32 : yb * 32 + 32, rank * 128 : rank * 128 + 128] = jnp.where(
                        hit, 1.0, 0.0
                    ).astype(BF16)

    for half in range(2):
        await_bytes(arrived.at[half], recv_one.at[half])
        for c in range(ROWS // 128):
            bins = slice(c * 128, (c + 1) * 128)
            part = jnp.transpose(arrived[half, :, bins])
            part_high = part.astype(BF16).astype(F32)
            rows_high[half, bins, :] = part_high
            rows_low[half, bins, :] = part - part_high
        gather_plane(half, rows_high, rows_low, labels_x, onehot_y, crossed)
    keep_matching(crossed, plane)
    solve_plane(tabs, kernel, plane, fields)
    spread_cells(fields, cells)
    own = replies.at[0, low]
    for half in range(2):
        answer(half, cells, labels_t, replies_t)
        for c in range(ROWS // 128):
            bins = slice(c * 128, (c + 1) * 128)
            replies[half, :, bins] = jnp.transpose(replies_t[half, bins, :])
        if half == 0:
            pltpu.make_async_copy(own, returned.at[core * 128 + low], recv_two).start()
            pltpu.make_async_copy(own, spare_two, send_two).start()
        send_half(
            half,
            lambda there: replies.at[half, place_of(there[0], there[1], there[2], 0)],
            returned.at[core * 128 + low],
            send_two,
            recv_two,
        )
    await_bytes(sent, send_one)
    await_bytes(returned, recv_two)

    field_high[...], field_low[...] = split(
        dot3((basis_t[0], basis_t[1]), split(returned[...]))
    )
    for c in range(ATOMS // CHUNK):
        lanes = slice(c * CHUNK, (c + 1) * CHUNK)
        key = tab_z[8:16, lanes]
        sums = []
        for k in range(3):
            total = dot3(
                (field_high[...], field_low[...]), (weights[2 * k, c], weights[2 * k + 1, c])
            )
            chosen = jnp.zeros((8, CHUNK), F32)
            for h in range(32):
                chosen = jnp.where(key == float(h), total[h * 8 : (h + 1) * 8], chosen)
            sums.append(chosen)
        wz = tab_z[0:8, lanes]
        potential = jnp.sum(wz * sums[0], axis=0, keepdims=True)
        charge = -charges[0:1, lanes]
        forces[0:1, lanes] = charge * jnp.sum(wz * sums[1], axis=0, keepdims=True)
        forces[1:2, lanes] = charge * jnp.sum(wz * sums[2], axis=0, keepdims=True)
        forces[2:3, lanes] = charge * jnp.sum(tab_z[16:24, lanes] * sums[0], axis=0, keepdims=True)
        atom = lax.broadcasted_iota(jnp.int32, (1, CHUNK), 1) + c * CHUNK
        potential = jnp.where(atom < atom_count[0], potential, 0.0)
        grad = potential * dot(w_in[...], lifts[:, lanes])
        for b in range(CHUNK // 128):
            rows = slice(c * CHUNK + b * 128, c * CHUNK + (b + 1) * 128)
            grads[rows, :] = jnp.transpose(grad[:, b * 128 : (b + 1) * 128]).astype(BF16)
    await_bytes(returned, send_two)


def coulomb(kernel, wave_index):
    half = GRID // 2

    def wave(index):
        return jnp.where(index <= half, index, index - half)

    wave_x = wave(lax.broadcasted_iota(jnp.int32, (GRID, GRID), 0))
    wave_y = wave(lax.broadcasted_iota(jnp.int32, (GRID, GRID), 1))
    wave_z = wave(wave_index)
    squared = (wave_x * wave_x + wave_y * wave_y + wave_z * wave_z).astype(F32)
    damped = jnp.exp(-((SMOOTH * math.pi / GRID) ** 2) * squared)
    values = COUPLE * damped * (GRID * GRID) / (4.0 * math.pi * math.pi * jnp.maximum(squared, 1.0))
    keep = (squared > 0) & (wave_x != half) & (wave_y != half) & (wave_z != half)
    kernel[...] = jnp.where(keep, values, 0.0)


def gather_plane(half, rows_high, rows_low, labels_x, onehot_y, crossed):
    @pl.loop(0, 32)
    def _(xb):
        left = []
        for rank in range(2):
            at = pl.ds(pl.multiple_of(rank * 256 + xb * 8, 8), 8)
            high, low = rows_high[half, at, :], rows_low[half, at, :]
            label_x = labels_x[half, at, :]
            hits = [label_x == float(h) for h in range(8)]
            parts = [jnp.where(hit, part, 0.0) for part in (high, low) for hit in hits]
            left.append(jnp.concatenate(parts, axis=0).astype(BF16))
        both = dot(jnp.concatenate(left, axis=1), onehot_y[half, xb], NT)
        total = both[0:64] + both[64:128]
        if half == 0:
            crossed[xb] = total
        else:
            crossed[xb] += total


def keep_matching(crossed, plane):
    lane_class = lax.broadcasted_iota(jnp.int32, (8, GRID), 1) // 32
    match = lane_class == lax.broadcasted_iota(jnp.int32, (8, GRID), 0)
    row = lax.broadcasted_iota(jnp.int32, (8, GRID), 0)

    @pl.loop(0, 32)
    def _(xb):
        total = jnp.zeros((8, GRID), F32)
        for h in range(8):
            part = jnp.where(match, crossed[xb, h * 8 : h * 8 + 8, :], 0.0)
            total = jnp.where(row == h, jnp.sum(part, axis=0, keepdims=True), total)
        plane[pl.ds(pl.multiple_of(xb * 8, 8), 8), :] = total


def solve_plane(tabs, kernel, plane, fields):
    along_x, back_x, along_y = [(tabs[2 * k], tabs[2 * k + 1]) for k in range(3)]
    spectrum = dot3(along_x, split(plane[...]))
    spectrum = dot3(split(spectrum), along_y, NT) * kernel[...]
    field = dot3(back_x, split(spectrum))
    field = dot3(split(field), along_y)
    fields[0] = field[:, :128]
    fields[1] = field[:, 128:]


def spread_cells(fields, cells):
    block = lax.broadcasted_iota(jnp.int32, (32, 128), 1) // 32
    for yb in range(8):
        for h in range(2):
            chosen = None
            for q in range(4):
                part = fields[yb // 4, pl.ds(4 * h + q, 32, stride=8), :]
                shift = (q - yb % 4) % 4 * 32
                part = pltpu.roll(part, shift, 1) if shift else part
                chosen = part if q == 0 else jnp.where(block == q, part, chosen)
            cells[yb, h] = chosen


def answer(half, cells, labels_t, replies_t):
    for yb in range(8):
        for rank in range(2):
            at = pl.ds(rank * 256 + yb, 32, stride=8)
            label = labels_t[half, at, :]
            index = label & 127
            upper = label >> 7
            value = jnp.zeros((32, 128), F32)
            for h in range(2):
                taken = jnp.take_along_axis(cells[yb, h], index, axis=1, mode="promise_in_bounds")
                value = jnp.where(upper == h, taken, value)
            replies_t[half, at, :] = value


VM = pl.BlockSpec(memory_space=pltpu.VMEM)
SM = pl.BlockSpec(memory_space=pltpu.SMEM)


def local(features, fractions, row_ids, stencil_slots, stencil_z, atom_count, w_in, w_out):
    basis, basis_t, plane = [jnp.asarray(table) for table in tables()]
    vmem = pltpu.VMEM
    chunks = ATOMS // CHUNK
    return pl.pallas_call(
        step_kernel,
        out_shape=(
            jax.ShapeDtypeStruct((3, ATOMS), F32),
            jax.ShapeDtypeStruct((ATOMS, 128), BF16),
        ),
        in_specs=[VM] * 4 + [SM] + [VM] * 6,
        out_specs=(VM, VM),
        scratch_shapes=[
            vmem((ROWS, 128), F32),
            vmem((ROWS, 128), F32),
            vmem((8, ROWS), F32),
            vmem((2, 4, 4, 8, ROWS), F32),
            vmem((1, ATOMS), F32),
            vmem((1, ATOMS), jnp.int32),
            vmem((3, 32, ATOMS), F32),
            vmem((24, ATOMS), F32),
            vmem((24, ATOMS), F32),
            vmem((GRID, CHUNK), BF16),
            vmem((GRID, CHUNK), BF16),
            vmem((GRID, ROWS), F32),
            vmem((DEVICES, ROWS), F32),
            vmem((2, 128, ROWS), F32),
            vmem((2, ROWS, 128), F32),
            vmem((2, ROWS, 128), F32),
            vmem((2, ROWS, 128), jnp.int32),
            vmem((2, ROWS, 128), F32),
            vmem((2, 32, GRID, 256), BF16),
            vmem((32, 64, GRID), F32),
            vmem((GRID, GRID), F32),
            vmem((2, GRID, 128), F32),
            vmem((8, 2, 32, 128), F32),
            vmem((2, ROWS, 128), F32),
            vmem((2, 128, ROWS), F32),
            vmem((DEVICES, ROWS), F32),
            vmem((ROWS,), F32),
            vmem((ROWS,), F32),
            vmem((128, ATOMS), BF16),
            vmem((GRID, GRID), F32),
            vmem((GRID, ROWS), BF16),
            vmem((GRID, ROWS), BF16),
            vmem((6, chunks, ROWS, CHUNK), BF16),
            pltpu.SemaphoreType.DMA((14,)),
            pltpu.SemaphoreType.DMA((14,)),
            pltpu.SemaphoreType.REGULAR((3,)),
        ]
        + [
            pltpu.SemaphoreType.DMA,
            pltpu.SemaphoreType.DMA,
            pltpu.SemaphoreType.DMA((2,)),
            pltpu.SemaphoreType.DMA,
            pltpu.SemaphoreType.DMA,
        ],
        compiler_params=pltpu.CompilerParams(
            vmem_limit_bytes=VMEM_LIMIT, collective_id=0, has_side_effects=True
        ),
        name="step",
    )(
        row_ids,
        stencil_slots,
        stencil_z.reshape(1, ATOMS),
        fractions,
        atom_count,
        features,
        w_in,
        w_out.reshape(1, 128),
        basis,
        basis_t,
        plane,
    )


def solution(mesh):
    placed = (
        P(("pen", "slab"), None),
        P(None, ("pen", "slab")),
        P(("pen", "slab"), None),
        P(None, ("pen", "slab")),
        P(("pen", "slab")),
        P(("pen", "slab")),
        P(),
        P(),
    )
    return jax.shard_map(
        local,
        mesh=mesh,
        in_specs=placed,
        out_specs=(P(None, ("pen", "slab")), P(("pen", "slab"), None)),
        check_vma=False,
    )
```

```python
import functools
import math

import jax
import jax.numpy as jnp
import ml_dtypes
import numpy as np
from jax import lax
from jax.experimental import pallas as pl
from jax.experimental.pallas import tpu as pltpu
from jax.sharding import PartitionSpec as P

GRID = 256
COUPLE = 8.0
SMOOTH = 1.0
ROWS = 512
ATOMS = 2048
DEVICES = 256
CHUNK = 512
UNROLL = 8
UNROLL_W = 2
UNROLL_Y = 4
VMEM_LIMIT = 56 * 1024 * 1024
F32 = jnp.float32
BF16 = jnp.bfloat16

NN = (((1,), (0,)), ((), ()))
NT = (((1,), (1,)), ((), ()))


def dot(left, right, dims=NN):
    return lax.dot_general(left, right, dims, preferred_element_type=F32)


def split(value):
    high = value.astype(BF16)
    low = (value - high.astype(F32)).astype(BF16)
    return (high, low)


def dot3(left, right, dims=NN):
    return (
        dot(left[0], right[0], dims)
        + dot(left[0], right[1], dims)
        + dot(left[1], right[0], dims)
    )


def fourier_basis():
    cell = np.arange(GRID)
    wave = np.arange(GRID)
    wave = np.where(wave <= GRID // 2, wave, wave - GRID // 2)
    angle = 2.0 * np.pi * ((wave[:, None] * cell[None, :]) % GRID) / GRID
    basis = np.where(np.arange(GRID)[:, None] <= GRID // 2, np.cos(angle), np.sin(angle))
    scale = np.where((np.arange(GRID) == 0) | (np.arange(GRID) == GRID // 2), 1.0, 2.0)
    return basis * np.sqrt(scale / GRID)[:, None]


def split_table(table):
    table = table.astype(np.float32)
    high = table.astype(ml_dtypes.bfloat16)
    low = (table - high.astype(np.float32)).astype(ml_dtypes.bfloat16)
    return [high, low]


def tables():
    basis = fourier_basis()
    place = np.arange(GRID)
    along_x = basis[:, (place % 8) * 32 + place // 8]
    along_y = basis[:, (place % 32) * 8 + place // 32]
    plane = np.stack(split_table(along_x) + split_table(along_x.T) + split_table(along_y))
    return (np.stack(split_table(basis)), np.stack(split_table(basis.T)), plane)


def spline_values(u):
    rest = 1.0 - u
    square = u * u
    cube = square * u
    return (
        rest * rest * rest / 6.0,
        (3.0 * cube - 6.0 * square + 4.0) / 6.0,
        (-3.0 * cube + 3.0 * square + 3.0 * u + 1.0) / 6.0,
        cube / 6.0,
    )


def spline_slopes(u):
    rest = 1.0 - u
    square = u * u
    return (
        -rest * rest / 2.0,
        (3.0 * square - 4.0 * u) / 2.0,
        (-3.0 * square + 2.0 * u + 1.0) / 2.0,
        square / 2.0,
    )


def pick(step, values):
    out = jnp.where(step == 3, values[3], 0.0)
    for k in (2, 1, 0):
        out = jnp.where(step == k, values[k], out)
    return out


def row_to_columns(row):
    return jnp.transpose(jnp.broadcast_to(row, (128, 128)))


def bin_labels(row_ids, ids_cols, bins_cols):
    ids = row_ids[...]
    used = ids >= 0
    x = ids >> 8
    y = ids & 255
    group = jnp.where(used, (x & 31) * 8 + (y & 7), -1)
    label = ((x >> 5) * 32 + (y >> 3)).astype(F32)
    place = lax.broadcasted_iota(jnp.int32, (128, ROWS), 1)
    row = lax.broadcasted_iota(jnp.int32, (128, ROWS), 0)
    rank = jnp.zeros((1, ROWS), F32)
    for c in range(ROWS // 128):
        lanes = slice(c * 128, (c + 1) * 128)
        column = row_to_columns(ids[:, lanes])
        ids_cols[lanes, :] = column.astype(F32)
        column = (column >> 8 & 31) * 8 + (column & 7)
        column = jnp.concatenate([column] * (ROWS // 128), axis=1)
        same = (column == group) & (row + c * 128 < place)
        rank += jnp.sum(jnp.where(same, 1.0, 0.0), axis=0, keepdims=True)
    target = jnp.where(used, rank.astype(jnp.int32) * 256 + group, -1)
    for c in range(ROWS // 128):
        hit = target == row + c * 128
        value = jnp.sum(jnp.where(hit, label + 1.0, 0.0), axis=1, keepdims=True) - 1.0
        bins_cols[c * 128 : (c + 1) * 128, :] = jnp.broadcast_to(value, (128, 128))


def corners(slots, ids_cols, corner):
    row = lax.broadcasted_iota(jnp.int32, (ROWS, 128), 0)
    for c in range(ATOMS // 128):
        lanes = slice(c * 128, (c + 1) * 128)
        hit = slots[0:1, lanes] == row
        value = jnp.sum(jnp.where(hit, ids_cols[...], 0.0), axis=0, keepdims=True)
        corner[0:1, lanes] = value.astype(jnp.int32)


def class_weights(corner, fractions, tab_x, tab_y, slopes):
    x0 = corner[0:1, :] >> 8
    y0 = corner[0:1, :] & 255
    value_x = spline_values(fractions[0:1, :])
    value_y = spline_values(fractions[1:2, :])
    step_y = (lax.broadcasted_iota(jnp.int32, (8, ATOMS), 0) - y0) & 7
    tab_y[0:8, :] = pick(step_y, value_y)
    tab_y[8:16, :] = ((((y0 + step_y) >> 3) & 31)).astype(F32)
    if slopes:
        slope_x = spline_slopes(fractions[0:1, :])
        slope_y = spline_slopes(fractions[1:2, :])
        tab_y[16:24, :] = pick(step_y, slope_y)
    for b in range(4):
        rows = slice(b * 8, (b + 1) * 8)
        step_x = (lax.broadcasted_iota(jnp.int32, (8, ATOMS), 0) + b * 8 - x0) & 31
        tab_x[0, rows, :] = pick(step_x, value_x)
        tab_x[1, rows, :] = ((((x0 + step_x) >> 5) & 7) * 32).astype(F32)
        if slopes:
            tab_x[2, rows, :] = pick(step_x, slope_x)


def class_weights_z(stencil_z, fractions, tab_z, slopes):
    z0 = stencil_z[0:1, :]
    step_z = (lax.broadcasted_iota(jnp.int32, (8, ATOMS), 0) - z0) & 7
    tab_z[0:8, :] = pick(step_z, spline_values(fractions[2:3, :]))
    tab_z[8:16, :] = ((((z0 + step_z) >> 3) & 31)).astype(F32)
    if slopes:
        tab_z[16:24, :] = pick(step_z, spline_slopes(fractions[2:3, :]))


def row_weights(tab_x, tab_y, bins_cols, lanes, outs, first, last):
    def twice(part):
        return jnp.concatenate([part, part], axis=0)

    wy = twice(tab_y[0:8, lanes])
    ky = twice(tab_y[8:16, lanes])
    sy = twice(tab_y[16:24, lanes])
    width = wy.shape[1]

    def pair(index, i):
        rows = [tab_x[index, pl.ds(2 * i + k, 1), lanes] for k in range(2)]
        return jnp.concatenate([jnp.broadcast_to(row, (8, width)) for row in rows], axis=0)

    def one(i):
        wx = pair(0, i)
        key = pair(1, i) + ky
        values = [wx * wy, pair(2, i) * wy, wx * sy][first:last]
        for rank in range(2):
            rows = pl.ds(pl.multiple_of(rank * 256 + i * 16, 16), 16)
            label = bins_cols[rows, :]
            label = jnp.concatenate([label] * (width // 128), axis=1)
            hit = key == label
            for k, value in enumerate(values):
                high, low = split(jnp.where(hit, value, 0.0))
                outs[2 * k][rows, :] = high
                outs[2 * k + 1][rows, :] = low

    @pl.loop(0, 16 // UNROLL_W)
    def _(step):
        for k in range(UNROLL_W):
            one(step * UNROLL_W + k)


def hidden(features, w_in, w_out, lanes):
    w_in_t = jnp.transpose(w_in[...].astype(F32)).astype(BF16)
    pre = dot(w_in_t, features[lanes, :], NT)
    sigma = jax.nn.sigmoid(pre)
    out_w = row_to_columns(w_out[...])
    out_w = jnp.concatenate([out_w] * (pre.shape[1] // 128), axis=1)
    return (pre, sigma, out_w)


MESH = pl.DeviceIdType.MESH
DZ = (4, 1, 7, 2, 6, 3, 5, 0)


def here():
    pen = lax.axis_index("pen")
    slab = lax.axis_index("slab")
    return (pen // 4, lax.rem(pen, 4), slab // 2, lax.rem(slab, 2))


def place_of(z, y, x, core):
    return ((core * 4 + x) * 4 + y) * 8 + z


def target_of(z, y, x, core):
    return (z * 4 + y, x * 2 + core)


def for_others(half, visit):
    z, y, x, core = here()
    other_core = lax.rem(core + half, 2)

    @pl.loop(0, 16)
    def _(k):
        other_y = lax.rem(y + lax.rem(k, 4), 4)
        other_x = lax.rem(x + k // 4, 4)
        for dz in DZ:
            there = (lax.rem(z + dz, 8), other_y, other_x, other_core)
            if dz == 0 and half == 0:
                pl.when(k > 0)(functools.partial(visit, there))
            else:
                visit(there)


def lines():
    z, y, x, core = here()
    return (
        [(lax.rem(z + k, 8), y, x, core) for k in range(1, 8)],
        [(z, lax.rem(y + k, 4), x, core) for k in range(1, 4)],
        [(z, y, lax.rem(x + k, 4), core) for k in range(1, 4)],
        [(z, y, x, 1 - core)],
    )


def send_half(half, row_of, landed, send_sem, recv_sem):
    def send(there):
        pltpu.make_async_remote_copy(
            src_ref=row_of(there),
            dst_ref=landed,
            send_sem=send_sem,
            recv_sem=recv_sem,
            device_id=target_of(*there),
            device_id_type=MESH,
        ).start()

    for_others(half, send)


def await_bytes(like, sem):
    pltpu.make_async_copy(like, like, sem).wait()


def label_copies(stage, all_labels, send_sems, recv_sems):
    z, y, x, core = here()
    part = (
        all_labels.at[core, x, y, z],
        all_labels.at[core, x, y],
        all_labels.at[core, x],
        all_labels.at[core],
    )[stage]
    first = (0, 7, 10, 13)[stage]
    peers = lines()[stage]
    return [
        pltpu.make_async_remote_copy(
            src_ref=part,
            dst_ref=part,
            send_sem=send_sems.at[first + k],
            recv_sem=recv_sems.at[first + k],
            device_id=target_of(*peer),
            device_id_type=MESH,
        )
        for k, peer in enumerate(peers)
    ]


def step_kernel(
    row_ids,
    slots,
    stencil_z,
    fractions,
    atom_count,
    features,
    w_in,
    w_out,
    basis,
    basis_t,
    tabs,
    forces,
    grads,
    ids_cols,
    bins_cols,
    own_labels,
    all_labels,
    charges,
    corner,
    tab_x,
    tab_y,
    tab_z,
    z_high,
    z_low,
    mesh_rows,
    sent,
    arrived,
    rows_high,
    rows_low,
    labels_t,
    labels_x,
    onehot_y,
    crossed,
    plane,
    fields,
    cells,
    replies_t,
    replies,
    returned,
    spare,
    spare_two,
    lifts,
    kernel,
    field_high,
    field_low,
    weights,
    label_send,
    label_recv,
    line_sems,
    sem_own,
    send_one,
    recv_one,
    send_two,
    recv_two,
):
    barrier = pltpu.get_barrier_semaphore()
    for peers in lines():
        for peer in peers:
            pl.semaphore_signal(barrier, inc=1, device_id=target_of(*peer), device_id_type=MESH)
    z, y, x, core = here()
    low = place_of(z, y, x, 0)
    bin_labels(row_ids, ids_cols, bins_cols)
    for c in range(ROWS // 128):
        part = jnp.transpose(bins_cols[c * 128 : (c + 1) * 128, :])
        own_labels[0:1, c * 128 : (c + 1) * 128] = part[0:1, :]
    pl.semaphore_wait(barrier, 14)
    mine = pltpu.make_async_copy(own_labels.at[0], all_labels.at[core, x, y, z], sem_own)
    mine.start()
    mine.wait()

    def labels_on(stage):
        if stage > 0:
            for copy in label_copies(stage - 1, all_labels, label_send, label_recv):
                copy.wait()
        if stage < 4:
            for copy in label_copies(stage, all_labels, label_send, label_recv):
                copy.start()

    def heard_from(stage):
        if stage > 0:
            pl.semaphore_wait(line_sems.at[stage - 1], (3, 3, 1)[stage - 1])
        if stage < 3:
            for peer in lines()[stage + 1]:
                pl.semaphore_signal(
                    line_sems.at[stage], inc=1, device_id=target_of(*peer), device_id_type=MESH
                )

    heard_from(0)
    labels_on(0)
    corners(slots, ids_cols, corner)
    class_weights(corner, fractions, tab_x, tab_y, True)
    class_weights_z(stencil_z, fractions, tab_z, True)
    for c in range(ATOMS // CHUNK):
        lanes = slice(c * CHUNK, (c + 1) * CHUNK)
        pre, sigma, out_w = hidden(features, w_in, w_out, lanes)
        charge = jnp.sum(pre * sigma * out_w, axis=0, keepdims=True)
        atom = lax.broadcasted_iota(jnp.int32, (1, CHUNK), 1) + c * CHUNK
        charges[0:1, lanes] = jnp.where(atom < atom_count[0], charge, 0.0)
        lifts[:, lanes] = (sigma * (1.0 + pre * (1.0 - sigma)) * out_w).astype(BF16)
    heard_from(1)
    labels_on(1)
    for c in range(ATOMS // CHUNK):
        lanes = slice(c * CHUNK, (c + 1) * CHUNK)
        row_weights(tab_x, tab_y, bins_cols, lanes, [weights.at[k, c] for k in range(2)], 0, 1)
        key = tab_z[8:16, lanes]
        amount = tab_z[0:8, lanes] * charges[0:1, lanes]
        amount_high = amount.astype(BF16).astype(F32)
        amount_low = amount - amount_high
        for h in range(0, 32, 2):
            rows = slice(h * 8, h * 8 + 16)
            hits = (key == float(h), key == float(h + 1))
            z_high[rows, :] = jnp.concatenate(
                [jnp.where(hit, amount_high, 0.0) for hit in hits], axis=0
            ).astype(BF16)
            z_low[rows, :] = jnp.concatenate(
                [jnp.where(hit, amount_low, 0.0) for hit in hits], axis=0
            ).astype(BF16)
        total = dot3((z_high[...], z_low[...]), (weights[0, c], weights[1, c]), NT)
        if c == 0:
            mesh_rows[...] = total
        else:
            mesh_rows[...] += total
        if c == 1:
            heard_from(2)
            labels_on(2)
    sent[...] = dot3((basis[0], basis[1]), split(mesh_rows[...]))
    heard_from(3)
    own = sent.at[core * 128 + low]
    pltpu.make_async_copy(own, arrived.at[0, low], recv_one.at[0]).start()
    pltpu.make_async_copy(own, spare, send_one).start()
    for half in range(2):
        send_half(
            half,
            lambda there: sent.at[place_of(*there)],
            arrived.at[half, low],
            send_one,
            recv_one.at[half],
        )
        if half == 0:
            labels_on(3)
    for c in range(ATOMS // CHUNK):
        lanes = slice(c * CHUNK, (c + 1) * CHUNK)
        row_weights(tab_x, tab_y, bins_cols, lanes, [weights.at[k, c] for k in range(2, 6)], 1, 3)
    coulomb(kernel, core * 128 + low)
    labels_on(4)
    cell_y = lax.broadcasted_iota(jnp.int32, (32, 128), 0).astype(F32)
    for half in range(2):
        for c in range(ROWS // 128):
            bins = slice(c * 128, (c + 1) * 128)
            part = all_labels[lax.rem(core + half, 2), :, :, :, bins].reshape(128, 128)
            part = jnp.transpose(part)
            labels_t[half, bins, :] = part.astype(jnp.int32)
            labels_x[half, bins, :] = jnp.floor(part * (1.0 / 32.0))

        @pl.loop(0, 32 // UNROLL_Y)
        def _(step):
            for k, rank in [(k, rank) for k in range(UNROLL_Y) for rank in range(2)]:
                xb = step * UNROLL_Y + k
                at = pl.ds(pl.multiple_of(rank * 256 + xb * 8, 8), 8)
                label_y = (labels_t[half, at, :] & 31).astype(F32)
                for yb in range(8):
                    hit = jnp.broadcast_to(label_y[yb : yb + 1], (32, 128)) == cell_y
                    onehot_y[half, xb, yb * 32 : yb * 32 + 32, rank * 128 : rank * 128 + 128] = jnp.where(
                        hit, 1.0, 0.0
                    ).astype(BF16)

    for half in range(2):
        await_bytes(arrived.at[half], recv_one.at[half])
        for c in range(ROWS // 128):
            bins = slice(c * 128, (c + 1) * 128)
            part = jnp.transpose(arrived[half, :, bins])
            part_high = part.astype(BF16).astype(F32)
            rows_high[half, bins, :] = part_high
            rows_low[half, bins, :] = part - part_high
        gather_plane(half, rows_high, rows_low, labels_x, onehot_y, crossed)
    keep_matching(crossed, plane)
    solve_plane(tabs, kernel, plane, fields)
    spread_cells(fields, cells)
    own = replies.at[0, low]
    for half in range(2):
        answer(half, cells, labels_t, replies_t)
        for c in range(ROWS // 128):
            bins = slice(c * 128, (c + 1) * 128)
            replies[half, :, bins] = jnp.transpose(replies_t[half, bins, :])
        if half == 0:
            pltpu.make_async_copy(own, returned.at[core * 128 + low], recv_two).start()
            pltpu.make_async_copy(own, spare_two, send_two).start()
        send_half(
            half,
            lambda there: replies.at[half, place_of(there[0], there[1], there[2], 0)],
            returned.at[core * 128 + low],
            send_two,
            recv_two,
        )
    await_bytes(sent, send_one)
    await_bytes(returned, recv_two)

    field_high[...], field_low[...] = split(
        dot3((basis_t[0], basis_t[1]), split(returned[...]))
    )
    for c in range(ATOMS // CHUNK):
        lanes = slice(c * CHUNK, (c + 1) * CHUNK)
        key = tab_z[8:16, lanes]
        sums = []
        for k in range(3):
            total = dot3(
                (field_high[...], field_low[...]), (weights[2 * k, c], weights[2 * k + 1, c])
            )
            chosen = jnp.zeros((8, CHUNK), F32)
            for h in range(32):
                chosen = jnp.where(key == float(h), total[h * 8 : (h + 1) * 8], chosen)
            sums.append(chosen)
        wz = tab_z[0:8, lanes]
        potential = jnp.sum(wz * sums[0], axis=0, keepdims=True)
        charge = -charges[0:1, lanes]
        forces[0:1, lanes] = charge * jnp.sum(wz * sums[1], axis=0, keepdims=True)
        forces[1:2, lanes] = charge * jnp.sum(wz * sums[2], axis=0, keepdims=True)
        forces[2:3, lanes] = charge * jnp.sum(tab_z[16:24, lanes] * sums[0], axis=0, keepdims=True)
        atom = lax.broadcasted_iota(jnp.int32, (1, CHUNK), 1) + c * CHUNK
        potential = jnp.where(atom < atom_count[0], potential, 0.0)
        grad = potential * dot(w_in[...], lifts[:, lanes])
        for b in range(CHUNK // 128):
            rows = slice(c * CHUNK + b * 128, c * CHUNK + (b + 1) * 128)
            grads[rows, :] = jnp.transpose(grad[:, b * 128 : (b + 1) * 128]).astype(BF16)
    await_bytes(returned, send_two)


def coulomb(kernel, wave_index):
    half = GRID // 2

    def wave(index):
        return jnp.where(index <= half, index, index - half)

    wave_x = wave(lax.broadcasted_iota(jnp.int32, (GRID, GRID), 0))
    wave_y = wave(lax.broadcasted_iota(jnp.int32, (GRID, GRID), 1))
    wave_z = wave(wave_index)
    squared = (wave_x * wave_x + wave_y * wave_y + wave_z * wave_z).astype(F32)
    damped = jnp.exp(-((SMOOTH * math.pi / GRID) ** 2) * squared)
    values = COUPLE * damped * (GRID * GRID) / (4.0 * math.pi * math.pi * jnp.maximum(squared, 1.0))
    keep = (squared > 0) & (wave_x != half) & (wave_y != half) & (wave_z != half)
    kernel[...] = jnp.where(keep, values, 0.0)


def gather_plane(half, rows_high, rows_low, labels_x, onehot_y, crossed):
    def one(xb):
        left = []
        for rank in range(2):
            at = pl.ds(pl.multiple_of(rank * 256 + xb * 8, 8), 8)
            high, low = rows_high[half, at, :], rows_low[half, at, :]
            label_x = labels_x[half, at, :]
            hits = [label_x == float(h) for h in range(8)]
            parts = [jnp.where(hit, part, 0.0) for part in (high, low) for hit in hits]
            left.append(jnp.concatenate(parts, axis=0).astype(BF16))
        both = dot(jnp.concatenate(left, axis=1), onehot_y[half, xb], NT)
        return both[0:64] + both[64:128]

    @pl.loop(0, 32 // UNROLL)
    def _(step):
        totals = [one(step * UNROLL + k) for k in range(UNROLL)]
        for k, total in enumerate(totals):
            if half == 0:
                crossed[step * UNROLL + k] = total
            else:
                crossed[step * UNROLL + k] += total


def keep_matching(crossed, plane):
    lane_class = lax.broadcasted_iota(jnp.int32, (8, GRID), 1) // 32
    match = lane_class == lax.broadcasted_iota(jnp.int32, (8, GRID), 0)
    row = lax.broadcasted_iota(jnp.int32, (8, GRID), 0)

    @pl.loop(0, 8)
    def _(step):
        for k in range(4):
            xb = step * 4 + k
            total = jnp.zeros((8, GRID), F32)
            for h in range(8):
                part = jnp.where(match, crossed[xb, h * 8 : h * 8 + 8, :], 0.0)
                total = jnp.where(row == h, jnp.sum(part, axis=0, keepdims=True), total)
            plane[pl.ds(pl.multiple_of(xb * 8, 8), 8), :] = total


def solve_plane(tabs, kernel, plane, fields):
    along_x, back_x, along_y = [(tabs[2 * k], tabs[2 * k + 1]) for k in range(3)]
    spectrum = dot3(along_x, split(plane[...]))
    spectrum = dot3(split(spectrum), along_y, NT) * kernel[...]
    field = dot3(back_x, split(spectrum))
    field = dot3(split(field), along_y)
    fields[0] = field[:, :128]
    fields[1] = field[:, 128:]


def spread_cells(fields, cells):
    block = lax.broadcasted_iota(jnp.int32, (32, 128), 1) // 32
    for yb in range(8):
        for h in range(2):
            chosen = None
            for q in range(4):
                part = fields[yb // 4, pl.ds(4 * h + q, 32, stride=8), :]
                shift = (q - yb % 4) % 4 * 32
                part = pltpu.roll(part, shift, 1) if shift else part
                chosen = part if q == 0 else jnp.where(block == q, part, chosen)
            cells[yb, h] = chosen


def answer(half, cells, labels_t, replies_t):
    for yb in range(8):
        for rank in range(2):
            at = pl.ds(rank * 256 + yb, 32, stride=8)
            label = labels_t[half, at, :]
            index = label & 127
            upper = label >> 7
            value = jnp.zeros((32, 128), F32)
            for h in range(2):
                taken = jnp.take_along_axis(cells[yb, h], index, axis=1, mode="promise_in_bounds")
                value = jnp.where(upper == h, taken, value)
            replies_t[half, at, :] = value


VM = pl.BlockSpec(memory_space=pltpu.VMEM)
SM = pl.BlockSpec(memory_space=pltpu.SMEM)


def local(features, fractions, row_ids, stencil_slots, stencil_z, atom_count, w_in, w_out):
    basis, basis_t, plane = [jnp.asarray(table) for table in tables()]
    vmem = pltpu.VMEM
    chunks = ATOMS // CHUNK
    return pl.pallas_call(
        step_kernel,
        out_shape=(
            jax.ShapeDtypeStruct((3, ATOMS), F32),
            jax.ShapeDtypeStruct((ATOMS, 128), BF16),
        ),
        in_specs=[VM] * 4 + [SM] + [VM] * 6,
        out_specs=(VM, VM),
        scratch_shapes=[
            vmem((ROWS, 128), F32),
            vmem((ROWS, 128), F32),
            vmem((8, ROWS), F32),
            vmem((2, 4, 4, 8, ROWS), F32),
            vmem((1, ATOMS), F32),
            vmem((1, ATOMS), jnp.int32),
            vmem((3, 32, ATOMS), F32),
            vmem((24, ATOMS), F32),
            vmem((24, ATOMS), F32),
            vmem((GRID, CHUNK), BF16),
            vmem((GRID, CHUNK), BF16),
            vmem((GRID, ROWS), F32),
            vmem((DEVICES, ROWS), F32),
            vmem((2, 128, ROWS), F32),
            vmem((2, ROWS, 128), F32),
            vmem((2, ROWS, 128), F32),
            vmem((2, ROWS, 128), jnp.int32),
            vmem((2, ROWS, 128), F32),
            vmem((2, 32, GRID, 256), BF16),
            vmem((32, 64, GRID), F32),
            vmem((GRID, GRID), F32),
            vmem((2, GRID, 128), F32),
            vmem((8, 2, 32, 128), F32),
            vmem((2, ROWS, 128), F32),
            vmem((2, 128, ROWS), F32),
            vmem((DEVICES, ROWS), F32),
            vmem((ROWS,), F32),
            vmem((ROWS,), F32),
            vmem((128, ATOMS), BF16),
            vmem((GRID, GRID), F32),
            vmem((GRID, ROWS), BF16),
            vmem((GRID, ROWS), BF16),
            vmem((6, chunks, ROWS, CHUNK), BF16),
            pltpu.SemaphoreType.DMA((14,)),
            pltpu.SemaphoreType.DMA((14,)),
            pltpu.SemaphoreType.REGULAR((3,)),
        ]
        + [
            pltpu.SemaphoreType.DMA,
            pltpu.SemaphoreType.DMA,
            pltpu.SemaphoreType.DMA((2,)),
            pltpu.SemaphoreType.DMA,
            pltpu.SemaphoreType.DMA,
        ],
        compiler_params=pltpu.CompilerParams(
            vmem_limit_bytes=VMEM_LIMIT, collective_id=0, has_side_effects=True
        ),
        name="step",
    )(
        row_ids,
        stencil_slots,
        stencil_z.reshape(1, ATOMS),
        fractions,
        atom_count,
        features,
        w_in,
        w_out.reshape(1, 128),
        basis,
        basis_t,
        plane,
    )


def solution(mesh):
    placed = (
        P(("pen", "slab"), None),
        P(None, ("pen", "slab")),
        P(("pen", "slab"), None),
        P(None, ("pen", "slab")),
        P(("pen", "slab")),
        P(("pen", "slab")),
        P(),
        P(),
    )
    return jax.shard_map(
        local,
        mesh=mesh,
        in_specs=placed,
        out_specs=(P(None, ("pen", "slab")), P(("pen", "slab"), None)),
        check_vma=False,
    )
```

```python
import functools
import math

import jax
import jax.numpy as jnp
import ml_dtypes
import numpy as np
from jax import lax
from jax.experimental import pallas as pl
from jax.experimental.pallas import tpu as pltpu
from jax.sharding import PartitionSpec as P

GRID = 256
COUPLE = 8.0
SMOOTH = 1.0
ROWS = 512
ATOMS = 2048
DEVICES = 256
CHUNK = 512
UNROLL = 8
UNROLL_W = 2
UNROLL_Y = 4
VMEM_LIMIT = 56 * 1024 * 1024
F32 = jnp.float32
BF16 = jnp.bfloat16

NN = (((1,), (0,)), ((), ()))
NT = (((1,), (1,)), ((), ()))


def dot(left, right, dims=NN):
    return lax.dot_general(left, right, dims, preferred_element_type=F32)


def split(value):
    high = value.astype(BF16)
    low = (value - high.astype(F32)).astype(BF16)
    return (high, low)


def dot3(left, right, dims=NN):
    return (
        dot(left[0], right[0], dims)
        + dot(left[0], right[1], dims)
        + dot(left[1], right[0], dims)
    )


def fourier_basis():
    cell = np.arange(GRID)
    wave = np.arange(GRID)
    wave = np.where(wave <= GRID // 2, wave, wave - GRID // 2)
    angle = 2.0 * np.pi * ((wave[:, None] * cell[None, :]) % GRID) / GRID
    basis = np.where(np.arange(GRID)[:, None] <= GRID // 2, np.cos(angle), np.sin(angle))
    scale = np.where((np.arange(GRID) == 0) | (np.arange(GRID) == GRID // 2), 1.0, 2.0)
    return basis * np.sqrt(scale / GRID)[:, None]


def split_table(table):
    table = table.astype(np.float32)
    high = table.astype(ml_dtypes.bfloat16)
    low = (table - high.astype(np.float32)).astype(ml_dtypes.bfloat16)
    return [high, low]


def tables():
    basis = fourier_basis()
    place = np.arange(GRID)
    along_x = basis[:, (place % 8) * 32 + place // 8]
    along_y = basis[:, (place % 32) * 8 + place // 32]
    plane = np.stack(split_table(along_x) + split_table(along_x.T) + split_table(along_y))
    return (np.stack(split_table(basis)), np.stack(split_table(basis.T)), plane)


def spline_values(u):
    rest = 1.0 - u
    square = u * u
    cube = square * u
    return (
        rest * rest * rest / 6.0,
        (3.0 * cube - 6.0 * square + 4.0) / 6.0,
        (-3.0 * cube + 3.0 * square + 3.0 * u + 1.0) / 6.0,
        cube / 6.0,
    )


def spline_slopes(u):
    rest = 1.0 - u
    square = u * u
    return (
        -rest * rest / 2.0,
        (3.0 * square - 4.0 * u) / 2.0,
        (-3.0 * square + 2.0 * u + 1.0) / 2.0,
        square / 2.0,
    )


def pick(step, values):
    out = jnp.where(step == 3, values[3], 0.0)
    for k in (2, 1, 0):
        out = jnp.where(step == k, values[k], out)
    return out


def row_to_columns(row):
    return jnp.transpose(jnp.broadcast_to(row, (128, 128)))


def bin_labels(row_ids, ids_cols, bins_cols):
    ids = row_ids[...]
    used = ids >= 0
    x = ids >> 8
    y = ids & 255
    group = jnp.where(used, (x & 31) * 8 + (y & 7), -1)
    label = ((x >> 5) * 32 + (y >> 3)).astype(F32)
    place = lax.broadcasted_iota(jnp.int32, (128, ROWS), 1)
    row = lax.broadcasted_iota(jnp.int32, (128, ROWS), 0)
    rank = jnp.zeros((1, ROWS), F32)
    for c in range(ROWS // 128):
        lanes = slice(c * 128, (c + 1) * 128)
        column = row_to_columns(ids[:, lanes])
        ids_cols[lanes, :] = column.astype(F32)
        column = (column >> 8 & 31) * 8 + (column & 7)
        column = jnp.concatenate([column] * (ROWS // 128), axis=1)
        same = (column == group) & (row + c * 128 < place)
        rank += jnp.sum(jnp.where(same, 1.0, 0.0), axis=0, keepdims=True)
    target = jnp.where(used, rank.astype(jnp.int32) * 256 + group, -1)
    for c in range(ROWS // 128):
        hit = target == row + c * 128
        value = jnp.sum(jnp.where(hit, label + 1.0, 0.0), axis=1, keepdims=True) - 1.0
        bins_cols[c * 128 : (c + 1) * 128, :] = jnp.broadcast_to(value, (128, 128))


def corners(slots, ids_cols, corner):
    row = lax.broadcasted_iota(jnp.int32, (ROWS, 128), 0)
    for c in range(ATOMS // 128):
        lanes = slice(c * 128, (c + 1) * 128)
        hit = slots[0:1, lanes] == row
        value = jnp.sum(jnp.where(hit, ids_cols[...], 0.0), axis=0, keepdims=True)
        corner[0:1, lanes] = value.astype(jnp.int32)


def class_weights(corner, fractions, tab_x, tab_y, slopes):
    x0 = corner[0:1, :] >> 8
    y0 = corner[0:1, :] & 255
    value_x = spline_values(fractions[0:1, :])
    value_y = spline_values(fractions[1:2, :])
    step_y = (lax.broadcasted_iota(jnp.int32, (8, ATOMS), 0) - y0) & 7
    tab_y[0:8, :] = pick(step_y, value_y)
    tab_y[8:16, :] = ((((y0 + step_y) >> 3) & 31)).astype(F32)
    if slopes:
        slope_x = spline_slopes(fractions[0:1, :])
        slope_y = spline_slopes(fractions[1:2, :])
        tab_y[16:24, :] = pick(step_y, slope_y)
    for b in range(4):
        rows = slice(b * 8, (b + 1) * 8)
        step_x = (lax.broadcasted_iota(jnp.int32, (8, ATOMS), 0) + b * 8 - x0) & 31
        tab_x[0, rows, :] = pick(step_x, value_x)
        tab_x[1, rows, :] = ((((x0 + step_x) >> 5) & 7) * 32).astype(F32)
        if slopes:
            tab_x[2, rows, :] = pick(step_x, slope_x)


def class_weights_z(stencil_z, fractions, tab_z, slopes):
    z0 = stencil_z[0:1, :]
    step_z = (lax.broadcasted_iota(jnp.int32, (8, ATOMS), 0) - z0) & 7
    tab_z[0:8, :] = pick(step_z, spline_values(fractions[2:3, :]))
    tab_z[8:16, :] = ((((z0 + step_z) >> 3) & 31)).astype(F32)
    if slopes:
        tab_z[16:24, :] = pick(step_z, spline_slopes(fractions[2:3, :]))


def row_weights(tab_x, tab_y, bins_cols, lanes, outs, last, step):
    def twice(part):
        return jnp.concatenate([part, part], axis=0)

    wy = twice(tab_y[0:8, lanes])
    ky = twice(tab_y[8:16, lanes])
    sy = twice(tab_y[16:24, lanes])
    width = wy.shape[1]

    def pair(index, i):
        rows = [tab_x[index, pl.ds(2 * i + k, 1), lanes] for k in range(2)]
        return jnp.concatenate([jnp.broadcast_to(row, (8, width)) for row in rows], axis=0)

    def one(i):
        wx = pair(0, i)
        key = pair(1, i) + ky
        values = [wx * wy, pair(2, i) * wy, wx * sy][:last]
        for rank in range(2):
            rows = pl.ds(pl.multiple_of(rank * 256 + i * 16, 16), 16)
            label = bins_cols[rows, :]
            label = jnp.concatenate([label] * (width // 128), axis=1)
            hit = key == label
            for k, value in enumerate(values):
                high, low = split(jnp.where(hit, value, 0.0))
                outs[step * k][rows, :] = high
                if step == 2:
                    outs[step * k + 1][rows, :] = low

    @pl.loop(0, 16 // UNROLL_W)
    def _(block):
        for k in range(UNROLL_W):
            one(block * UNROLL_W + k)


MESH = pl.DeviceIdType.MESH
DZ = (4, 1, 7, 2, 6, 3, 5, 0)


def here():
    pen = lax.axis_index("pen")
    slab = lax.axis_index("slab")
    return (pen // 4, lax.rem(pen, 4), slab // 2, lax.rem(slab, 2))


def place_of(z, y, x, core):
    return ((core * 4 + x) * 4 + y) * 8 + z


def target_of(z, y, x, core):
    return (z * 4 + y, x * 2 + core)


def for_others(half, visit):
    z, y, x, core = here()
    other_core = lax.rem(core + half, 2)

    @pl.loop(0, 16)
    def _(k):
        other_y = lax.rem(y + lax.rem(k, 4), 4)
        other_x = lax.rem(x + k // 4, 4)
        for dz in DZ:
            there = (lax.rem(z + dz, 8), other_y, other_x, other_core)
            if dz == 0 and half == 0:
                pl.when(k > 0)(functools.partial(visit, there))
            else:
                visit(there)


def lines():
    z, y, x, core = here()
    return (
        [(lax.rem(z + k, 8), y, x, core) for k in range(1, 8)],
        [(z, lax.rem(y + k, 4), x, core) for k in range(1, 4)],
        [(z, y, lax.rem(x + k, 4), core) for k in range(1, 4)],
        [(z, y, x, 1 - core)],
    )


def send_half(half, row_of, landed, send_sem, recv_sem):
    def send(there):
        pltpu.make_async_remote_copy(
            src_ref=row_of(there),
            dst_ref=landed,
            send_sem=send_sem,
            recv_sem=recv_sem,
            device_id=target_of(*there),
            device_id_type=MESH,
        ).start()

    for_others(half, send)


def await_bytes(like, sem):
    pltpu.make_async_copy(like, like, sem).wait()


def label_copies(stage, all_labels, send_sems, recv_sems):
    z, y, x, core = here()
    part = (
        all_labels.at[core, x, y, z],
        all_labels.at[core, x, y],
        all_labels.at[core, x],
        all_labels.at[core],
    )[stage]
    first = (0, 7, 10, 13)[stage]
    peers = lines()[stage]
    return [
        pltpu.make_async_remote_copy(
            src_ref=part,
            dst_ref=part,
            send_sem=send_sems.at[first + k],
            recv_sem=recv_sems.at[first + k],
            device_id=target_of(*peer),
            device_id_type=MESH,
        )
        for k, peer in enumerate(peers)
    ]


def step_kernel(
    row_ids,
    slots,
    stencil_z,
    fractions,
    atom_count,
    features,
    w_in,
    w_out,
    basis,
    basis_t,
    tabs,
    sums,
    lifts,
    ids_cols,
    bins_cols,
    own_labels,
    all_labels,
    charges,
    corner,
    tab_x,
    tab_y,
    tab_z,
    z_high,
    z_low,
    mesh_rows,
    sent,
    arrived,
    rows_high,
    rows_low,
    labels_t,
    labels_x,
    onehot_y,
    crossed,
    plane,
    fields,
    cells,
    replies_t,
    replies,
    returned,
    spare,
    spare_two,
    kernel,
    field_high,
    field_low,
    weights,
    label_send,
    label_recv,
    line_sems,
    sem_own,
    send_one,
    recv_one,
    send_two,
    recv_two,
):
    barrier = pltpu.get_barrier_semaphore()
    for peers in lines():
        for peer in peers:
            pl.semaphore_signal(barrier, inc=1, device_id=target_of(*peer), device_id_type=MESH)
    z, y, x, core = here()
    low = place_of(z, y, x, 0)
    bin_labels(row_ids, ids_cols, bins_cols)
    for c in range(ROWS // 128):
        part = jnp.transpose(bins_cols[c * 128 : (c + 1) * 128, :])
        own_labels[0:1, c * 128 : (c + 1) * 128] = part[0:1, :]
    pl.semaphore_wait(barrier, 14)
    mine = pltpu.make_async_copy(own_labels.at[0], all_labels.at[core, x, y, z], sem_own)
    mine.start()
    mine.wait()

    def labels_on(stage):
        if stage > 0:
            for copy in label_copies(stage - 1, all_labels, label_send, label_recv):
                copy.wait()
        if stage < 4:
            for copy in label_copies(stage, all_labels, label_send, label_recv):
                copy.start()

    def heard_from(stage):
        if stage > 0:
            pl.semaphore_wait(line_sems.at[stage - 1], (3, 3, 1)[stage - 1])
        if stage < 3:
            for peer in lines()[stage + 1]:
                pl.semaphore_signal(
                    line_sems.at[stage], inc=1, device_id=target_of(*peer), device_id_type=MESH
                )

    heard_from(0)
    labels_on(0)
    corners(slots, ids_cols, corner)
    class_weights(corner, fractions, tab_x, tab_y, True)
    class_weights_z(stencil_z, fractions, tab_z, True)
    w_in_t = jnp.transpose(w_in[...].astype(F32)).astype(BF16)
    out_w = jnp.concatenate([row_to_columns(w_out[...])] * (CHUNK // 128), axis=1)
    for c in range(ATOMS // CHUNK):
        lanes = slice(c * CHUNK, (c + 1) * CHUNK)
        pre = dot(w_in_t, features[lanes, :], NT)
        sigma = jax.nn.sigmoid(pre)
        charge = jnp.sum(pre * sigma * out_w, axis=0, keepdims=True)
        atom = lax.broadcasted_iota(jnp.int32, (1, CHUNK), 1) + c * CHUNK
        charges[0:1, lanes] = jnp.where(atom < atom_count[0], charge, 0.0)
        lifts[:, lanes] = (sigma * (1.0 + pre * (1.0 - sigma)) * out_w).astype(BF16)
    heard_from(1)
    labels_on(1)
    for c in range(ATOMS // CHUNK):
        lanes = slice(c * CHUNK, (c + 1) * CHUNK)
        row_weights(tab_x, tab_y, bins_cols, lanes, [weights.at[0, c]], 1, 1)
        key = tab_z[8:16, lanes]
        amount = tab_z[0:8, lanes] * charges[0:1, lanes]
        amount_high = amount.astype(BF16).astype(F32)
        amount_low = amount - amount_high
        for h in range(0, 32, 2):
            rows = slice(h * 8, h * 8 + 16)
            hits = (key == float(h), key == float(h + 1))
            z_high[rows, :] = jnp.concatenate(
                [jnp.where(hit, amount_high, 0.0) for hit in hits], axis=0
            ).astype(BF16)
            z_low[rows, :] = jnp.concatenate(
                [jnp.where(hit, amount_low, 0.0) for hit in hits], axis=0
            ).astype(BF16)
        total = dot(z_high[...], weights[0, c], NT) + dot(z_low[...], weights[0, c], NT)
        if c == 0:
            mesh_rows[...] = total
        else:
            mesh_rows[...] += total
        if c == 1:
            heard_from(2)
            labels_on(2)
    sent[...] = dot3((basis[0], basis[1]), split(mesh_rows[...]))
    heard_from(3)
    own = sent.at[core * 128 + low]
    pltpu.make_async_copy(own, arrived.at[0, low], recv_one.at[0]).start()
    pltpu.make_async_copy(own, spare, send_one).start()
    for half in range(2):
        send_half(
            half,
            lambda there: sent.at[place_of(*there)],
            arrived.at[half, low],
            send_one,
            recv_one.at[half],
        )
        if half == 0:
            labels_on(3)
    for c in range(ATOMS // CHUNK):
        lanes = slice(c * CHUNK, (c + 1) * CHUNK)
        row_weights(tab_x, tab_y, bins_cols, lanes, [weights.at[k, c] for k in range(6)], 3, 2)
    coulomb(kernel, core * 128 + low)
    labels_on(4)
    cell_y = lax.broadcasted_iota(jnp.int32, (32, 128), 0).astype(F32)
    for half in range(2):
        for c in range(ROWS // 128):
            bins = slice(c * 128, (c + 1) * 128)
            part = all_labels[lax.rem(core + half, 2), :, :, :, bins].reshape(128, 128)
            part = jnp.transpose(part)
            labels_t[half, bins, :] = part.astype(jnp.int32)
            labels_x[half, bins, :] = jnp.floor(part * (1.0 / 32.0))

        @pl.loop(0, 32 // UNROLL_Y)
        def _(step):
            for k, rank in [(k, rank) for k in range(UNROLL_Y) for rank in range(2)]:
                xb = step * UNROLL_Y + k
                at = pl.ds(pl.multiple_of(rank * 256 + xb * 8, 8), 8)
                label_y = (labels_t[half, at, :] & 31).astype(F32)
                for yb in range(8):
                    hit = jnp.broadcast_to(label_y[yb : yb + 1], (32, 128)) == cell_y
                    onehot_y[half, xb, yb * 32 : yb * 32 + 32, rank * 128 : rank * 128 + 128] = jnp.where(
                        hit, 1.0, 0.0
                    ).astype(BF16)

    for half in range(2):
        await_bytes(arrived.at[half], recv_one.at[half])
        for c in range(ROWS // 128):
            bins = slice(c * 128, (c + 1) * 128)
            part = jnp.transpose(arrived[half, :, bins])
            part_high = part.astype(BF16).astype(F32)
            rows_high[half, bins, :] = part_high
            rows_low[half, bins, :] = part - part_high
        gather_plane(half, rows_high, rows_low, labels_x, onehot_y, crossed)
    keep_matching(crossed, plane)
    solve_plane(tabs, kernel, plane, fields)
    spread_cells(fields, cells)
    own = replies.at[0, low]
    for half in range(2):
        answer(half, cells, labels_t, replies_t)
        for c in range(ROWS // 128):
            bins = slice(c * 128, (c + 1) * 128)
            replies[half, :, bins] = jnp.transpose(replies_t[half, bins, :])
        if half == 0:
            pltpu.make_async_copy(own, returned.at[core * 128 + low], recv_two).start()
            pltpu.make_async_copy(own, spare_two, send_two).start()
        send_half(
            half,
            lambda there: replies.at[half, place_of(there[0], there[1], there[2], 0)],
            returned.at[core * 128 + low],
            send_two,
            recv_two,
        )
    await_bytes(sent, send_one)
    await_bytes(returned, recv_two)

    field_high[...], field_low[...] = split(
        dot3((basis_t[0], basis_t[1]), split(returned[...]))
    )
    for c in range(ATOMS // CHUNK):
        lanes = slice(c * CHUNK, (c + 1) * CHUNK)
        key = tab_z[8:16, lanes]
        picked = []
        for k in range(3):
            total = dot3(
                (field_high[...], field_low[...]), (weights[2 * k, c], weights[2 * k + 1, c])
            )
            chosen = jnp.zeros((8, CHUNK), F32)
            for h in range(32):
                chosen = jnp.where(key == float(h), total[h * 8 : (h + 1) * 8], chosen)
            picked.append(chosen)
        wz = tab_z[0:8, lanes]
        potential = jnp.sum(wz * picked[0], axis=0, keepdims=True)
        charge = -charges[0:1, lanes]
        sums[0:1, lanes] = charge * jnp.sum(wz * picked[1], axis=0, keepdims=True)
        sums[1:2, lanes] = charge * jnp.sum(wz * picked[2], axis=0, keepdims=True)
        sums[2:3, lanes] = charge * jnp.sum(tab_z[16:24, lanes] * picked[0], axis=0, keepdims=True)
        atom = lax.broadcasted_iota(jnp.int32, (1, CHUNK), 1) + c * CHUNK
        sums[3:4, lanes] = jnp.where(atom < atom_count[0], potential, 0.0)
    await_bytes(returned, send_two)


def finish_kernel(sums, lifts, w_in, forces, grads):
    forces[...] = sums[0:3, :]
    for c in range(ATOMS // CHUNK):
        lanes = slice(c * CHUNK, (c + 1) * CHUNK)
        grad = sums[3:4, lanes] * dot(w_in[...], lifts[:, lanes])
        for b in range(CHUNK // 128):
            rows = slice(c * CHUNK + b * 128, c * CHUNK + (b + 1) * 128)
            grads[rows, :] = jnp.transpose(grad[:, b * 128 : (b + 1) * 128]).astype(BF16)


def coulomb(kernel, wave_index):
    half = GRID // 2

    def wave(index):
        return jnp.where(index <= half, index, index - half)

    wave_x = wave(lax.broadcasted_iota(jnp.int32, (GRID, GRID), 0))
    wave_y = wave(lax.broadcasted_iota(jnp.int32, (GRID, GRID), 1))
    wave_z = wave(wave_index)
    squared = (wave_x * wave_x + wave_y * wave_y + wave_z * wave_z).astype(F32)
    damped = jnp.exp(-((SMOOTH * math.pi / GRID) ** 2) * squared)
    values = COUPLE * damped * (GRID * GRID) / (4.0 * math.pi * math.pi * jnp.maximum(squared, 1.0))
    keep = (squared > 0) & (wave_x != half) & (wave_y != half) & (wave_z != half)
    kernel[...] = jnp.where(keep, values, 0.0)


def gather_plane(half, rows_high, rows_low, labels_x, onehot_y, crossed):
    def one(xb):
        left = []
        for rank in range(2):
            at = pl.ds(pl.multiple_of(rank * 256 + xb * 8, 8), 8)
            high, low = rows_high[half, at, :], rows_low[half, at, :]
            label_x = labels_x[half, at, :]
            hits = [label_x == float(h) for h in range(8)]
            parts = [jnp.where(hit, part, 0.0) for part in (high, low) for hit in hits]
            left.append(jnp.concatenate(parts, axis=0).astype(BF16))
        both = dot(jnp.concatenate(left, axis=1), onehot_y[half, xb], NT)
        return both[0:64] + both[64:128]

    @pl.loop(0, 32 // UNROLL)
    def _(step):
        totals = [one(step * UNROLL + k) for k in range(UNROLL)]
        for k, total in enumerate(totals):
            if half == 0:
                crossed[step * UNROLL + k] = total
            else:
                crossed[step * UNROLL + k] += total


def keep_matching(crossed, plane):
    lane_class = lax.broadcasted_iota(jnp.int32, (8, GRID), 1) // 32
    match = lane_class == lax.broadcasted_iota(jnp.int32, (8, GRID), 0)
    row = lax.broadcasted_iota(jnp.int32, (8, GRID), 0)

    @pl.loop(0, 8)
    def _(step):
        for k in range(4):
            xb = step * 4 + k
            total = jnp.zeros((8, GRID), F32)
            for h in range(8):
                part = jnp.where(match, crossed[xb, h * 8 : h * 8 + 8, :], 0.0)
                total = jnp.where(row == h, jnp.sum(part, axis=0, keepdims=True), total)
            plane[pl.ds(pl.multiple_of(xb * 8, 8), 8), :] = total


def solve_plane(tabs, kernel, plane, fields):
    along_x, back_x, along_y = [(tabs[2 * k], tabs[2 * k + 1]) for k in range(3)]
    spectrum = dot3(along_x, split(plane[...]))
    spectrum = dot3(split(spectrum), along_y, NT) * kernel[...]
    field = dot3(back_x, split(spectrum))
    field = dot3(split(field), along_y)
    fields[0] = field[:, :128]
    fields[1] = field[:, 128:]


def spread_cells(fields, cells):
    block = lax.broadcasted_iota(jnp.int32, (32, 128), 1) // 32
    for yb in range(8):
        for h in range(2):
            chosen = None
            for q in range(4):
                part = fields[yb // 4, pl.ds(4 * h + q, 32, stride=8), :]
                shift = (q - yb % 4) % 4 * 32
                part = pltpu.roll(part, shift, 1) if shift else part
                chosen = part if q == 0 else jnp.where(block == q, part, chosen)
            cells[yb, h] = chosen


def answer(half, cells, labels_t, replies_t):
    for yb in range(8):
        for rank in range(2):
            at = pl.ds(rank * 256 + yb, 32, stride=8)
            label = labels_t[half, at, :]
            index = label & 127
            upper = label >> 7
            value = jnp.zeros((32, 128), F32)
            for h in range(2):
                taken = jnp.take_along_axis(cells[yb, h], index, axis=1, mode="promise_in_bounds")
                value = jnp.where(upper == h, taken, value)
            replies_t[half, at, :] = value


VM = pl.BlockSpec(memory_space=pltpu.VMEM)
SM = pl.BlockSpec(memory_space=pltpu.SMEM)


def local(features, fractions, row_ids, stencil_slots, stencil_z, atom_count, w_in, w_out):
    basis, basis_t, plane = [jnp.asarray(table) for table in tables()]
    vmem = pltpu.VMEM
    chunks = ATOMS // CHUNK
    sums, lifts = pl.pallas_call(
        step_kernel,
        out_shape=(
            jax.ShapeDtypeStruct((8, ATOMS), F32),
            jax.ShapeDtypeStruct((128, ATOMS), BF16),
        ),
        in_specs=[VM] * 4 + [SM] + [VM] * 6,
        out_specs=(VM, VM),
        scratch_shapes=[
            vmem((ROWS, 128), F32),
            vmem((ROWS, 128), F32),
            vmem((8, ROWS), F32),
            vmem((2, 4, 4, 8, ROWS), F32),
            vmem((1, ATOMS), F32),
            vmem((1, ATOMS), jnp.int32),
            vmem((3, 32, ATOMS), F32),
            vmem((24, ATOMS), F32),
            vmem((24, ATOMS), F32),
            vmem((GRID, CHUNK), BF16),
            vmem((GRID, CHUNK), BF16),
            vmem((GRID, ROWS), F32),
            vmem((DEVICES, ROWS), F32),
            vmem((2, 128, ROWS), F32),
            vmem((2, ROWS, 128), F32),
            vmem((2, ROWS, 128), F32),
            vmem((2, ROWS, 128), jnp.int32),
            vmem((2, ROWS, 128), F32),
            vmem((2, 32, GRID, 256), BF16),
            vmem((32, 64, GRID), F32),
            vmem((GRID, GRID), F32),
            vmem((2, GRID, 128), F32),
            vmem((8, 2, 32, 128), F32),
            vmem((2, ROWS, 128), F32),
            vmem((2, 128, ROWS), F32),
            vmem((DEVICES, ROWS), F32),
            vmem((ROWS,), F32),
            vmem((ROWS,), F32),
            vmem((GRID, GRID), F32),
            vmem((GRID, ROWS), BF16),
            vmem((GRID, ROWS), BF16),
            vmem((6, chunks, ROWS, CHUNK), BF16),
            pltpu.SemaphoreType.DMA((14,)),
            pltpu.SemaphoreType.DMA((14,)),
            pltpu.SemaphoreType.REGULAR((3,)),
        ]
        + [
            pltpu.SemaphoreType.DMA,
            pltpu.SemaphoreType.DMA,
            pltpu.SemaphoreType.DMA((2,)),
            pltpu.SemaphoreType.DMA,
            pltpu.SemaphoreType.DMA,
        ],
        compiler_params=pltpu.CompilerParams(
            vmem_limit_bytes=VMEM_LIMIT, collective_id=0, has_side_effects=True
        ),
        name="step",
    )(
        row_ids,
        stencil_slots,
        stencil_z.reshape(1, ATOMS),
        fractions,
        atom_count,
        features,
        w_in,
        w_out.reshape(1, 128),
        basis,
        basis_t,
        plane,
    )
    return pl.pallas_call(
        finish_kernel,
        out_shape=(
            jax.ShapeDtypeStruct((3, ATOMS), F32),
            jax.ShapeDtypeStruct((ATOMS, 128), BF16),
        ),
        in_specs=[VM] * 3,
        out_specs=(VM, VM),
        compiler_params=pltpu.CompilerParams(vmem_limit_bytes=VMEM_LIMIT),
        name="finish",
    )(sums, lifts, w_in)


def solution(mesh):
    placed = (
        P(("pen", "slab"), None),
        P(None, ("pen", "slab")),
        P(("pen", "slab"), None),
        P(None, ("pen", "slab")),
        P(("pen", "slab")),
        P(("pen", "slab")),
        P(),
        P(),
    )
    return jax.shard_map(
        local,
        mesh=mesh,
        in_specs=placed,
        out_specs=(P(None, ("pen", "slab")), P(("pen", "slab"), None)),
        check_vma=False,
    )
```

```python
import functools
import math

import jax
import jax.numpy as jnp
import ml_dtypes
import numpy as np
from jax import lax
from jax.experimental import pallas as pl
from jax.experimental.pallas import tpu as pltpu
from jax.sharding import PartitionSpec as P

GRID = 256
COUPLE = 8.0
SMOOTH = 1.0
ROWS = 512
ATOMS = 2048
DEVICES = 256
CHUNK = 512
UNROLL = 8
UNROLL_W = 2
UNROLL_Y = 4
VMEM_LIMIT = 56 * 1024 * 1024
F32 = jnp.float32
BF16 = jnp.bfloat16

NN = (((1,), (0,)), ((), ()))
NT = (((1,), (1,)), ((), ()))


def dot(left, right, dims=NN):
    return lax.dot_general(left, right, dims, preferred_element_type=F32)


def split(value):
    high = value.astype(BF16)
    low = (value - high.astype(F32)).astype(BF16)
    return (high, low)


def dot3(left, right, dims=NN):
    return (
        dot(left[0], right[0], dims)
        + dot(left[0], right[1], dims)
        + dot(left[1], right[0], dims)
    )


def fourier_basis():
    cell = np.arange(GRID)
    wave = np.arange(GRID)
    wave = np.where(wave <= GRID // 2, wave, wave - GRID // 2)
    angle = 2.0 * np.pi * ((wave[:, None] * cell[None, :]) % GRID) / GRID
    basis = np.where(np.arange(GRID)[:, None] <= GRID // 2, np.cos(angle), np.sin(angle))
    scale = np.where((np.arange(GRID) == 0) | (np.arange(GRID) == GRID // 2), 1.0, 2.0)
    return basis * np.sqrt(scale / GRID)[:, None]


def split_table(table):
    table = table.astype(np.float32)
    high = table.astype(ml_dtypes.bfloat16)
    low = (table - high.astype(np.float32)).astype(ml_dtypes.bfloat16)
    return [high, low]


def tables():
    basis = fourier_basis()
    place = np.arange(GRID)
    along_x = basis[:, (place % 8) * 32 + place // 8]
    along_y = basis[:, (place % 32) * 8 + place // 32]
    plane = np.stack(split_table(along_x) + split_table(along_x.T) + split_table(along_y))
    return (np.stack(split_table(basis)), np.stack(split_table(basis.T)), plane)


def spline_values(u):
    rest = 1.0 - u
    square = u * u
    cube = square * u
    return (
        rest * rest * rest / 6.0,
        (3.0 * cube - 6.0 * square + 4.0) / 6.0,
        (-3.0 * cube + 3.0 * square + 3.0 * u + 1.0) / 6.0,
        cube / 6.0,
    )


def spline_slopes(u):
    rest = 1.0 - u
    square = u * u
    return (
        -rest * rest / 2.0,
        (3.0 * square - 4.0 * u) / 2.0,
        (-3.0 * square + 2.0 * u + 1.0) / 2.0,
        square / 2.0,
    )


def pick(step, values):
    out = jnp.where(step == 3, values[3], 0.0)
    for k in (2, 1, 0):
        out = jnp.where(step == k, values[k], out)
    return out


def row_to_columns(row):
    return jnp.transpose(jnp.broadcast_to(row, (128, 128)))


def bin_labels(row_ids, ids_cols, bins_cols):
    ids = row_ids[...]
    used = ids >= 0
    x = ids >> 8
    y = ids & 255
    group = jnp.where(used, (x & 31) * 8 + (y & 7), -1)
    label = ((x >> 5) * 32 + (y >> 3)).astype(F32)
    place = lax.broadcasted_iota(jnp.int32, (128, ROWS), 1)
    row = lax.broadcasted_iota(jnp.int32, (128, ROWS), 0)
    rank = jnp.zeros((1, ROWS), F32)
    for c in range(ROWS // 128):
        lanes = slice(c * 128, (c + 1) * 128)
        column = row_to_columns(ids[:, lanes])
        ids_cols[lanes, :] = column.astype(F32)
        column = (column >> 8 & 31) * 8 + (column & 7)
        column = jnp.concatenate([column] * (ROWS // 128), axis=1)
        same = (column == group) & (row + c * 128 < place)
        rank += jnp.sum(jnp.where(same, 1.0, 0.0), axis=0, keepdims=True)
    target = jnp.where(used, rank.astype(jnp.int32) * 256 + group, -1)
    for c in range(ROWS // 128):
        hit = target == row + c * 128
        value = jnp.sum(jnp.where(hit, label + 1.0, 0.0), axis=1, keepdims=True) - 1.0
        bins_cols[c * 128 : (c + 1) * 128, :] = jnp.broadcast_to(value, (128, 128))


def corners(slots, ids_cols, corner):
    row = lax.broadcasted_iota(jnp.int32, (ROWS, 128), 0)
    for c in range(ATOMS // 128):
        lanes = slice(c * 128, (c + 1) * 128)
        hit = slots[0:1, lanes] == row
        value = jnp.sum(jnp.where(hit, ids_cols[...], 0.0), axis=0, keepdims=True)
        corner[0:1, lanes] = value.astype(jnp.int32)


def class_weights(corner, fractions, tab_x, tab_y, slopes):
    x0 = corner[0:1, :] >> 8
    y0 = corner[0:1, :] & 255
    value_x = spline_values(fractions[0:1, :])
    value_y = spline_values(fractions[1:2, :])
    step_y = (lax.broadcasted_iota(jnp.int32, (8, ATOMS), 0) - y0) & 7
    tab_y[0:8, :] = pick(step_y, value_y)
    tab_y[8:16, :] = ((((y0 + step_y) >> 3) & 31)).astype(F32)
    if slopes:
        slope_x = spline_slopes(fractions[0:1, :])
        slope_y = spline_slopes(fractions[1:2, :])
        tab_y[16:24, :] = pick(step_y, slope_y)
    for b in range(4):
        rows = slice(b * 8, (b + 1) * 8)
        step_x = (lax.broadcasted_iota(jnp.int32, (8, ATOMS), 0) + b * 8 - x0) & 31
        tab_x[0, rows, :] = pick(step_x, value_x)
        tab_x[1, rows, :] = ((((x0 + step_x) >> 5) & 7) * 32).astype(F32)
        if slopes:
            tab_x[2, rows, :] = pick(step_x, slope_x)


def class_weights_z(stencil_z, fractions, tab_z, slopes):
    z0 = stencil_z[0:1, :]
    step_z = (lax.broadcasted_iota(jnp.int32, (8, ATOMS), 0) - z0) & 7
    tab_z[0:8, :] = pick(step_z, spline_values(fractions[2:3, :]))
    tab_z[8:16, :] = ((((z0 + step_z) >> 3) & 31)).astype(F32)
    if slopes:
        tab_z[16:24, :] = pick(step_z, spline_slopes(fractions[2:3, :]))


def row_weights(tab_x, tab_y, bins_cols, lanes, outs, last, step):
    def twice(part):
        return jnp.concatenate([part, part], axis=0)

    wy = twice(tab_y[0:8, lanes])
    ky = twice(tab_y[8:16, lanes])
    sy = twice(tab_y[16:24, lanes])
    width = wy.shape[1]

    def pair(index, i):
        rows = [tab_x[index, pl.ds(2 * i + k, 1), lanes] for k in range(2)]
        return jnp.concatenate([jnp.broadcast_to(row, (8, width)) for row in rows], axis=0)

    def one(i):
        wx = pair(0, i)
        key = pair(1, i) + ky
        values = [wx * wy, pair(2, i) * wy, wx * sy][:last]
        for rank in range(2):
            rows = pl.ds(pl.multiple_of(rank * 256 + i * 16, 16), 16)
            label = bins_cols[rows, :]
            label = jnp.concatenate([label] * (width // 128), axis=1)
            hit = key == label
            for k, value in enumerate(values):
                high, low = split(jnp.where(hit, value, 0.0))
                outs[step * k][rows, :] = high
                if step == 2:
                    outs[step * k + 1][rows, :] = low

    return one


def run_all(one):
    @pl.loop(0, 16 // UNROLL_W)
    def _(block):
        for k in range(UNROLL_W):
            one(block * UNROLL_W + k)


MESH = pl.DeviceIdType.MESH
DZ = (4, 1, 7, 2, 6, 3, 5, 0)


def here():
    pen = lax.axis_index("pen")
    slab = lax.axis_index("slab")
    return (pen // 4, lax.rem(pen, 4), slab // 2, lax.rem(slab, 2))


def place_of(z, y, x, core):
    return ((core * 4 + x) * 4 + y) * 8 + z


def target_of(z, y, x, core):
    return (z * 4 + y, x * 2 + core)


def for_others(half, visit, beside):
    z, y, x, core = here()
    other_core = lax.rem(core + half, 2)

    @pl.loop(0, 16)
    def _(k):
        other_y = lax.rem(y + lax.rem(k, 4), 4)
        other_x = lax.rem(x + k // 4, 4)
        for dz in DZ:
            there = (lax.rem(z + dz, 8), other_y, other_x, other_core)
            if dz == 0 and half == 0:
                pl.when(k > 0)(functools.partial(visit, there))
            else:
                visit(there)
        for work in beside:
            work(k)


def lines():
    z, y, x, core = here()
    return (
        [(lax.rem(z + k, 8), y, x, core) for k in range(1, 8)],
        [(z, lax.rem(y + k, 4), x, core) for k in range(1, 4)],
        [(z, y, lax.rem(x + k, 4), core) for k in range(1, 4)],
        [(z, y, x, 1 - core)],
    )


def send_half(half, row_of, landed, send_sem, recv_sem, beside=()):
    def send(there):
        pltpu.make_async_remote_copy(
            src_ref=row_of(there),
            dst_ref=landed,
            send_sem=send_sem,
            recv_sem=recv_sem,
            device_id=target_of(*there),
            device_id_type=MESH,
        ).start()

    for_others(half, send, beside)


def await_bytes(like, sem):
    pltpu.make_async_copy(like, like, sem).wait()


def label_copies(stage, all_labels, send_sems, recv_sems):
    z, y, x, core = here()
    part = (
        all_labels.at[core, x, y, z],
        all_labels.at[core, x, y],
        all_labels.at[core, x],
        all_labels.at[core],
    )[stage]
    first = (0, 7, 10, 13)[stage]
    peers = lines()[stage]
    return [
        pltpu.make_async_remote_copy(
            src_ref=part,
            dst_ref=part,
            send_sem=send_sems.at[first + k],
            recv_sem=recv_sems.at[first + k],
            device_id=target_of(*peer),
            device_id_type=MESH,
        )
        for k, peer in enumerate(peers)
    ]


def step_kernel(
    row_ids,
    slots,
    stencil_z,
    fractions,
    atom_count,
    features,
    w_in,
    w_out,
    basis,
    basis_t,
    tabs,
    sums,
    lifts,
    ids_cols,
    bins_cols,
    own_labels,
    all_labels,
    charges,
    corner,
    tab_x,
    tab_y,
    tab_z,
    z_high,
    z_low,
    mesh_rows,
    sent,
    arrived,
    rows_high,
    rows_low,
    labels_t,
    labels_x,
    onehot_y,
    crossed,
    plane,
    fields,
    cells,
    replies_t,
    replies,
    returned,
    spare,
    spare_two,
    kernel,
    field_high,
    field_low,
    weights,
    label_send,
    label_recv,
    line_sems,
    sem_own,
    send_one,
    recv_one,
    send_two,
    recv_two,
):
    barrier = pltpu.get_barrier_semaphore()
    for peers in lines():
        for peer in peers:
            pl.semaphore_signal(barrier, inc=1, device_id=target_of(*peer), device_id_type=MESH)
    z, y, x, core = here()
    low = place_of(z, y, x, 0)
    bin_labels(row_ids, ids_cols, bins_cols)
    for c in range(ROWS // 128):
        part = jnp.transpose(bins_cols[c * 128 : (c + 1) * 128, :])
        own_labels[0:1, c * 128 : (c + 1) * 128] = part[0:1, :]
    pl.semaphore_wait(barrier, 14)
    mine = pltpu.make_async_copy(own_labels.at[0], all_labels.at[core, x, y, z], sem_own)
    mine.start()
    mine.wait()

    def labels_on(stage):
        if stage > 0:
            for copy in label_copies(stage - 1, all_labels, label_send, label_recv):
                copy.wait()
        if stage < 4:
            for copy in label_copies(stage, all_labels, label_send, label_recv):
                copy.start()

    def heard_from(stage):
        if stage > 0:
            pl.semaphore_wait(line_sems.at[stage - 1], (3, 3, 1)[stage - 1])
        if stage < 3:
            for peer in lines()[stage + 1]:
                pl.semaphore_signal(
                    line_sems.at[stage], inc=1, device_id=target_of(*peer), device_id_type=MESH
                )

    heard_from(0)
    labels_on(0)
    corners(slots, ids_cols, corner)
    class_weights(corner, fractions, tab_x, tab_y, True)
    class_weights_z(stencil_z, fractions, tab_z, True)
    w_in_t = jnp.transpose(w_in[...].astype(F32)).astype(BF16)
    out_w = jnp.concatenate([row_to_columns(w_out[...])] * (CHUNK // 128), axis=1)
    for c in range(ATOMS // CHUNK):
        lanes = slice(c * CHUNK, (c + 1) * CHUNK)
        pre = dot(w_in_t, features[lanes, :], NT)
        sigma = jax.nn.sigmoid(pre)
        charge = jnp.sum(pre * sigma * out_w, axis=0, keepdims=True)
        atom = lax.broadcasted_iota(jnp.int32, (1, CHUNK), 1) + c * CHUNK
        charges[0:1, lanes] = jnp.where(atom < atom_count[0], charge, 0.0)
        lifts[:, lanes] = (sigma * (1.0 + pre * (1.0 - sigma)) * out_w).astype(BF16)
    heard_from(1)
    labels_on(1)
    for c in range(ATOMS // CHUNK):
        lanes = slice(c * CHUNK, (c + 1) * CHUNK)
        run_all(row_weights(tab_x, tab_y, bins_cols, lanes, [weights.at[0, c]], 1, 1))
        key = tab_z[8:16, lanes]
        amount = tab_z[0:8, lanes] * charges[0:1, lanes]
        amount_high = amount.astype(BF16).astype(F32)
        amount_low = amount - amount_high
        for h in range(0, 32, 2):
            rows = slice(h * 8, h * 8 + 16)
            hits = (key == float(h), key == float(h + 1))
            z_high[rows, :] = jnp.concatenate(
                [jnp.where(hit, amount_high, 0.0) for hit in hits], axis=0
            ).astype(BF16)
            z_low[rows, :] = jnp.concatenate(
                [jnp.where(hit, amount_low, 0.0) for hit in hits], axis=0
            ).astype(BF16)
        total = dot(z_high[...], weights[0, c], NT) + dot(z_low[...], weights[0, c], NT)
        if c == 0:
            mesh_rows[...] = total
        else:
            mesh_rows[...] += total
        if c == 1:
            heard_from(2)
            labels_on(2)
    sent[...] = dot3((basis[0], basis[1]), split(mesh_rows[...]))
    heard_from(3)
    own = sent.at[core * 128 + low]
    pltpu.make_async_copy(own, arrived.at[0, low], recv_one.at[0]).start()
    pltpu.make_async_copy(own, spare, send_one).start()
    for half in range(2):
        send_half(
            half,
            lambda there: sent.at[place_of(*there)],
            arrived.at[half, low],
            send_one,
            recv_one.at[half],
            [
                row_weights(
                    tab_x,
                    tab_y,
                    bins_cols,
                    slice(c * CHUNK, (c + 1) * CHUNK),
                    [weights.at[k, c] for k in range(6)],
                    3,
                    2,
                )
                for c in (2 * half, 2 * half + 1)
            ],
        )
        if half == 0:
            labels_on(3)
    coulomb(kernel, core * 128 + low)
    labels_on(4)
    cell_y = lax.broadcasted_iota(jnp.int32, (32, 128), 0).astype(F32)
    for half in range(2):
        for c in range(ROWS // 128):
            bins = slice(c * 128, (c + 1) * 128)
            part = all_labels[lax.rem(core + half, 2), :, :, :, bins].reshape(128, 128)
            part = jnp.transpose(part)
            labels_t[half, bins, :] = part.astype(jnp.int32)
            labels_x[half, bins, :] = jnp.floor(part * (1.0 / 32.0))

        @pl.loop(0, 32 // UNROLL_Y)
        def _(step):
            for k, rank in [(k, rank) for k in range(UNROLL_Y) for rank in range(2)]:
                xb = step * UNROLL_Y + k
                at = pl.ds(pl.multiple_of(rank * 256 + xb * 8, 8), 8)
                label_y = (labels_t[half, at, :] & 31).astype(F32)
                for yb in range(8):
                    hit = jnp.broadcast_to(label_y[yb : yb + 1], (32, 128)) == cell_y
                    onehot_y[half, xb, yb * 32 : yb * 32 + 32, rank * 128 : rank * 128 + 128] = jnp.where(
                        hit, 1.0, 0.0
                    ).astype(BF16)

    for half in range(2):
        await_bytes(arrived.at[half], recv_one.at[half])
        for c in range(ROWS // 128):
            bins = slice(c * 128, (c + 1) * 128)
            part = jnp.transpose(arrived[half, :, bins])
            part_high = part.astype(BF16).astype(F32)
            rows_high[half, bins, :] = part_high
            rows_low[half, bins, :] = part - part_high
        gather_plane(half, rows_high, rows_low, labels_x, onehot_y, crossed)
    keep_matching(crossed, plane)
    solve_plane(tabs, kernel, plane, fields)
    spread_cells(fields, cells)
    own = replies.at[0, low]
    for half in range(2):
        answer(half, cells, labels_t, replies_t)
        for c in range(ROWS // 128):
            bins = slice(c * 128, (c + 1) * 128)
            replies[half, :, bins] = jnp.transpose(replies_t[half, bins, :])
        if half == 0:
            pltpu.make_async_copy(own, returned.at[core * 128 + low], recv_two).start()
            pltpu.make_async_copy(own, spare_two, send_two).start()
        send_half(
            half,
            lambda there: replies.at[half, place_of(there[0], there[1], there[2], 0)],
            returned.at[core * 128 + low],
            send_two,
            recv_two,
        )
    await_bytes(sent, send_one)
    await_bytes(returned, recv_two)

    field_high[...], field_low[...] = split(
        dot3((basis_t[0], basis_t[1]), split(returned[...]))
    )
    for c in range(ATOMS // CHUNK):
        lanes = slice(c * CHUNK, (c + 1) * CHUNK)
        key = tab_z[8:16, lanes]
        picked = []
        for k in range(3):
            total = dot3(
                (field_high[...], field_low[...]), (weights[2 * k, c], weights[2 * k + 1, c])
            )
            chosen = jnp.zeros((8, CHUNK), F32)
            for h in range(32):
                chosen = jnp.where(key == float(h), total[h * 8 : (h + 1) * 8], chosen)
            picked.append(chosen)
        wz = tab_z[0:8, lanes]
        potential = jnp.sum(wz * picked[0], axis=0, keepdims=True)
        charge = -charges[0:1, lanes]
        sums[0:1, lanes] = charge * jnp.sum(wz * picked[1], axis=0, keepdims=True)
        sums[1:2, lanes] = charge * jnp.sum(wz * picked[2], axis=0, keepdims=True)
        sums[2:3, lanes] = charge * jnp.sum(tab_z[16:24, lanes] * picked[0], axis=0, keepdims=True)
        atom = lax.broadcasted_iota(jnp.int32, (1, CHUNK), 1) + c * CHUNK
        sums[3:4, lanes] = jnp.where(atom < atom_count[0], potential, 0.0)
    await_bytes(returned, send_two)


def finish_kernel(sums, lifts, w_in, forces, grads):
    forces[...] = sums[0:3, :]
    for c in range(ATOMS // CHUNK):
        lanes = slice(c * CHUNK, (c + 1) * CHUNK)
        grad = sums[3:4, lanes] * dot(w_in[...], lifts[:, lanes])
        for b in range(CHUNK // 128):
            rows = slice(c * CHUNK + b * 128, c * CHUNK + (b + 1) * 128)
            grads[rows, :] = jnp.transpose(grad[:, b * 128 : (b + 1) * 128]).astype(BF16)


def coulomb(kernel, wave_index):
    half = GRID // 2

    def wave(index):
        return jnp.where(index <= half, index, index - half)

    wave_x = wave(lax.broadcasted_iota(jnp.int32, (GRID, GRID), 0))
    wave_y = wave(lax.broadcasted_iota(jnp.int32, (GRID, GRID), 1))
    wave_z = wave(wave_index)
    squared = (wave_x * wave_x + wave_y * wave_y + wave_z * wave_z).astype(F32)
    damped = jnp.exp(-((SMOOTH * math.pi / GRID) ** 2) * squared)
    values = COUPLE * damped * (GRID * GRID) / (4.0 * math.pi * math.pi * jnp.maximum(squared, 1.0))
    keep = (squared > 0) & (wave_x != half) & (wave_y != half) & (wave_z != half)
    kernel[...] = jnp.where(keep, values, 0.0)


def gather_plane(half, rows_high, rows_low, labels_x, onehot_y, crossed):
    def one(xb):
        left = []
        for rank in range(2):
            at = pl.ds(pl.multiple_of(rank * 256 + xb * 8, 8), 8)
            high, low = rows_high[half, at, :], rows_low[half, at, :]
            label_x = labels_x[half, at, :]
            hits = [label_x == float(h) for h in range(8)]
            parts = [jnp.where(hit, part, 0.0) for part in (high, low) for hit in hits]
            left.append(jnp.concatenate(parts, axis=0).astype(BF16))
        both = dot(jnp.concatenate(left, axis=1), onehot_y[half, xb], NT)
        return both[0:64] + both[64:128]

    @pl.loop(0, 32 // UNROLL)
    def _(step):
        totals = [one(step * UNROLL + k) for k in range(UNROLL)]
        for k, total in enumerate(totals):
            if half == 0:
                crossed[step * UNROLL + k] = total
            else:
                crossed[step * UNROLL + k] += total


def keep_matching(crossed, plane):
    lane_class = lax.broadcasted_iota(jnp.int32, (8, GRID), 1) // 32
    match = lane_class == lax.broadcasted_iota(jnp.int32, (8, GRID), 0)
    row = lax.broadcasted_iota(jnp.int32, (8, GRID), 0)

    @pl.loop(0, 8)
    def _(step):
        for k in range(4):
            xb = step * 4 + k
            total = jnp.zeros((8, GRID), F32)
            for h in range(8):
                part = jnp.where(match, crossed[xb, h * 8 : h * 8 + 8, :], 0.0)
                total = jnp.where(row == h, jnp.sum(part, axis=0, keepdims=True), total)
            plane[pl.ds(pl.multiple_of(xb * 8, 8), 8), :] = total


def solve_plane(tabs, kernel, plane, fields):
    along_x, back_x, along_y = [(tabs[2 * k], tabs[2 * k + 1]) for k in range(3)]
    spectrum = dot3(along_x, split(plane[...]))
    spectrum = dot3(split(spectrum), along_y, NT) * kernel[...]
    field = dot3(back_x, split(spectrum))
    field = dot3(split(field), along_y)
    fields[0] = field[:, :128]
    fields[1] = field[:, 128:]


def spread_cells(fields, cells):
    block = lax.broadcasted_iota(jnp.int32, (32, 128), 1) // 32
    for yb in range(8):
        for h in range(2):
            chosen = None
            for q in range(4):
                part = fields[yb // 4, pl.ds(4 * h + q, 32, stride=8), :]
                shift = (q - yb % 4) % 4 * 32
                part = pltpu.roll(part, shift, 1) if shift else part
                chosen = part if q == 0 else jnp.where(block == q, part, chosen)
            cells[yb, h] = chosen


def answer(half, cells, labels_t, replies_t):
    for yb in range(8):
        for rank in range(2):
            at = pl.ds(rank * 256 + yb, 32, stride=8)
            label = labels_t[half, at, :]
            index = label & 127
            upper = label >> 7
            value = jnp.zeros((32, 128), F32)
            for h in range(2):
                taken = jnp.take_along_axis(cells[yb, h], index, axis=1, mode="promise_in_bounds")
                value = jnp.where(upper == h, taken, value)
            replies_t[half, at, :] = value


VM = pl.BlockSpec(memory_space=pltpu.VMEM)
SM = pl.BlockSpec(memory_space=pltpu.SMEM)


def local(features, fractions, row_ids, stencil_slots, stencil_z, atom_count, w_in, w_out):
    basis, basis_t, plane = [jnp.asarray(table) for table in tables()]
    vmem = pltpu.VMEM
    chunks = ATOMS // CHUNK
    sums, lifts = pl.pallas_call(
        step_kernel,
        out_shape=(
            jax.ShapeDtypeStruct((8, ATOMS), F32),
            jax.ShapeDtypeStruct((128, ATOMS), BF16),
        ),
        in_specs=[VM] * 4 + [SM] + [VM] * 6,
        out_specs=(VM, VM),
        scratch_shapes=[
            vmem((ROWS, 128), F32),
            vmem((ROWS, 128), F32),
            vmem((8, ROWS), F32),
            vmem((2, 4, 4, 8, ROWS), F32),
            vmem((1, ATOMS), F32),
            vmem((1, ATOMS), jnp.int32),
            vmem((3, 32, ATOMS), F32),
            vmem((24, ATOMS), F32),
            vmem((24, ATOMS), F32),
            vmem((GRID, CHUNK), BF16),
            vmem((GRID, CHUNK), BF16),
            vmem((GRID, ROWS), F32),
            vmem((DEVICES, ROWS), F32),
            vmem((2, 128, ROWS), F32),
            vmem((2, ROWS, 128), F32),
            vmem((2, ROWS, 128), F32),
            vmem((2, ROWS, 128), jnp.int32),
            vmem((2, ROWS, 128), F32),
            vmem((2, 32, GRID, 256), BF16),
            vmem((32, 64, GRID), F32),
            vmem((GRID, GRID), F32),
            vmem((2, GRID, 128), F32),
            vmem((8, 2, 32, 128), F32),
            vmem((2, ROWS, 128), F32),
            vmem((2, 128, ROWS), F32),
            vmem((DEVICES, ROWS), F32),
            vmem((ROWS,), F32),
            vmem((ROWS,), F32),
            vmem((GRID, GRID), F32),
            vmem((GRID, ROWS), BF16),
            vmem((GRID, ROWS), BF16),
            vmem((6, chunks, ROWS, CHUNK), BF16),
            pltpu.SemaphoreType.DMA((14,)),
            pltpu.SemaphoreType.DMA((14,)),
            pltpu.SemaphoreType.REGULAR((3,)),
        ]
        + [
            pltpu.SemaphoreType.DMA,
            pltpu.SemaphoreType.DMA,
            pltpu.SemaphoreType.DMA((2,)),
            pltpu.SemaphoreType.DMA,
            pltpu.SemaphoreType.DMA,
        ],
        compiler_params=pltpu.CompilerParams(
            vmem_limit_bytes=VMEM_LIMIT, collective_id=0, has_side_effects=True
        ),
        name="step",
    )(
        row_ids,
        stencil_slots,
        stencil_z.reshape(1, ATOMS),
        fractions,
        atom_count,
        features,
        w_in,
        w_out.reshape(1, 128),
        basis,
        basis_t,
        plane,
    )
    return pl.pallas_call(
        finish_kernel,
        out_shape=(
            jax.ShapeDtypeStruct((3, ATOMS), F32),
            jax.ShapeDtypeStruct((ATOMS, 128), BF16),
        ),
        in_specs=[VM] * 3,
        out_specs=(VM, VM),
        compiler_params=pltpu.CompilerParams(vmem_limit_bytes=VMEM_LIMIT),
        name="finish",
    )(sums, lifts, w_in)


def solution(mesh):
    placed = (
        P(("pen", "slab"), None),
        P(None, ("pen", "slab")),
        P(("pen", "slab"), None),
        P(None, ("pen", "slab")),
        P(("pen", "slab")),
        P(("pen", "slab")),
        P(),
        P(),
    )
    return jax.shard_map(
        local,
        mesh=mesh,
        in_specs=placed,
        out_specs=(P(None, ("pen", "slab")), P(("pen", "slab"), None)),
        check_vma=False,
    )
```

```python
import functools
import math

import jax
import jax.numpy as jnp
import ml_dtypes
import numpy as np
from jax import lax
from jax.experimental import pallas as pl
from jax.experimental.pallas import tpu as pltpu
from jax.sharding import PartitionSpec as P

GRID = 256
COUPLE = 8.0
SMOOTH = 1.0
ROWS = 512
ATOMS = 2048
DEVICES = 256
CHUNK = 512
UNROLL = 8
UNROLL_W = 2
UNROLL_Y = 4
VMEM_LIMIT = 56 * 1024 * 1024
F32 = jnp.float32
BF16 = jnp.bfloat16

NN = (((1,), (0,)), ((), ()))
NT = (((1,), (1,)), ((), ()))


def dot(left, right, dims=NN):
    return lax.dot_general(left, right, dims, preferred_element_type=F32)


def split(value):
    high = value.astype(BF16)
    low = (value - high.astype(F32)).astype(BF16)
    return (high, low)


def dot3(left, right, dims=NN):
    return (
        dot(left[0], right[0], dims)
        + dot(left[0], right[1], dims)
        + dot(left[1], right[0], dims)
    )


def fourier_basis():
    cell = np.arange(GRID)
    wave = np.arange(GRID)
    wave = np.where(wave <= GRID // 2, wave, wave - GRID // 2)
    angle = 2.0 * np.pi * ((wave[:, None] * cell[None, :]) % GRID) / GRID
    basis = np.where(np.arange(GRID)[:, None] <= GRID // 2, np.cos(angle), np.sin(angle))
    scale = np.where((np.arange(GRID) == 0) | (np.arange(GRID) == GRID // 2), 1.0, 2.0)
    return basis * np.sqrt(scale / GRID)[:, None]


def split_table(table):
    table = table.astype(np.float32)
    high = table.astype(ml_dtypes.bfloat16)
    low = (table - high.astype(np.float32)).astype(ml_dtypes.bfloat16)
    return [high, low]


def tables():
    basis = fourier_basis()
    place = np.arange(GRID)
    along_x = basis[:, (place % 8) * 32 + place // 8]
    along_y = basis[:, (place % 32) * 8 + place // 32]
    plane = np.stack(split_table(along_x) + split_table(along_x.T) + split_table(along_y))
    return (np.stack(split_table(basis)), np.stack(split_table(basis.T)), plane)


def spline_values(u):
    rest = 1.0 - u
    square = u * u
    cube = square * u
    return (
        rest * rest * rest / 6.0,
        (3.0 * cube - 6.0 * square + 4.0) / 6.0,
        (-3.0 * cube + 3.0 * square + 3.0 * u + 1.0) / 6.0,
        cube / 6.0,
    )


def spline_slopes(u):
    rest = 1.0 - u
    square = u * u
    return (
        -rest * rest / 2.0,
        (3.0 * square - 4.0 * u) / 2.0,
        (-3.0 * square + 2.0 * u + 1.0) / 2.0,
        square / 2.0,
    )


def pick(step, values):
    out = jnp.where(step == 3, values[3], 0.0)
    for k in (2, 1, 0):
        out = jnp.where(step == k, values[k], out)
    return out


def row_to_columns(row):
    return jnp.transpose(jnp.broadcast_to(row, (128, 128)))


def bin_labels(row_ids, ids_cols, bins_cols):
    ids = row_ids[...]
    used = ids >= 0
    x = ids >> 8
    y = ids & 255
    group = jnp.where(used, (x & 31) * 8 + (y & 7), -1)
    label = ((x >> 5) * 32 + (y >> 3)).astype(F32)
    place = lax.broadcasted_iota(jnp.int32, (128, ROWS), 1)
    row = lax.broadcasted_iota(jnp.int32, (128, ROWS), 0)
    rank = jnp.zeros((1, ROWS), F32)
    for c in range(ROWS // 128):
        lanes = slice(c * 128, (c + 1) * 128)
        column = row_to_columns(ids[:, lanes])
        ids_cols[lanes, :] = column.astype(F32)
        column = (column >> 8 & 31) * 8 + (column & 7)
        column = jnp.concatenate([column] * (ROWS // 128), axis=1)
        same = (column == group) & (row + c * 128 < place)
        rank += jnp.sum(jnp.where(same, 1.0, 0.0), axis=0, keepdims=True)
    target = jnp.where(used, rank.astype(jnp.int32) * 256 + group, -1)
    for c in range(ROWS // 128):
        hit = target == row + c * 128
        value = jnp.sum(jnp.where(hit, label + 1.0, 0.0), axis=1, keepdims=True) - 1.0
        bins_cols[c * 128 : (c + 1) * 128, :] = jnp.broadcast_to(value, (128, 128))


def corners(slots, ids_cols, corner):
    row = lax.broadcasted_iota(jnp.int32, (ROWS, 128), 0)
    for c in range(ATOMS // 128):
        lanes = slice(c * 128, (c + 1) * 128)
        hit = slots[0:1, lanes] == row
        value = jnp.sum(jnp.where(hit, ids_cols[...], 0.0), axis=0, keepdims=True)
        corner[0:1, lanes] = value.astype(jnp.int32)


def class_weights(corner, fractions, tab_x, tab_y, slopes):
    x0 = corner[0:1, :] >> 8
    y0 = corner[0:1, :] & 255
    value_x = spline_values(fractions[0:1, :])
    value_y = spline_values(fractions[1:2, :])
    step_y = (lax.broadcasted_iota(jnp.int32, (8, ATOMS), 0) - y0) & 7
    tab_y[0:8, :] = pick(step_y, value_y)
    tab_y[8:16, :] = ((((y0 + step_y) >> 3) & 31)).astype(F32)
    if slopes:
        slope_x = spline_slopes(fractions[0:1, :])
        slope_y = spline_slopes(fractions[1:2, :])
        tab_y[16:24, :] = pick(step_y, slope_y)
    for b in range(4):
        rows = slice(b * 8, (b + 1) * 8)
        step_x = (lax.broadcasted_iota(jnp.int32, (8, ATOMS), 0) + b * 8 - x0) & 31
        tab_x[0, rows, :] = pick(step_x, value_x)
        tab_x[1, rows, :] = ((((x0 + step_x) >> 5) & 7) * 32).astype(F32)
        if slopes:
            tab_x[2, rows, :] = pick(step_x, slope_x)


def class_weights_z(stencil_z, fractions, tab_z, slopes):
    z0 = stencil_z[0:1, :]
    step_z = (lax.broadcasted_iota(jnp.int32, (8, ATOMS), 0) - z0) & 7
    tab_z[0:8, :] = pick(step_z, spline_values(fractions[2:3, :]))
    tab_z[8:16, :] = ((((z0 + step_z) >> 3) & 31)).astype(F32)
    if slopes:
        tab_z[16:24, :] = pick(step_z, spline_slopes(fractions[2:3, :]))


def row_weights(tab_x, tab_y, bins_cols, lanes, outs, last, step):
    def twice(part):
        return jnp.concatenate([part, part], axis=0)

    wy = twice(tab_y[0:8, lanes])
    ky = twice(tab_y[8:16, lanes])
    sy = twice(tab_y[16:24, lanes])
    width = wy.shape[1]

    def pair(index, i):
        rows = [tab_x[index, pl.ds(2 * i + k, 1), lanes] for k in range(2)]
        return jnp.concatenate([jnp.broadcast_to(row, (8, width)) for row in rows], axis=0)

    def one(i):
        wx = pair(0, i)
        key = pair(1, i) + ky
        values = [wx * wy, pair(2, i) * wy, wx * sy][:last]
        for rank in range(2):
            rows = pl.ds(pl.multiple_of(rank * 256 + i * 16, 16), 16)
            label = bins_cols[rows, :]
            label = jnp.concatenate([label] * (width // 128), axis=1)
            hit = key == label
            for k, value in enumerate(values):
                high, low = split(jnp.where(hit, value, 0.0))
                outs[step * k][rows, :] = high
                if step == 2:
                    outs[step * k + 1][rows, :] = low

    @pl.loop(0, 16 // UNROLL_W)
    def _(block):
        for k in range(UNROLL_W):
            one(block * UNROLL_W + k)


MESH = pl.DeviceIdType.MESH
DZ = (4, 1, 7, 2, 6, 3, 5, 0)


def here():
    pen = lax.axis_index("pen")
    slab = lax.axis_index("slab")
    return (pen // 4, lax.rem(pen, 4), slab // 2, lax.rem(slab, 2))


def place_of(z, y, x, core):
    return ((core * 4 + x) * 4 + y) * 8 + z


def target_of(z, y, x, core):
    return (z * 4 + y, x * 2 + core)


def for_others(half, visit):
    z, y, x, core = here()
    other_core = lax.rem(core + half, 2)

    @pl.loop(0, 16)
    def _(k):
        other_y = lax.rem(y + lax.rem(k, 4), 4)
        other_x = lax.rem(x + k // 4, 4)
        for dz in DZ:
            there = (lax.rem(z + dz, 8), other_y, other_x, other_core)
            if dz == 0 and half == 0:
                pl.when(k > 0)(functools.partial(visit, there))
            else:
                visit(there)


def lines():
    z, y, x, core = here()
    return (
        [(lax.rem(z + k, 8), y, x, core) for k in range(1, 8)],
        [(z, lax.rem(y + k, 4), x, core) for k in range(1, 4)],
        [(z, y, lax.rem(x + k, 4), core) for k in range(1, 4)],
        [(z, y, x, 1 - core)],
    )


def send_half(half, row_of, landed, send_sem, recv_sem):
    def send(there):
        pltpu.make_async_remote_copy(
            src_ref=row_of(there),
            dst_ref=landed,
            send_sem=send_sem,
            recv_sem=recv_sem,
            device_id=target_of(*there),
            device_id_type=MESH,
        ).start()

    for_others(half, send)


def await_bytes(like, sem):
    pltpu.make_async_copy(like, like, sem).wait()


def label_copies(stage, all_labels, send_sems, recv_sems):
    z, y, x, core = here()
    part = (
        all_labels.at[core, x, y, z],
        all_labels.at[core, x, y],
        all_labels.at[core, x],
        all_labels.at[core],
    )[stage]
    first = (0, 7, 10, 13)[stage]
    peers = lines()[stage]
    return [
        pltpu.make_async_remote_copy(
            src_ref=part,
            dst_ref=part,
            send_sem=send_sems.at[first + k],
            recv_sem=recv_sems.at[first + k],
            device_id=target_of(*peer),
            device_id_type=MESH,
        )
        for k, peer in enumerate(peers)
    ]


def step_kernel(
    row_ids,
    slots,
    stencil_z,
    fractions,
    atom_count,
    features,
    w_in,
    w_out,
    basis,
    basis_t,
    tabs,
    sums,
    lifts,
    ids_cols,
    bins_cols,
    own_labels,
    all_labels,
    charges,
    corner,
    tab_x,
    tab_y,
    tab_z,
    z_high,
    z_low,
    mesh_rows,
    sent,
    arrived,
    rows_high,
    rows_low,
    labels_t,
    labels_x,
    onehot_y,
    crossed,
    plane,
    fields,
    cells,
    replies_t,
    replies,
    returned,
    spare,
    spare_two,
    kernel,
    field_high,
    field_low,
    weights,
    label_send,
    label_recv,
    line_sems,
    sem_own,
    send_one,
    recv_one,
    send_two,
    recv_two,
):
    barrier = pltpu.get_barrier_semaphore()
    for peers in lines():
        for peer in peers:
            pl.semaphore_signal(barrier, inc=1, device_id=target_of(*peer), device_id_type=MESH)
    z, y, x, core = here()
    low = place_of(z, y, x, 0)
    bin_labels(row_ids, ids_cols, bins_cols)
    for c in range(ROWS // 128):
        part = jnp.transpose(bins_cols[c * 128 : (c + 1) * 128, :])
        own_labels[0:1, c * 128 : (c + 1) * 128] = part[0:1, :]
    pl.semaphore_wait(barrier, 14)
    mine = pltpu.make_async_copy(own_labels.at[0], all_labels.at[core, x, y, z], sem_own)
    mine.start()
    mine.wait()

    def labels_on(stage):
        if stage > 0:
            for copy in label_copies(stage - 1, all_labels, label_send, label_recv):
                copy.wait()
        if stage < 4:
            for copy in label_copies(stage, all_labels, label_send, label_recv):
                copy.start()

    def heard_from(stage):
        if stage > 0:
            pl.semaphore_wait(line_sems.at[stage - 1], (3, 3, 1)[stage - 1])
        if stage < 3:
            for peer in lines()[stage + 1]:
                pl.semaphore_signal(
                    line_sems.at[stage], inc=1, device_id=target_of(*peer), device_id_type=MESH
                )

    heard_from(0)
    labels_on(0)
    corners(slots, ids_cols, corner)
    class_weights(corner, fractions, tab_x, tab_y, True)
    class_weights_z(stencil_z, fractions, tab_z, True)
    w_in_t = jnp.transpose(w_in[...].astype(F32)).astype(BF16)
    out_w = jnp.concatenate([row_to_columns(w_out[...])] * (CHUNK // 128), axis=1)
    for c in range(ATOMS // CHUNK):
        lanes = slice(c * CHUNK, (c + 1) * CHUNK)
        pre = dot(w_in_t, features[lanes, :], NT)
        sigma = jax.nn.sigmoid(pre)
        charge = jnp.sum(pre * sigma * out_w, axis=0, keepdims=True)
        atom = lax.broadcasted_iota(jnp.int32, (1, CHUNK), 1) + c * CHUNK
        charges[0:1, lanes] = jnp.where(atom < atom_count[0], charge, 0.0)
        lifts[:, lanes] = (sigma * (1.0 + pre * (1.0 - sigma)) * out_w).astype(BF16)
    heard_from(1)
    labels_on(1)
    for c in range(ATOMS // CHUNK):
        lanes = slice(c * CHUNK, (c + 1) * CHUNK)
        row_weights(tab_x, tab_y, bins_cols, lanes, [weights.at[0, c]], 1, 1)
        key = tab_z[8:16, lanes]
        amount = tab_z[0:8, lanes] * charges[0:1, lanes]
        amount_high = amount.astype(BF16).astype(F32)
        amount_low = amount - amount_high
        for h in range(0, 32, 2):
            rows = slice(h * 8, h * 8 + 16)
            hits = (key == float(h), key == float(h + 1))
            z_high[rows, :] = jnp.concatenate(
                [jnp.where(hit, amount_high, 0.0) for hit in hits], axis=0
            ).astype(BF16)
            z_low[rows, :] = jnp.concatenate(
                [jnp.where(hit, amount_low, 0.0) for hit in hits], axis=0
            ).astype(BF16)
        total = dot(z_high[...], weights[0, c], NT) + dot(z_low[...], weights[0, c], NT)
        if c == 0:
            mesh_rows[...] = total
        else:
            mesh_rows[...] += total
        if c == 1:
            heard_from(2)
            labels_on(2)
    sent[...] = dot3((basis[0], basis[1]), split(mesh_rows[...]))
    heard_from(3)
    own = sent.at[core * 128 + low]
    pltpu.make_async_copy(own, arrived.at[0, low], recv_one.at[0]).start()
    pltpu.make_async_copy(own, spare, send_one).start()
    for half in range(2):
        send_half(
            half,
            lambda there: sent.at[place_of(*there)],
            arrived.at[half, low],
            send_one,
            recv_one.at[half],
        )
        if half == 0:
            labels_on(3)
    for c in range(ATOMS // CHUNK):
        lanes = slice(c * CHUNK, (c + 1) * CHUNK)
        row_weights(tab_x, tab_y, bins_cols, lanes, [weights.at[k, c] for k in range(6)], 3, 2)
    coulomb(kernel, core * 128 + low)
    labels_on(4)
    cell_y = lax.broadcasted_iota(jnp.int32, (32, 128), 0).astype(F32)
    for half in range(2):
        for c in range(ROWS // 128):
            bins = slice(c * 128, (c + 1) * 128)
            part = all_labels[lax.rem(core + half, 2), :, :, :, bins].reshape(128, 128)
            part = jnp.transpose(part)
            labels_t[half, bins, :] = part.astype(jnp.int32)
            labels_x[half, bins, :] = jnp.floor(part * (1.0 / 32.0))

        @pl.loop(0, 32 // UNROLL_Y)
        def _(step):
            for k, rank in [(k, rank) for k in range(UNROLL_Y) for rank in range(2)]:
                xb = step * UNROLL_Y + k
                at = pl.ds(pl.multiple_of(rank * 256 + xb * 8, 8), 8)
                label_y = (labels_t[half, at, :] & 31).astype(F32)
                for yb in range(8):
                    hit = jnp.broadcast_to(label_y[yb : yb + 1], (32, 128)) == cell_y
                    onehot_y[half, xb, yb * 32 : yb * 32 + 32, rank * 128 : rank * 128 + 128] = jnp.where(
                        hit, 1.0, 0.0
                    ).astype(BF16)

    for half in range(2):
        await_bytes(arrived.at[half], recv_one.at[half])
        for c in range(ROWS // 128):
            bins = slice(c * 128, (c + 1) * 128)
            part = jnp.transpose(arrived[half, :, bins])
            part_high = part.astype(BF16).astype(F32)
            rows_high[half, bins, :] = part_high
            rows_low[half, bins, :] = part - part_high
        gather_plane(half, rows_high, rows_low, labels_x, onehot_y, crossed)
    keep_matching(crossed, plane)
    solve_plane(tabs, kernel, plane, fields)
    spread_cells(fields, cells)
    own = replies.at[0, low]
    for half in range(2):
        answer(half, cells, labels_t, replies_t)
        for c in range(ROWS // 128):
            bins = slice(c * 128, (c + 1) * 128)
            replies[half, :, bins] = jnp.transpose(replies_t[half, bins, :])
        if half == 0:
            pltpu.make_async_copy(own, returned.at[core * 128 + low], recv_two.at[0]).start()
            pltpu.make_async_copy(own, spare_two, send_two).start()
        send_half(
            half,
            lambda there: replies.at[half, place_of(there[0], there[1], there[2], 0)],
            returned.at[core * 128 + low],
            send_two,
            recv_two.at[half],
        )
    await_bytes(sent, send_one)

    for half in range(2):
        at = pl.ds(pl.multiple_of(lax.rem(core + half, 2) * 128, 128), 128)
        await_bytes(returned.at[at], recv_two.at[half])
        part = dot3((basis_t[0, :, at], basis_t[1, :, at]), split(returned[at, :]))
        if half == 0:
            mesh_rows[...] = part
        else:
            field_high[...], field_low[...] = split(mesh_rows[...] + part)
    for c in range(ATOMS // CHUNK):
        lanes = slice(c * CHUNK, (c + 1) * CHUNK)
        key = tab_z[8:16, lanes]
        picked = []
        for k in range(3):
            total = dot3(
                (field_high[...], field_low[...]), (weights[2 * k, c], weights[2 * k + 1, c])
            )
            chosen = jnp.zeros((8, CHUNK), F32)
            for h in range(32):
                chosen = jnp.where(key == float(h), total[h * 8 : (h + 1) * 8], chosen)
            picked.append(chosen)
        wz = tab_z[0:8, lanes]
        potential = jnp.sum(wz * picked[0], axis=0, keepdims=True)
        charge = -charges[0:1, lanes]
        sums[0:1, lanes] = charge * jnp.sum(wz * picked[1], axis=0, keepdims=True)
        sums[1:2, lanes] = charge * jnp.sum(wz * picked[2], axis=0, keepdims=True)
        sums[2:3, lanes] = charge * jnp.sum(tab_z[16:24, lanes] * picked[0], axis=0, keepdims=True)
        atom = lax.broadcasted_iota(jnp.int32, (1, CHUNK), 1) + c * CHUNK
        sums[3:4, lanes] = jnp.where(atom < atom_count[0], potential, 0.0)
    await_bytes(returned, send_two)


def finish_kernel(sums, lifts, w_in, forces, grads):
    forces[...] = sums[0:3, :]
    for c in range(ATOMS // CHUNK):
        lanes = slice(c * CHUNK, (c + 1) * CHUNK)
        grad = sums[3:4, lanes] * dot(w_in[...], lifts[:, lanes])
        for b in range(CHUNK // 128):
            rows = slice(c * CHUNK + b * 128, c * CHUNK + (b + 1) * 128)
            grads[rows, :] = jnp.transpose(grad[:, b * 128 : (b + 1) * 128]).astype(BF16)


def coulomb(kernel, wave_index):
    half = GRID // 2

    def wave(index):
        return jnp.where(index <= half, index, index - half)

    wave_x = wave(lax.broadcasted_iota(jnp.int32, (GRID, GRID), 0))
    wave_y = wave(lax.broadcasted_iota(jnp.int32, (GRID, GRID), 1))
    wave_z = wave(wave_index)
    squared = (wave_x * wave_x + wave_y * wave_y + wave_z * wave_z).astype(F32)
    damped = jnp.exp(-((SMOOTH * math.pi / GRID) ** 2) * squared)
    values = COUPLE * damped * (GRID * GRID) / (4.0 * math.pi * math.pi * jnp.maximum(squared, 1.0))
    keep = (squared > 0) & (wave_x != half) & (wave_y != half) & (wave_z != half)
    kernel[...] = jnp.where(keep, values, 0.0)


def gather_plane(half, rows_high, rows_low, labels_x, onehot_y, crossed):
    def one(xb):
        left = []
        for rank in range(2):
            at = pl.ds(pl.multiple_of(rank * 256 + xb * 8, 8), 8)
            high, low = rows_high[half, at, :], rows_low[half, at, :]
            label_x = labels_x[half, at, :]
            hits = [label_x == float(h) for h in range(8)]
            parts = [jnp.where(hit, part, 0.0) for part in (high, low) for hit in hits]
            left.append(jnp.concatenate(parts, axis=0).astype(BF16))
        both = dot(jnp.concatenate(left, axis=1), onehot_y[half, xb], NT)
        return both[0:64] + both[64:128]

    @pl.loop(0, 32 // UNROLL)
    def _(step):
        totals = [one(step * UNROLL + k) for k in range(UNROLL)]
        for k, total in enumerate(totals):
            if half == 0:
                crossed[step * UNROLL + k] = total
            else:
                crossed[step * UNROLL + k] += total


def keep_matching(crossed, plane):
    lane_class = lax.broadcasted_iota(jnp.int32, (8, GRID), 1) // 32
    match = lane_class == lax.broadcasted_iota(jnp.int32, (8, GRID), 0)
    row = lax.broadcasted_iota(jnp.int32, (8, GRID), 0)

    @pl.loop(0, 8)
    def _(step):
        for k in range(4):
            xb = step * 4 + k
            total = jnp.zeros((8, GRID), F32)
            for h in range(8):
                part = jnp.where(match, crossed[xb, h * 8 : h * 8 + 8, :], 0.0)
                total = jnp.where(row == h, jnp.sum(part, axis=0, keepdims=True), total)
            plane[pl.ds(pl.multiple_of(xb * 8, 8), 8), :] = total


def solve_plane(tabs, kernel, plane, fields):
    along_x, back_x, along_y = [(tabs[2 * k], tabs[2 * k + 1]) for k in range(3)]
    spectrum = dot3(along_x, split(plane[...]))
    spectrum = dot3(split(spectrum), along_y, NT) * kernel[...]
    field = dot3(back_x, split(spectrum))
    field = dot3(split(field), along_y)
    fields[0] = field[:, :128]
    fields[1] = field[:, 128:]


def spread_cells(fields, cells):
    block = lax.broadcasted_iota(jnp.int32, (32, 128), 1) // 32
    for yb in range(8):
        for h in range(2):
            chosen = None
            for q in range(4):
                part = fields[yb // 4, pl.ds(4 * h + q, 32, stride=8), :]
                shift = (q - yb % 4) % 4 * 32
                part = pltpu.roll(part, shift, 1) if shift else part
                chosen = part if q == 0 else jnp.where(block == q, part, chosen)
            cells[yb, h] = chosen


def answer(half, cells, labels_t, replies_t):
    for yb in range(8):
        for rank in range(2):
            at = pl.ds(rank * 256 + yb, 32, stride=8)
            label = labels_t[half, at, :]
            index = label & 127
            upper = label >> 7
            value = jnp.zeros((32, 128), F32)
            for h in range(2):
                taken = jnp.take_along_axis(cells[yb, h], index, axis=1, mode="promise_in_bounds")
                value = jnp.where(upper == h, taken, value)
            replies_t[half, at, :] = value


VM = pl.BlockSpec(memory_space=pltpu.VMEM)
SM = pl.BlockSpec(memory_space=pltpu.SMEM)


def local(features, fractions, row_ids, stencil_slots, stencil_z, atom_count, w_in, w_out):
    basis, basis_t, plane = [jnp.asarray(table) for table in tables()]
    vmem = pltpu.VMEM
    chunks = ATOMS // CHUNK
    sums, lifts = pl.pallas_call(
        step_kernel,
        out_shape=(
            jax.ShapeDtypeStruct((8, ATOMS), F32),
            jax.ShapeDtypeStruct((128, ATOMS), BF16),
        ),
        in_specs=[VM] * 4 + [SM] + [VM] * 6,
        out_specs=(VM, VM),
        scratch_shapes=[
            vmem((ROWS, 128), F32),
            vmem((ROWS, 128), F32),
            vmem((8, ROWS), F32),
            vmem((2, 4, 4, 8, ROWS), F32),
            vmem((1, ATOMS), F32),
            vmem((1, ATOMS), jnp.int32),
            vmem((3, 32, ATOMS), F32),
            vmem((24, ATOMS), F32),
            vmem((24, ATOMS), F32),
            vmem((GRID, CHUNK), BF16),
            vmem((GRID, CHUNK), BF16),
            vmem((GRID, ROWS), F32),
            vmem((DEVICES, ROWS), F32),
            vmem((2, 128, ROWS), F32),
            vmem((2, ROWS, 128), F32),
            vmem((2, ROWS, 128), F32),
            vmem((2, ROWS, 128), jnp.int32),
            vmem((2, ROWS, 128), F32),
            vmem((2, 32, GRID, 256), BF16),
            vmem((32, 64, GRID), F32),
            vmem((GRID, GRID), F32),
            vmem((2, GRID, 128), F32),
            vmem((8, 2, 32, 128), F32),
            vmem((2, ROWS, 128), F32),
            vmem((2, 128, ROWS), F32),
            vmem((DEVICES, ROWS), F32),
            vmem((ROWS,), F32),
            vmem((ROWS,), F32),
            vmem((GRID, GRID), F32),
            vmem((GRID, ROWS), BF16),
            vmem((GRID, ROWS), BF16),
            vmem((6, chunks, ROWS, CHUNK), BF16),
            pltpu.SemaphoreType.DMA((14,)),
            pltpu.SemaphoreType.DMA((14,)),
            pltpu.SemaphoreType.REGULAR((3,)),
        ]
        + [
            pltpu.SemaphoreType.DMA,
            pltpu.SemaphoreType.DMA,
            pltpu.SemaphoreType.DMA((2,)),
            pltpu.SemaphoreType.DMA,
            pltpu.SemaphoreType.DMA((2,)),
        ],
        compiler_params=pltpu.CompilerParams(
            vmem_limit_bytes=VMEM_LIMIT, collective_id=0, has_side_effects=True
        ),
        name="step",
    )(
        row_ids,
        stencil_slots,
        stencil_z.reshape(1, ATOMS),
        fractions,
        atom_count,
        features,
        w_in,
        w_out.reshape(1, 128),
        basis,
        basis_t,
        plane,
    )
    return pl.pallas_call(
        finish_kernel,
        out_shape=(
            jax.ShapeDtypeStruct((3, ATOMS), F32),
            jax.ShapeDtypeStruct((ATOMS, 128), BF16),
        ),
        in_specs=[VM] * 3,
        out_specs=(VM, VM),
        compiler_params=pltpu.CompilerParams(vmem_limit_bytes=VMEM_LIMIT),
        name="finish",
    )(sums, lifts, w_in)


def solution(mesh):
    placed = (
        P(("pen", "slab"), None),
        P(None, ("pen", "slab")),
        P(("pen", "slab"), None),
        P(None, ("pen", "slab")),
        P(("pen", "slab")),
        P(("pen", "slab")),
        P(),
        P(),
    )
    return jax.shard_map(
        local,
        mesh=mesh,
        in_specs=placed,
        out_specs=(P(None, ("pen", "slab")), P(("pen", "slab"), None)),
        check_vma=False,
    )
```
